512 devices in a mesh: dp: 64 (over z, x, core), mp: 8 (over y).
Axes of the slice: x: 4, y: 8, z: 8, core: 2. Of those that a mesh axis runs over, the one named last changes fastest.
Arguments:
- hidden: bfloat16 [2, 8192, 28672], P(None, 'dp', 'mp'), may hold values from -17 to 17
- cotangent: bfloat16 [2, 8192, 8192], P(None, ('dp', 'mp')), may hold values from -74 to 74
- start_q: float32 [32, 8192], P(None, 'mp'), may hold values from -6 to 6
Outputs:
- factor_q: float32 [32, 8192], P(None, 'mp')
The draws below stay inside these ranges and needn't reach their ends.
All inputs are finite; a program needn't handle non-finite values.
Results may differ from the reference program's by a relative error of at most 0.014.
Values may be sent and summed in bfloat16 or wider, within the bound.
A program may use at most 64 MiB of HBM per device.

```python
import jax
import jax.numpy as jnp
from jax import lax

D = 8192
FF = 28672
RANK = 32
STEPS = 2
TOK = 128
TOKENS = 8192
N_DP = 64


def draw_hidden(key, part):
    key = jax.random.fold_in(key, 11)
    extent = (STEPS, TOKENS, FF)
    column = jnp.arange(FF, dtype=jnp.float32) / max(FF - 1, 1)
    values = jnp.clip(jax.random.normal(key, extent, jnp.float32), -6.0, 6.0)
    growth = 8.0
    factor_col = jnp.exp(jnp.log(growth) * (column - 0.5))
    return (values * factor_col[None, None, :]).astype(jnp.bfloat16)


def draw_cotangent(key, part):
    key = jax.random.fold_in(key, 23)
    extent = (STEPS, TOKENS, D)
    replica = (jnp.arange(TOKENS, dtype=jnp.int32) // TOK).astype(jnp.float32)
    position = replica / max(TOKENS // TOK - 1, 1)
    values = jnp.clip(jax.random.normal(key, extent, jnp.float32), -6.0, 6.0)
    growth = 100.0
    factor_row = jnp.exp(jnp.log(growth) * (position - 0.5))
    return (values * factor_row[None, :, None]).astype(jnp.bfloat16)


def levels(rng, dims, split, low, top_value):
    def one(axis_at, parts):
        heights = jax.random.uniform(jax.random.fold_in(jax.random.fold_in(rng, 6), axis_at), (parts,), jnp.float32, low / len(split), top_value / len(split))
        return jnp.repeat(jnp.exp(heights), dims[axis_at] // parts).reshape((-1,) + (1,) * (len(dims) - axis_at - 1))

    loudness = one(*split[0])
    for cut in split[1:]:
        loudness = loudness * one(*cut)
    return loudness


def scatter_about(rng, dims, scale, bound, pieces=(), held_as=jnp.bfloat16):
    factor_of = levels(rng, dims, pieces, -0.22, 0.18) if pieces else 1.0
    entries = jax.random.normal(rng, dims, jnp.float32) * scale * factor_of
    return jnp.minimum(jnp.maximum(entries, -bound), bound).astype(held_as)


def setup_inputs(seed: int = 0) -> dict:
    key_of = jax.random.split(jax.random.key(seed), 4)
    hidden = draw_hidden(jax.random.fold_in(key_of[3], 71), 0)
    cotangent = draw_cotangent(jax.random.fold_in(key_of[3], 71), 0)
    start_q = scatter_about(key_of[2], (RANK, D), 1.0, 6.0, ((1, 8),), jnp.float32)
    return {"hidden": hidden, "cotangent": cotangent, "start_q": start_q}


def lower_solve(lower_factor, right):
    return lax.linalg.triangular_solve(lower_factor, right, left_side=True, lower=True)

def reference(hidden, cotangent, start_q):
    hid_groups = hidden.reshape(STEPS, N_DP, TOK, FF)
    cot_groups = cotangent.reshape(STEPS, N_DP, TOK, D)
    highest = lax.Precision.HIGHEST
    current = start_q
    past_p = []
    past_q = []
    for turn_index in range(STEPS):
        used_steps = turn_index + 1
        qround = current.astype(jnp.bfloat16)

        def p_body(replica, total):
            for earlier in range(used_steps):
                rows_cot = cot_groups[earlier, replica].astype(jnp.float32)
                sketch = jnp.dot(rows_cot, qround.astype(jnp.float32).T).astype(jnp.bfloat16)
                rows_hid = hid_groups[earlier, replica].astype(jnp.float32)
                total = total + jnp.dot(sketch.astype(jnp.float32).T, rows_hid)
            return total
        factor = lax.fori_loop(0, N_DP, p_body, jnp.zeros((RANK, FF), jnp.float32)) / N_DP
        for earlier in range(turn_index):
            weights = jnp.dot(past_q[earlier], current.T, precision=highest)
            factor = factor - jnp.dot(weights.T, past_p[earlier], precision=highest)
        stacked = jnp.stack([factor] + past_p)
        correlations = jnp.einsum('jrf,qf->jrq', stacked, factor, precision=highest)
        lower_factor = jnp.linalg.cholesky(correlations[0])
        orthonormal = lower_solve(lower_factor, factor)
        pround = orthonormal.astype(jnp.bfloat16)

        def q_body(replica, total):
            for earlier in range(used_steps):
                rows_hid = hid_groups[earlier, replica].astype(jnp.float32)
                mixed_rows = jnp.dot(rows_hid, pround.astype(jnp.float32).T).astype(jnp.bfloat16)
                rows_cot = cot_groups[earlier, replica].astype(jnp.float32)
                total = total + jnp.dot(mixed_rows.astype(jnp.float32).T, rows_cot)
            return total
        update = lax.fori_loop(0, N_DP, q_body, jnp.zeros((RANK, D), jnp.float32)) / N_DP
        for earlier in range(turn_index):
            back_solve = lower_solve(lower_factor, correlations[earlier + 1].T)
            update = update - jnp.dot(back_solve, past_q[earlier], precision=highest)
        past_p.append(orthonormal)
        past_q.append(update)
        current = update
    return current
```

```python
import functools

import jax
import jax.numpy as jnp
from jax import lax
from jax.experimental import pallas as pl
from jax.experimental.pallas import tpu as pltpu
from jax.sharding import PartitionSpec as P

MESH = pl.DeviceIdType.MESH
BF = jnp.bfloat16
F32 = jnp.float32
NY = 8
NZ = 8
NX = 4
CHIPS = NZ * NX
TILES = 28
QBLOCKS = 8
HALF = 16
RANK = 32
LANES = 128
Y_ORDER = (4, 3, 5, 2, 6, 1, 7)


def _hops(dz, dx):
    return min(dz, NZ - dz) + min(dx, NX - dx)


ZX_ORDER = sorted(
    [(dz, dx) for dz in range(NZ) for dx in range(NX) if (dz, dx) != (0, 0)],
    key=lambda d: (-_hops(*d), d),
)


def nt_dot(a, b):
    return lax.dot_general(a, b, (((1,), (1,)), ((), ())), preferred_element_type=F32)


def dot(a, b):
    return jnp.dot(a, b, preferred_element_type=F32)


def exact_dot(a, b):
    return jnp.dot(a, b, preferred_element_type=F32, precision=lax.Precision.HIGHEST)


def wait_bytes(ref, sem):
    pltpu.make_async_copy(ref, ref, sem).wait()


def inverse_lower(gram):
    rows = lax.broadcasted_iota(jnp.int32, (RANK, LANES), 0)
    lanes = lax.broadcasted_iota(jnp.int32, (RANK, LANES), 1)
    work = jnp.where(lanes < RANK, gram, jnp.where(lanes == rows + RANK, 1.0, 0.0))
    row_ids = lax.broadcasted_iota(jnp.int32, (RANK, 1), 0)
    scale = jnp.zeros((RANK, 1), F32)
    for j in range(RANK):
        row = work[j : j + 1, :]
        pivot = work[j : j + 1, j : j + 1]
        scale = jnp.where(row_ids == j, pivot, scale)
        if j < RANK - 1:
            factor = jnp.where(row_ids > j, work[:, j : j + 1] / pivot, 0.0)
            work = work - factor * row
    return (work * lax.rsqrt(scale))[:, RANK : 2 * RANK]


def kernel(
    hid, cot, startq, out,
    hbuf, cbuf, tbuf, qf, qsrc, qgat, sk0, sk1, ptsrc, ptrs, pt, mx0, mx1, gram, wbuf,
    zsrc, zrs, zx, qall, qout, minv, umat,
    s_local, s_core, r_core, s_q, r_q, s_sk, r_sk, s_t, r_t, s_tc, r_tc, s_prs, r_prs, s_pag, r_pag,
    s_ptc, r_ptc, s_mx, r_mx, s_g, r_g, s_w, r_w, s_zrs, r_zrs, s_zx, r_zx, s_qag, r_qag,
):
    dp = lax.axis_index("dp")
    y = lax.axis_index("mp")
    c = lax.rem(dp, 2)
    chip = lax.div(dp, 2)
    z = lax.div(chip, NX)
    x = lax.rem(chip, NX)
    sib = {"dp": dp + 1 - 2 * c, "mp": y}

    def y_dev(k):
        return {"dp": dp, "mp": lax.rem(y + k, NY)}

    def zx_chip(dz, dx):
        return lax.rem(z + dz, NZ) * NX + lax.rem(x + dx, NX)

    def zx_dev(there):
        return {"dp": there * 2 + c, "mp": y}

    def send(src, dst, ssem, rsem, dev):
        pltpu.make_async_remote_copy(
            src_ref=src, dst_ref=dst, send_sem=ssem, recv_sem=rsem, device_id=dev, device_id_type=MESH
        ).start()

    load_q = pltpu.make_async_copy(startq, qf, s_local.at[0])
    load_q.start()
    bar = pltpu.get_barrier_semaphore()
    for k in Y_ORDER:
        pl.semaphore_signal(bar, inc=1, device_id=y_dev(k), device_id_type=MESH)
    for d in ZX_ORDER:
        pl.semaphore_signal(bar, inc=1, device_id=zx_dev(zx_chip(*d)), device_id_type=MESH)
    pl.semaphore_signal(bar, inc=1, device_id=sib, device_id_type=MESH)
    load_c = pltpu.make_async_copy(cot.at[0], cbuf.at[c], s_local.at[1])
    load_c.start()
    load_h = [pltpu.make_async_copy(hid.at[j], hbuf.at[j, :, c], s_local.at[2 + j]) for j in range(2)]
    load_h[0].start()
    load_h[1].start()
    load_q.wait()
    qsrc[...] = qf[pl.ds(pl.multiple_of(c * HALF, HALF), HALF), :].astype(BF)
    pl.semaphore_wait(bar, NY - 1 + CHIPS - 1 + 1)

    for n, k in enumerate(Y_ORDER):
        send(qsrc, qgat.at[n], s_q, r_q.at[n], y_dev(k))
    send(cot.at[0], cbuf.at[c], s_core.at[0], r_core.at[0], sib)
    send(hid.at[0], hbuf.at[0, :, c], s_core.at[1], r_core.at[1], sib)
    send(hid.at[1], hbuf.at[1, :, c], s_core.at[2], r_core.at[2], sib)
    load_c.wait()
    wait_bytes(cbuf.at[0], r_core.at[0])

    def block_sketch(q_rows, owner):
        cols = pl.ds(pl.multiple_of(owner * 1024, 1024), 1024)
        return nt_dot(q_rows, cbuf[:, :, cols].reshape(RANK, 1024))

    sketch = block_sketch(qsrc[...], y)
    for n, k in sorted(enumerate(Y_ORDER), key=lambda e: min(e[1], NY - e[1])):
        wait_bytes(qgat.at[n], r_q.at[n])
        sketch = sketch + block_sketch(qgat[n], lax.rem(y - k + NY, NY))
    spot = lax.broadcasted_iota(jnp.int32, (RANK, LANES), 0) + RANK * lax.rem(y, 4)
    place = jnp.where(lax.broadcasted_iota(jnp.int32, (RANK, LANES), 1) == spot, 1.0, 0.0).astype(BF)
    sk0[y] = dot(sketch.astype(BF), place).astype(BF)
    for k in Y_ORDER:
        send(sk0.at[y], sk0.at[y], s_sk.at[0], r_sk.at[0], y_dev(k))
    wait_bytes(sk0.at[pl.ds(0, NY - 1)], r_sk.at[0])

    for j in range(2):
        for k in Y_ORDER:
            there = lax.rem(y + k, NY)
            cols = pl.ds(pl.multiple_of(there * 1024, 1024), 1024)
            send(cot.at[j, :, cols], tbuf.at[j, y, c], s_t.at[j], r_t.at[j], y_dev(k))
        own = pl.ds(pl.multiple_of(y * 1024, 1024), 1024)
        pltpu.make_async_copy(cot.at[j, :, own], tbuf.at[j, y, c], s_local.at[4 + j]).start()

    left = jnp.concatenate(
        [
            (sk0[0] + sk0[1]) + (sk0[2] + sk0[3]),
            (sk0[4] + sk0[5]) + (sk0[6] + sk0[7]),
        ],
        axis=1,
    )

    q_owner = x == lax.rem(z, NX)
    for s in range(2):
        used = s + 1
        for j in range(used):
            if s == j:
                load_h[j].wait()
                wait_bytes(hbuf.at[j, :, 0], r_core.at[1 + j])
        for g in range(4):
            cols = slice(g * 896, (g + 1) * 896)
            part = None
            for j in range(used):
                term = dot(left[:, j * 256 : (j + 1) * 256], hbuf[j, :, :, :, cols].reshape(256, 896))
                part = term if part is None else part + term
            part = part.astype(BF)
            for n in range(7):
                ptsrc[s, g * 7 + n] = part[:, n * LANES : (n + 1) * LANES]
        for d in ZX_ORDER:
            there = zx_chip(*d)

            @pl.when(there < TILES)
            def _(there=there):
                send(ptsrc.at[s, there], ptrs.at[s, chip], s_prs.at[s], r_prs.at[s], zx_dev(there))

        if s == 1:
            wait_bytes(wbuf.at[pl.ds(0, NY - 1)], r_w)
            weights = wbuf[0]
            for n in range(1, NY):
                weights = weights + wbuf[n]
            umat[...] = exact_dot(weights[:, :RANK], minv[0])

        @pl.when(chip < TILES)
        def _():
            ptrs[s, chip] = ptsrc[s, chip]
            wait_bytes(ptrs.at[s, pl.ds(0, CHIPS - 1)], r_prs.at[s])
            total = ptrs[s, 0].astype(F32)
            for n in range(1, CHIPS):
                total = total + ptrs[s, n].astype(F32)
            total = total * (1.0 / 64.0)
            if s == 1:
                past = jnp.concatenate([pt[0, 0, chip], pt[0, 1, chip]], axis=0).astype(F32)
                own_rows = umat[pl.ds(pl.multiple_of(c * HALF, HALF), HALF), :]
                total = total - exact_dot(own_rows, past)
            pt[s, c, chip] = total.astype(BF)
            for d in ZX_ORDER:
                send(pt.at[s, c, chip], pt.at[s, c, chip], s_pag.at[s], r_pag.at[s], zx_dev(zx_chip(*d)))
            wait_bytes(pt.at[s, c, pl.ds(0, TILES - 1)], r_pag.at[s])

        @pl.when(chip >= TILES)
        def _():
            wait_bytes(pt.at[s, c, pl.ds(0, TILES)], r_pag.at[s])

        send(pt.at[s, c], pt.at[s, c], s_ptc.at[s], r_ptc.at[s], sib)

        if s == 0:
            for j in range(2):
                pltpu.make_async_copy(cot.at[j, :, pl.ds(0, 1024)], tbuf.at[j, y, c], s_local.at[4 + j]).wait()
                wait_bytes(tbuf.at[j, pl.ds(0, NY - 1), 0], r_t.at[j])
                send(tbuf.at[j, :, c], tbuf.at[j, :, c], s_tc.at[j], r_tc.at[j], sib)

        mx = mx0 if s == 0 else mx1
        rows = jnp.concatenate([pt[s, c, n] for n in range(TILES)], axis=1)
        for j in range(used):
            mx[y, :, j * 256 : (j + 1) * 256] = nt_dot(rows, hbuf[j].reshape(256, 3584)).astype(BF)
        for k in Y_ORDER:
            send(mx.at[y], mx.at[y], s_mx.at[s], r_mx.at[s], y_dev(k))

        wait_bytes(pt.at[s, 0], r_ptc.at[s])

        def both(step):
            return jnp.concatenate(
                [jnp.concatenate([pt[step, e, n] for n in range(TILES)], axis=1) for e in range(2)], axis=0
            )

        now = both(s)
        other = now if s == 0 else both(0)
        gram[s, y] = nt_dot(now, jnp.concatenate([now, other, now, other], axis=0))
        for k in Y_ORDER:
            send(gram.at[s, y], gram.at[s, y], s_g.at[s], r_g.at[s], y_dev(k))

        wait_bytes(mx.at[pl.ds(0, NY - 1)], r_mx.at[s])
        mixed = mx[0].astype(F32)
        for n in range(1, NY):
            mixed = mixed + mx[n].astype(F32)
        mixed = mixed.astype(BF)

        if s == 0:
            for j in range(2):
                wait_bytes(tbuf.at[j, :, 0], r_tc.at[j])
        part = None
        for j in range(used):
            term = dot(mixed[:, j * 256 : (j + 1) * 256], tbuf[j].reshape(256, 1024))
            part = term if part is None else part + term
        part = part.astype(BF)
        for b in range(QBLOCKS):
            zsrc[s, b] = part[:, b * LANES : (b + 1) * LANES]
        for step in (4, 3, 5, 2, 6, 1, 7, 0):
            b = lax.rem(z + step, NZ)
            there = b * NX + lax.rem(b, NX)

            @pl.when(there != chip)
            def _(b=b, there=there):
                send(zsrc.at[s, b], zrs.at[s, chip], s_zrs.at[s], r_zrs.at[s], zx_dev(there))

        wait_bytes(gram.at[s, pl.ds(0, NY - 1)], r_g.at[s])
        inner = gram[s, 0]
        for n in range(1, NY):
            inner = inner + gram[s, n]
        minv[s] = inverse_lower(inner)
        if s == 1:
            cross = lax.dot_general(
                inner[:, RANK : 2 * RANK], minv[0], (((1,), (1,)), ((), ())),
                preferred_element_type=F32, precision=lax.Precision.HIGHEST,
            )

        dest = qall if s == 0 else qout

        @pl.when(q_owner)
        def _():
            zrs[s, chip] = zsrc[s, z]
            wait_bytes(zrs.at[s, pl.ds(0, CHIPS - 1)], r_zrs.at[s])
            total = zrs[s, 0].astype(F32)
            for n in range(1, CHIPS):
                total = total + zrs[s, n].astype(F32)
            zx[s, c] = total * (1.0 / 64.0)
            send(zx.at[s, c], zx.at[s, c], s_zx.at[s], r_zx.at[s], sib)
            wait_bytes(zx.at[s, 0], r_zx.at[s])
            value = zx[s].reshape(RANK, LANES)
            if s == 1:
                value = value - exact_dot(cross, qall[z].astype(F32))
            dest[z] = exact_dot(minv[s], value).astype(dest.dtype)
            for d in ZX_ORDER:
                send(dest.at[z], dest.at[z], s_qag.at[s], r_qag.at[s], zx_dev(zx_chip(*d)))
            wait_bytes(dest.at[pl.ds(0, QBLOCKS - 1)], r_qag.at[s])

        @pl.when(jnp.logical_not(q_owner))
        def _():
            wait_bytes(dest.at[pl.ds(0, QBLOCKS)], r_qag.at[s])

        if s == 0:
            own_rows = pl.ds(pl.multiple_of(c * HALF, HALF), HALF)
            rows = jnp.concatenate([qall[b, own_rows, :] for b in range(QBLOCKS)], axis=1)
            for j in range(2):
                sk1[y, :, j * 256 : (j + 1) * 256] = nt_dot(rows, tbuf[j].reshape(256, 1024)).astype(BF)
            for k in Y_ORDER:
                send(sk1.at[y], sk1.at[y], s_sk.at[1], r_sk.at[1], y_dev(k))
            whole = jnp.concatenate([qall[b] for b in range(QBLOCKS)], axis=1)
            wbuf[y] = nt_dot(whole, jnp.concatenate([whole] * 4, axis=0))
            for k in Y_ORDER:
                send(wbuf.at[y], wbuf.at[y], s_w, r_w, y_dev(k))
            wait_bytes(sk1.at[pl.ds(0, NY - 1)], r_sk.at[1])
            total = sk1[0].astype(F32)
            for n in range(1, NY):
                total = total + sk1[n].astype(F32)
            left = total.astype(BF)
        else:
            for b in range(QBLOCKS):
                out[:, b * LANES : (b + 1) * LANES] = qout[b].astype(F32)

    wait_bytes(qgat, s_q)
    wait_bytes(cbuf.at[0], s_core.at[0])
    wait_bytes(hbuf.at[0, :, 0], s_core.at[1])
    wait_bytes(hbuf.at[1, :, 0], s_core.at[2])
    wait_bytes(sk0.at[pl.ds(0, NY - 1)], s_sk.at[0])
    wait_bytes(sk1.at[pl.ds(0, NY - 1)], s_sk.at[1])
    wait_bytes(wbuf.at[pl.ds(0, NY - 1)], s_w)
    for s in range(2):
        wait_bytes(tbuf.at[s, pl.ds(0, NY - 1), 0], s_t.at[s])
        wait_bytes(tbuf.at[s, :, 0], s_tc.at[s])
        wait_bytes(pt.at[s, 0], s_ptc.at[s])
        mx = mx0 if s == 0 else mx1
        wait_bytes(mx.at[pl.ds(0, NY - 1)], s_mx.at[s])
        wait_bytes(gram.at[s, pl.ds(0, NY - 1)], s_g.at[s])
        dest = qall if s == 0 else qout

        @pl.when(chip < TILES)
        def _():
            wait_bytes(ptsrc.at[s, pl.ds(0, TILES - 1)], s_prs.at[s])
            wait_bytes(ptrs.at[s, pl.ds(0, CHIPS - 1)], s_pag.at[s])

        @pl.when(chip >= TILES)
        def _():
            wait_bytes(ptsrc.at[s], s_prs.at[s])

        @pl.when(q_owner)
        def _():
            wait_bytes(zsrc.at[s, pl.ds(0, QBLOCKS - 1)], s_zrs.at[s])
            wait_bytes(zx.at[s, 0], s_zx.at[s])
            for _ in range(CHIPS - 1):
                wait_bytes(dest.at[0], s_qag.at[s])

        @pl.when(jnp.logical_not(q_owner))
        def _():
            wait_bytes(zsrc.at[s], s_zrs.at[s])


def on_device(hidden, cotangent, start_q):
    hidden = hidden.reshape(2, NY, 16, 3584)
    dma = pltpu.SemaphoreType.DMA
    vm = pltpu.VMEM
    anywhere = pl.BlockSpec(memory_space=pl.ANY)
    return pl.pallas_call(
        kernel,
        out_shape=jax.ShapeDtypeStruct((RANK, 1024), F32),
        in_specs=[anywhere] * 3,
        out_specs=pl.BlockSpec(memory_space=pltpu.VMEM),
        scratch_shapes=[
            vm((2, NY, 2, 16, 3584), BF),
            vm((2, 16, 8192), BF),
            vm((2, NY, 2, 16, 1024), BF),
            vm((RANK, 1024), F32),
            vm((HALF, 1024), BF),
            vm((NY - 1, HALF, 1024), BF),
            vm((NY, HALF, LANES), BF),
            vm((NY, HALF, 512), BF),
            vm((2, TILES, HALF, LANES), BF),
            vm((2, CHIPS, HALF, LANES), BF),
            vm((2, 2, TILES, HALF, LANES), BF),
            vm((NY, HALF, 256), BF),
            vm((NY, HALF, 512), BF),
            vm((2, NY, RANK, LANES), F32),
            vm((NY, RANK, LANES), F32),
            vm((2, QBLOCKS, HALF, LANES), BF),
            vm((2, CHIPS, HALF, LANES), BF),
            vm((2, 2, HALF, LANES), F32),
            vm((QBLOCKS, RANK, LANES), BF),
            vm((QBLOCKS, RANK, LANES), F32),
            vm((2, RANK, RANK), F32),
            vm((RANK, RANK), F32),
            dma((6,)),
            dma((3,)), dma((3,)),
            dma, dma((NY - 1,)),
            dma((2,)), dma((2,)),
            dma((2,)), dma((2,)),
            dma((2,)), dma((2,)),
            dma((2,)), dma((2,)),
            dma((2,)), dma((2,)),
            dma((2,)), dma((2,)),
            dma((2,)), dma((2,)),
            dma((2,)), dma((2,)),
            dma, dma,
            dma((2,)), dma((2,)),
            dma((2,)), dma((2,)),
            dma((2,)), dma((2,)),
        ],
        compiler_params=pltpu.CompilerParams(
            collective_id=0, has_side_effects=True, vmem_limit_bytes=32 * 1024 * 1024
        ),
        name="powersgd",
    )(hidden, cotangent, start_q)


def solution(mesh):
    return jax.shard_map(
        on_device,
        mesh=mesh,
        in_specs=(P(None, "dp", "mp"), P(None, ("dp", "mp"), None), P(None, "mp")),
        out_specs=P(None, "mp"),
        check_vma=False,
    )
```

```python
import functools

import jax
import jax.numpy as jnp
from jax import lax
from jax.experimental import pallas as pl
from jax.experimental.pallas import tpu as pltpu
from jax.sharding import PartitionSpec as P

MESH = pl.DeviceIdType.MESH
BF = jnp.bfloat16
F32 = jnp.float32
NY = 8
NZ = 8
NX = 4
CHIPS = NZ * NX
TILES = 28
QBLOCKS = 8
HALF = 16
RANK = 32
LANES = 128
GROUP = 7 * LANES
Y_ORDER = (4, 3, 5, 2, 6, 1, 7)


def _hops(dz, dx):
    return min(dz, NZ - dz) + min(dx, NX - dx)


ZX_ORDER = sorted(
    [(dz, dx) for dz in range(NZ) for dx in range(NX) if (dz, dx) != (0, 0)],
    key=lambda d: (-_hops(*d), d),
)


def nt_dot(a, b):
    return lax.dot_general(a, b, (((1,), (1,)), ((), ())), preferred_element_type=F32)


def dot(a, b):
    return jnp.dot(a, b, preferred_element_type=F32)


def exact_dot(a, b):
    return jnp.dot(a, b, preferred_element_type=F32, precision=lax.Precision.HIGHEST)


def wait_bytes(ref, sem):
    pltpu.make_async_copy(ref, ref, sem).wait()


def exact_nt_dot(a, b):
    return lax.dot_general(
        a, b, (((1,), (1,)), ((), ())), preferred_element_type=F32, precision=lax.Precision.HIGHEST
    )


def pack(value, rows):
    width = LANES * rows // RANK
    lanes = lax.broadcasted_iota(jnp.int32, (rows, LANES), 1)
    packed = value[:rows]
    for k in range(1, RANK // rows):
        packed = jnp.where(lanes >= k * width, value[k * rows : (k + 1) * rows], packed)
    return packed


def unpack(packed):
    rows = packed.shape[0]
    width = LANES * rows // RANK
    return jnp.concatenate(
        [packed] + [pltpu.roll(packed, LANES - k * width, 1) for k in range(1, RANK // rows)], axis=0
    )


def sum_slots(ref, count):
    terms = [ref[n].astype(F32) for n in range(count)]
    while len(terms) > 1:
        terms = [a + b for a, b in zip(terms[::2], terms[1::2])]
    return terms[0]


def inverse_lower(gram):
    rows = lax.broadcasted_iota(jnp.int32, (RANK, LANES), 0)
    lanes = lax.broadcasted_iota(jnp.int32, (RANK, LANES), 1)
    work = jnp.where(lanes < RANK, gram, jnp.where(lanes == rows + RANK, 1.0, 0.0))
    row_ids = lax.broadcasted_iota(jnp.int32, (RANK, 1), 0)
    scale = jnp.zeros((RANK, 1), F32)
    for j in range(RANK):
        row = work[j : j + 1, :]
        pivot = work[j : j + 1, j : j + 1]
        scale = jnp.where(row_ids == j, pivot, scale)
        if j < RANK - 1:
            factor = jnp.where(row_ids > j, work[:, j : j + 1] / pivot, 0.0)
            work = work - factor * row
    return (work * lax.rsqrt(scale))[:, RANK : 2 * RANK]


def kernel(
    hid, cot, startq, out,
    hbuf, cbuf, tbuf, qf, qsrc, qgat, sk0, sk1, ptsrc, ptrs, pt, mx0, mx1, gram0, gram1, wbuf,
    zsrc, zrs, zall, minv, umat,
    s_local, s_core, r_core, s_q, r_q, s_sk, r_sk, s_t, r_t, s_tc, r_tc, s_prs, r_prs, s_pag, r_pag,
    s_ptc, r_ptc, s_mx, r_mx, s_g, r_g, s_w, r_w, s_zrs, r_zrs, s_zx, r_zx, s_qag, r_qag,
):
    dp = lax.axis_index("dp")
    y = lax.axis_index("mp")
    c = lax.rem(dp, 2)
    chip = lax.div(dp, 2)
    z = lax.div(chip, NX)
    x = lax.rem(chip, NX)
    sib = {"dp": dp + 1 - 2 * c, "mp": y}
    pt_owner = z < NZ - 1
    q_owner = lax.rem(x, 2) == lax.rem(z + c, 2)
    ending = []

    def y_dev(k):
        return {"dp": dp, "mp": lax.rem(y + k, NY)}

    def zx_chip(dz, dx):
        return lax.rem(z + dz, NZ) * NX + lax.rem(x + dx, NX)

    def zx_dev(there):
        return {"dp": there * 2 + c, "mp": y}

    def send(src, dst, ssem, rsem, dev):
        pltpu.make_async_remote_copy(
            src_ref=src, dst_ref=dst, send_sem=ssem, recv_sem=rsem, device_id=dev, device_id_type=MESH
        ).start()

    def sent(ref, sem, when=None):
        def wait():
            wait_bytes(ref, sem)

        ending.append(wait if when is None else lambda: pl.when(when)(wait))

    def wait_t1(s):
        if s == 0:
            load_t[1].wait()
            wait_bytes(tbuf.at[1, pl.ds(0, NY - 1), 0], r_t.at[1])

    def wait_t(s):
        if s == 0:
            load_t[0].wait()
            wait_bytes(tbuf.at[0, pl.ds(0, NY - 1), 0], r_t.at[0])
        wait_t1(s)

    def finish():
        for wait in ending:
            wait()

    load_q = pltpu.make_async_copy(startq, qf, s_local.at[0])
    load_q.start()
    bar = pltpu.get_barrier_semaphore()
    for k in Y_ORDER:
        pl.semaphore_signal(bar, inc=1, device_id=y_dev(k), device_id_type=MESH)
    for d in ZX_ORDER:
        pl.semaphore_signal(bar, inc=1, device_id=zx_dev(zx_chip(*d)), device_id_type=MESH)
    pl.semaphore_signal(bar, inc=1, device_id=sib, device_id_type=MESH)
    load_c = pltpu.make_async_copy(cot.at[0], cbuf.at[c], s_local.at[1])
    load_c.start()
    load_h = [pltpu.make_async_copy(hid.at[j], hbuf.at[j, :, c], s_local.at[2 + j]) for j in range(2)]
    load_h[0].start()
    load_h[1].start()
    load_q.wait()
    qsrc[...] = qf[pl.ds(pl.multiple_of(c * HALF, HALF), HALF), :].astype(BF)
    pl.semaphore_wait(bar, NY - 1 + CHIPS - 1 + 1)

    for n, k in enumerate(Y_ORDER):
        send(qsrc, qgat.at[n], s_q, r_q.at[n], y_dev(k))
    sent(qgat, s_q)
    send(cot.at[0], cbuf.at[c], s_core.at[0], r_core.at[0], sib)
    sent(cbuf.at[0], s_core.at[0])
    for j in range(2):
        send(hid.at[j], hbuf.at[j, :, c], s_core.at[1 + j], r_core.at[1 + j], sib)
        sent(hbuf.at[j, :, 0], s_core.at[1 + j])
    load_c.wait()
    wait_bytes(cbuf.at[0], r_core.at[0])

    def block_sketch(q_rows, owner):
        cols = pl.ds(pl.multiple_of(owner * 1024, 1024), 1024)
        return nt_dot(q_rows, cbuf[:, :, cols].reshape(RANK, 1024))

    sketch = block_sketch(qsrc[...], y)
    for n, k in sorted(enumerate(Y_ORDER), key=lambda e: min(e[1], NY - e[1])):
        wait_bytes(qgat.at[n], r_q.at[n])
        sketch = sketch + block_sketch(qgat[n], lax.rem(y - k + NY, NY))
    spot = lax.broadcasted_iota(jnp.int32, (RANK, LANES), 0) + RANK * lax.rem(y, 4)
    place = jnp.where(lax.broadcasted_iota(jnp.int32, (RANK, LANES), 1) == spot, 1.0, 0.0).astype(BF)
    sk0[y] = dot(sketch.astype(BF), place).astype(BF)
    for k in Y_ORDER:
        send(sk0.at[y], sk0.at[y], s_sk.at[0], r_sk.at[0], y_dev(k))
    sent(sk0.at[pl.ds(0, NY - 1)], s_sk.at[0])
    wait_bytes(sk0.at[pl.ds(0, NY - 1)], r_sk.at[0])

    own_cols = pl.ds(pl.multiple_of(y * 1024, 1024), 1024)
    load_t = [pltpu.make_async_copy(cot.at[j, :, own_cols], tbuf.at[j, y, c], s_local.at[4 + j]) for j in range(2)]
    for j in range(2):
        for k in Y_ORDER:
            there = lax.rem(y + k, NY)
            cols = pl.ds(pl.multiple_of(there * 1024, 1024), 1024)
            send(cot.at[j, :, cols], tbuf.at[j, y, c], s_t.at[j], r_t.at[j], y_dev(k))
        sent(tbuf.at[j, pl.ds(0, NY - 1), 0], s_t.at[j])
        load_t[j].start()

    def share_t(j):
        load_t[j].wait()
        wait_bytes(tbuf.at[j, pl.ds(0, NY - 1), 0], r_t.at[j])
        send(tbuf.at[j, :, c], tbuf.at[j, :, c], s_tc.at[j], r_tc.at[j], sib)
        sent(tbuf.at[j, :, 0], s_tc.at[j])

    left = jnp.concatenate(
        [
            (sk0[0] + sk0[1]) + (sk0[2] + sk0[3]),
            (sk0[4] + sk0[5]) + (sk0[6] + sk0[7]),
        ],
        axis=1,
    )

    for s in range(2):
        used = s + 1
        if s == 0:
            load_h[0].wait()
            wait_bytes(hbuf.at[0, :, 0], r_core.at[1])
        for dx in (2, 1, 3, 0):
            g = lax.rem(x + dx, NX)
            cols = pl.ds(pl.multiple_of(g * GROUP, GROUP), GROUP)
            part = None
            for j in range(used):
                term = dot(left[:, j * 256 : (j + 1) * 256], hbuf[j, :, :, :, cols].reshape(256, GROUP))
                part = term if part is None else part + term
            part = part.astype(BF)
            for n in range(7):
                ptsrc[s, g, n] = part[:, n * LANES : (n + 1) * LANES]
            for dz in (4, 3, 5, 2, 6, 1, 7) + ((0,) if dx else ()):
                n = lax.rem(z + dz, NZ)

                @pl.when(n < NZ - 1)
                def _(n=n, g=g):
                    send(ptsrc.at[s, g, n], ptrs.at[s, chip], s_prs.at[s], r_prs.at[s], zx_dev(n * NX + g))

        sent(ptrs.at[s, pl.ds(0, TILES - 1)], s_prs.at[s], pt_owner)
        sent(ptrs.at[s, pl.ds(0, TILES)], s_prs.at[s], jnp.logical_not(pt_owner))

        if s == 0:
            load_h[1].wait()
            wait_bytes(hbuf.at[1, :, 0], r_core.at[2])
        if s == 1:
            wait_bytes(wbuf.at[pl.ds(0, NY - 1)], r_w)
            weights = unpack(sum_slots(wbuf, NY))
            umat[...] = exact_dot(weights[:, :RANK], minv[0])

        @pl.when(pt_owner)
        def _():
            correction = 0.0
            if s == 1:
                past = jnp.concatenate([pt[0, 0, x, z], pt[0, 1, x, z]], axis=0).astype(F32)
                own_rows = umat[pl.ds(pl.multiple_of(c * HALF, HALF), HALF), :]
                correction = exact_dot(own_rows, past)
            ptrs[s, chip] = ptsrc[s, x, z]
            wait_bytes(ptrs.at[s, pl.ds(0, CHIPS - 1)], r_prs.at[s])
            total = sum_slots(ptrs.at[s], CHIPS) * (1.0 / 64.0) - correction
            pt[s, c, x, z] = total.astype(BF)
            for dx in (0, 1, 3, 2):
                for dz in (4, 3, 5, 2, 6, 1, 7) + ((0,) if dx else ()):
                    there = zx_chip(dz, dx)
                    send(pt.at[s, c, x, z], pt.at[s, c, x, z], s_pag.at[s], r_pag.at[s, x], zx_dev(there))

        sent(ptrs.at[s, pl.ds(0, CHIPS - 1)], s_pag.at[s], pt_owner)

        mx = mx0 if s == 0 else mx1
        mixed = [None] * used
        for dx in (0, 1, 3, 2):
            g = lax.rem(x + dx, NX)
            if dx == 0:

                @pl.when(pt_owner)
                def _():
                    wait_bytes(pt.at[s, c, x, pl.ds(0, 6)], r_pag.at[s, x])

                @pl.when(jnp.logical_not(pt_owner))
                def _():
                    wait_bytes(pt.at[s, c, x], r_pag.at[s, x])

            else:
                wait_bytes(pt.at[s, c, g], r_pag.at[s, g])
            cols = pl.ds(pl.multiple_of(g * GROUP, GROUP), GROUP)
            rows = jnp.concatenate([pt[s, c, g, n] for n in range(7)], axis=1)
            for j in range(used):
                term = nt_dot(rows, hbuf[j, :, :, :, cols].reshape(256, GROUP))
                mixed[j] = term if mixed[j] is None else mixed[j] + term
        for j in range(used):
            mx[y, :, j * 256 : (j + 1) * 256] = mixed[j].astype(BF)
        for k in Y_ORDER:
            send(mx.at[y], mx.at[y], s_mx.at[s], r_mx.at[s], y_dev(k))
        sent(mx.at[pl.ds(0, NY - 1)], s_mx.at[s])

        send(pt.at[s, c], pt.at[s, c], s_ptc.at[s], r_ptc.at[s], sib)
        sent(pt.at[s, 0], s_ptc.at[s])
        if s == 0:
            share_t(0)

        wait_bytes(pt.at[s, 0], r_ptc.at[s])

        def both(step):
            return jnp.concatenate(
                [
                    jnp.concatenate([pt[step, e, g, n] for g in range(NX) for n in range(7)], axis=1)
                    for e in range(2)
                ],
                axis=0,
            )

        now = both(s)
        other = now if s == 0 else both(0)
        gram = gram0 if s == 0 else gram1
        gram[y] = pack(nt_dot(now, jnp.concatenate([now, other, now, other], axis=0)), gram.shape[1])
        for k in Y_ORDER:
            send(gram.at[y], gram.at[y], s_g.at[s], r_g.at[s], y_dev(k))
        sent(gram.at[pl.ds(0, NY - 1)], s_g.at[s])

        wait_bytes(mx.at[pl.ds(0, NY - 1)], r_mx.at[s])
        mixed = sum_slots(mx, NY).astype(BF)

        if s == 0:
            wait_bytes(tbuf.at[0, :, 0], r_tc.at[0])
        part = None
        for j in range(used):
            term = dot(mixed[:, j * 256 : (j + 1) * 256], tbuf[j].reshape(256, 1024))
            part = term if part is None else part + term
        for b in range(QBLOCKS):
            zsrc[s, b] = part[:, b * LANES : (b + 1) * LANES]
        for dz in (4, 3, 5, 2, 6, 1, 7, 0):
            b = lax.rem(z + dz, NZ)
            for h in range(2):
                there = b * NX + lax.rem(b + c, 2) + 2 * h

                @pl.when(there != chip)
                def _(b=b, h=h, there=there):
                    send(zsrc.at[s, b, pl.ds(8 * h, 8)], zrs.at[s, chip], s_zrs.at[s], r_zrs.at[s], zx_dev(there))

        sent(zrs.at[s, pl.ds(0, 15)], s_zrs.at[s], q_owner)
        sent(zrs.at[s, pl.ds(0, 16)], s_zrs.at[s], jnp.logical_not(q_owner))
        if s == 0:
            share_t(1)

        wait_bytes(gram.at[pl.ds(0, NY - 1)], r_g.at[s])
        inner = unpack(sum_slots(gram, NY))
        minv[s] = inverse_lower(inner)
        if s == 1:
            cross = lax.dot_general(
                inner[:, RANK : 2 * RANK], minv[0], (((1,), (1,)), ((), ())),
                preferred_element_type=F32, precision=lax.Precision.HIGHEST,
            )
            shift = exact_dot(cross, qf[...])

        @pl.when(q_owner)
        def _():
            mine = pl.ds(pl.multiple_of(8 * lax.div(x, 2), 8), 8)
            zrs[s, chip] = zsrc[s, z, mine, :]
            wait_bytes(zrs.at[s, pl.ds(0, CHIPS - 1)], r_zrs.at[s])
            zall[s, c, z, mine, :] = sum_slots(zrs.at[s], CHIPS) * (1.0 / 64.0)
            for d in ZX_ORDER:
                there = zx_chip(*d)
                send(zall.at[s, c, z, mine], zall.at[s, c, z, mine], s_qag.at[s], r_qag.at[s], zx_dev(there))
            wait_bytes(zrs.at[s, pl.ds(0, 15)], r_qag.at[s])

        sent(zrs.at[s, pl.ds(0, CHIPS - 1)], s_qag.at[s], q_owner)

        @pl.when(jnp.logical_not(q_owner))
        def _():
            wait_bytes(zrs.at[s, pl.ds(0, 16)], r_qag.at[s])

        send(zall.at[s, c], zall.at[s, c], s_zx.at[s], r_zx.at[s], sib)
        sent(zall.at[s, 0], s_zx.at[s])
        wait_bytes(zall.at[s, 0], r_zx.at[s])
        value = jnp.concatenate(
            [jnp.concatenate([zall[s, e, b] for b in range(QBLOCKS)], axis=1) for e in range(2)], axis=0
        )
        if s == 1:
            value = value - shift
        value = exact_dot(minv[s], value)
        if s == 0:
            qf[...] = value
            rows = qf[pl.ds(pl.multiple_of(c * HALF, HALF), HALF), :].astype(BF)
            wait_bytes(tbuf.at[1, :, 0], r_tc.at[1])
            for j in range(2):
                sk1[y, :, j * 256 : (j + 1) * 256] = nt_dot(rows, tbuf[j].reshape(256, 1024)).astype(BF)
            for k in Y_ORDER:
                send(sk1.at[y], sk1.at[y], s_sk.at[1], r_sk.at[1], y_dev(k))
            sent(sk1.at[pl.ds(0, NY - 1)], s_sk.at[1])
            wbuf[y] = pack(exact_nt_dot(value, jnp.concatenate([value] * 4, axis=0)), 8)
            for k in Y_ORDER:
                send(wbuf.at[y], wbuf.at[y], s_w, r_w, y_dev(k))
            sent(wbuf.at[pl.ds(0, NY - 1)], s_w)
            wait_bytes(sk1.at[pl.ds(0, NY - 1)], r_sk.at[1])
            left = sum_slots(sk1, NY).astype(BF)
        else:
            out[...] = value

    finish()


def on_device(hidden, cotangent, start_q):
    hidden = hidden.reshape(2, NY, 16, 3584)
    dma = pltpu.SemaphoreType.DMA
    vm = pltpu.VMEM
    in_hbm = pl.BlockSpec(memory_space=pltpu.HBM)
    return pl.pallas_call(
        kernel,
        out_shape=jax.ShapeDtypeStruct((RANK, 1024), F32),
        in_specs=[in_hbm] * 3,
        out_specs=pl.BlockSpec(memory_space=pltpu.VMEM),
        scratch_shapes=[
            vm((2, NY, 2, 16, 3584), BF),
            vm((2, 16, 8192), BF),
            vm((2, NY, 2, 16, 1024), BF),
            vm((RANK, 1024), F32),
            vm((HALF, 1024), BF),
            vm((NY - 1, HALF, 1024), BF),
            vm((NY, HALF, LANES), BF),
            vm((NY, HALF, 512), BF),
            vm((2, NX, 7, HALF, LANES), BF),
            vm((2, CHIPS, HALF, LANES), BF),
            vm((2, 2, NX, 7, HALF, LANES), BF),
            vm((NY, HALF, 256), BF),
            vm((NY, HALF, 512), BF),
            vm((NY, 8, LANES), F32),
            vm((NY, 16, LANES), F32),
            vm((NY, 8, LANES), F32),
            vm((2, QBLOCKS, HALF, LANES), F32),
            vm((2, CHIPS, 8, LANES), F32),
            vm((2, 2, QBLOCKS, HALF, LANES), F32),
            vm((2, RANK, RANK), F32),
            vm((RANK, RANK), F32),
            dma((6,)),
            dma((3,)), dma((3,)),
            dma, dma((NY - 1,)),
            dma((2,)), dma((2,)),
            dma((2,)), dma((2,)),
            dma((2,)), dma((2,)),
            dma((2,)), dma((2,)),
            dma((2,)), dma((2, NX)),
            dma((2,)), dma((2,)),
            dma((2,)), dma((2,)),
            dma((2,)), dma((2,)),
            dma, dma,
            dma((2,)), dma((2,)),
            dma((2,)), dma((2,)),
            dma((2,)), dma((2,)),
        ],
        compiler_params=pltpu.CompilerParams(
            collective_id=0, has_side_effects=True, vmem_limit_bytes=62 * 1024 * 1024
        ),
        name="powersgd",
    )(hidden, cotangent, start_q)


def solution(mesh):
    return jax.shard_map(
        on_device,
        mesh=mesh,
        in_specs=(P(None, "dp", "mp"), P(None, ("dp", "mp"), None), P(None, "mp")),
        out_specs=P(None, "mp"),
        check_vma=False,
    )
```

```python
import functools

import jax
import jax.numpy as jnp
from jax import lax
from jax.experimental import pallas as pl
from jax.experimental.pallas import tpu as pltpu
from jax.sharding import PartitionSpec as P

MESH = pl.DeviceIdType.MESH
BF = jnp.bfloat16
F32 = jnp.float32
NY = 8
NZ = 8
NX = 4
CHIPS = NZ * NX
TILES = 28
QBLOCKS = 8
HALF = 16
RANK = 32
LANES = 128
GROUP = 7 * LANES
Y_ORDER = (4, 3, 5, 2, 6, 1, 7)


def _hops(dz, dx):
    return min(dz, NZ - dz) + min(dx, NX - dx)


ZX_ORDER = sorted(
    [(dz, dx) for dz in range(NZ) for dx in range(NX) if (dz, dx) != (0, 0)],
    key=lambda d: (-_hops(*d), d),
)
NEAR_ORDER = [d for d in ZX_ORDER if _hops(*d) < 3 or (_hops(*d) == 3 and d[0] < 4)]


def nt_dot(a, b):
    return lax.dot_general(a, b, (((1,), (1,)), ((), ())), preferred_element_type=F32)


def dot(a, b):
    return jnp.dot(a, b, preferred_element_type=F32)


def exact_dot(a, b):
    return jnp.dot(a, b, preferred_element_type=F32, precision=lax.Precision.HIGHEST)


def wait_bytes(ref, sem):
    pltpu.make_async_copy(ref, ref, sem).wait()


def exact_nt_dot(a, b):
    return lax.dot_general(
        a, b, (((1,), (1,)), ((), ())), preferred_element_type=F32, precision=lax.Precision.HIGHEST
    )


def pack(value, rows):
    width = LANES * rows // RANK
    lanes = lax.broadcasted_iota(jnp.int32, (rows, LANES), 1)
    packed = value[:rows]
    for k in range(1, RANK // rows):
        packed = jnp.where(lanes >= k * width, value[k * rows : (k + 1) * rows], packed)
    return packed


def unpack(packed):
    rows = packed.shape[0]
    width = LANES * rows // RANK
    return jnp.concatenate(
        [packed] + [pltpu.roll(packed, LANES - k * width, 1) for k in range(1, RANK // rows)], axis=0
    )


def sum_slots(ref, count):
    terms = [ref[n].astype(F32) for n in range(count)]
    while len(terms) > 1:
        terms = [a + b for a, b in zip(terms[::2], terms[1::2])]
    return terms[0]


def inverse_lower(gram):
    rows = lax.broadcasted_iota(jnp.int32, (RANK, LANES), 0)
    lanes = lax.broadcasted_iota(jnp.int32, (RANK, LANES), 1)
    work = jnp.where(lanes < RANK, gram, jnp.where(lanes == rows + RANK, 1.0, 0.0))
    row_ids = lax.broadcasted_iota(jnp.int32, (RANK, 1), 0)
    scale = jnp.zeros((RANK, 1), F32)
    for j in range(RANK):
        row = work[j : j + 1, :]
        pivot = work[j : j + 1, j : j + 1]
        scale = jnp.where(row_ids == j, pivot, scale)
        if j < RANK - 1:
            factor = jnp.where(row_ids > j, work[:, j : j + 1] / pivot, 0.0)
            work = work - factor * row
    return (work * lax.rsqrt(scale))[:, RANK : 2 * RANK]


def kernel(
    hid, cot, startq, out,
    hbuf, cbuf, tbuf, qf, qsrc, qgat, sk0, sk1, ptsrc, ptrs, pt, mx0, mx1, gram0, gram1, wbuf,
    zsrc, zrs, zall, minv, umat,
    s_local, s_core, r_core, s_q, r_q, s_sk, r_sk, s_t, r_t, s_tc, r_tc, s_prs, r_prs, s_pag, r_pag,
    s_ptc, r_ptc, s_mx, r_mx, s_g, r_g, s_w, r_w, s_zrs, r_zrs, s_zx, r_zx, s_qag, r_qag,
):
    dp = lax.axis_index("dp")
    y = lax.axis_index("mp")
    c = lax.rem(dp, 2)
    chip = lax.div(dp, 2)
    z = lax.div(chip, NX)
    x = lax.rem(chip, NX)
    sib = {"dp": dp + 1 - 2 * c, "mp": y}
    pt_owner = z < NZ - 1
    q_side = lax.rem(x + 8 - 2 * c - 2 * lax.div(z, 4), NX)
    q_owner = q_side < 2
    q_mine = lax.rem(z, 4) + 4 * lax.rem(q_side, 2)
    ending = []

    def y_dev(k):
        return {"dp": dp, "mp": lax.rem(y + k, NY)}

    def zx_chip(dz, dx):
        return lax.rem(z + dz, NZ) * NX + lax.rem(x + dx, NX)

    def zx_dev(there):
        return {"dp": there * 2 + c, "mp": y}

    def send(src, dst, ssem, rsem, dev):
        pltpu.make_async_remote_copy(
            src_ref=src, dst_ref=dst, send_sem=ssem, recv_sem=rsem, device_id=dev, device_id_type=MESH
        ).start()

    def sent(ref, sem, when=None):
        def wait():
            wait_bytes(ref, sem)

        ending.append(wait if when is None else lambda: pl.when(when)(wait))

    def finish():
        while ending:
            ending.pop(0)()

    load_q = pltpu.make_async_copy(startq, qf, s_local.at[0])
    load_q.start()
    bar = pltpu.get_barrier_semaphore()
    for k in Y_ORDER:
        pl.semaphore_signal(bar, inc=1, device_id=y_dev(k), device_id_type=MESH)
    for d in ZX_ORDER:
        pl.semaphore_signal(bar, inc=1, device_id=zx_dev(zx_chip(*d)), device_id_type=MESH)
    pl.semaphore_signal(bar, inc=1, device_id=sib, device_id_type=MESH)
    load_c = pltpu.make_async_copy(cot.at[0], cbuf.at[c], s_local.at[1])
    load_c.start()
    load_h = [pltpu.make_async_copy(hid.at[j], hbuf.at[j, :, c], s_local.at[2 + j]) for j in range(2)]
    load_h[0].start()
    load_h[1].start()
    load_q.wait()
    qsrc[...] = qf[pl.ds(pl.multiple_of(c * HALF, HALF), HALF), :].astype(BF)
    pl.semaphore_wait(bar, NY - 1 + CHIPS - 1 + 1)

    for n, k in enumerate(Y_ORDER):
        send(qsrc, qgat.at[n], s_q, r_q.at[n], y_dev(k))
    sent(qgat, s_q)
    send(cot.at[0], cbuf.at[c], s_core.at[0], r_core.at[0], sib)
    sent(cbuf.at[0], s_core.at[0])
    for j in range(2):
        send(hid.at[j], hbuf.at[j, :, c], s_core.at[1 + j], r_core.at[1 + j], sib)
        sent(hbuf.at[j, :, 0], s_core.at[1 + j])
    load_c.wait()
    wait_bytes(cbuf.at[0], r_core.at[0])

    def block_sketch(q_rows, owner):
        cols = pl.ds(pl.multiple_of(owner * 1024, 1024), 1024)
        return nt_dot(q_rows, cbuf[:, :, cols].reshape(RANK, 1024))

    sketch = block_sketch(qsrc[...], y)
    for n, k in sorted(enumerate(Y_ORDER), key=lambda e: min(e[1], NY - e[1])):
        wait_bytes(qgat.at[n], r_q.at[n])
        sketch = sketch + block_sketch(qgat[n], lax.rem(y - k + NY, NY))
    spot = lax.broadcasted_iota(jnp.int32, (RANK, LANES), 0) + RANK * lax.rem(y, 4)
    place = jnp.where(lax.broadcasted_iota(jnp.int32, (RANK, LANES), 1) == spot, 1.0, 0.0).astype(BF)
    sk0[y] = dot(sketch.astype(BF), place).astype(BF)
    for k in Y_ORDER:
        send(sk0.at[y], sk0.at[y], s_sk.at[0], r_sk.at[0], y_dev(k))
    sent(sk0.at[pl.ds(0, NY - 1)], s_sk.at[0])
    wait_bytes(sk0.at[pl.ds(0, NY - 1)], r_sk.at[0])

    own_cols = pl.ds(pl.multiple_of(y * 1024, 1024), 1024)
    load_t = [pltpu.make_async_copy(cot.at[j, :, own_cols], tbuf.at[j, y, c], s_local.at[4 + j]) for j in range(2)]

    def spread_t(j):
        for k in Y_ORDER:
            there = lax.rem(y + k, NY)
            cols = pl.ds(pl.multiple_of(there * 1024, 1024), 1024)
            send(cot.at[j, :, cols], tbuf.at[j, y, c], s_t.at[j], r_t.at[j], y_dev(k))
        sent(tbuf.at[j, pl.ds(0, NY - 1), 0], s_t.at[j])
        load_t[j].start()

    def share_t(j):
        load_t[j].wait()
        wait_bytes(tbuf.at[j, pl.ds(0, NY - 1), 0], r_t.at[j])
        send(tbuf.at[j, :, c], tbuf.at[j, :, c], s_tc.at[j], r_tc.at[j], sib)
        sent(tbuf.at[j, :, 0], s_tc.at[j])

    left = jnp.concatenate(
        [
            (sk0[0] + sk0[1]) + (sk0[2] + sk0[3]),
            (sk0[4] + sk0[5]) + (sk0[6] + sk0[7]),
        ],
        axis=1,
    )

    for s in range(2):
        used = s + 1
        if s == 0:
            load_h[0].wait()
            wait_bytes(hbuf.at[0, :, 0], r_core.at[1])
        even = lax.rem(z, 2)

        def send_tiles(g, dx, odd):
            for dz in (4, 2, 6, 0):
                n = lax.rem(z + dz + odd, NZ)

                @pl.when(jnp.logical_and(n < NZ - 1, n * NX + g != chip))
                def _(n=n, g=g):
                    send(ptsrc.at[s, g, n], ptrs.at[s, chip], s_prs.at[s], r_prs.at[s], zx_dev(n * NX + g))

        for dx in (2, 1, 3, 0):
            g = lax.rem(x + dx, NX)
            cols = pl.ds(pl.multiple_of(g * GROUP, GROUP), GROUP)
            part = None
            for j in range(used):
                term = dot(left[:, j * 256 : (j + 1) * 256], hbuf[j, :, :, :, cols].reshape(256, GROUP))
                part = term if part is None else part + term
            part = part.astype(BF)
            for n in range(7):
                ptsrc[s, g, n] = part[:, n * LANES : (n + 1) * LANES]
            send_tiles(g, dx, even)
        for dx in (2, 1, 3, 0):
            send_tiles(lax.rem(x + dx, NX), dx, 1 - even)
        if s == 0:
            spread_t(0)

        sent(ptrs.at[s, pl.ds(0, TILES - 1)], s_prs.at[s], pt_owner)
        sent(ptrs.at[s, pl.ds(0, TILES)], s_prs.at[s], jnp.logical_not(pt_owner))

        if s == 0:
            load_h[1].wait()
            wait_bytes(hbuf.at[1, :, 0], r_core.at[2])
        if s == 1:
            wait_bytes(wbuf.at[pl.ds(0, NY - 1)], r_w)
            weights = unpack(sum_slots(wbuf, NY))
            umat[...] = exact_dot(weights[:, :RANK], minv[0])

        @pl.when(pt_owner)
        def _():
            correction = 0.0
            if s == 1:
                past = jnp.concatenate([pt[0, 0, x, z], pt[0, 1, x, z]], axis=0).astype(F32)
                own_rows = umat[pl.ds(pl.multiple_of(c * HALF, HALF), HALF), :]
                correction = exact_dot(own_rows, past)
            ptrs[s, chip] = ptsrc[s, x, z]
            wait_bytes(ptrs.at[s, pl.ds(0, CHIPS - 1)], r_prs.at[s])
            total = sum_slots(ptrs.at[s], CHIPS) * (1.0 / 64.0) - correction
            pt[s, c, x, z] = total.astype(BF)
            for dx in (0, 1, 3, 2):
                for dz in (4, 3, 5, 2, 6, 1, 7) + ((0,) if dx else ()):
                    there = zx_chip(dz, dx)
                    send(pt.at[s, c, x, z], pt.at[s, c, x, z], s_pag.at[s], r_pag.at[s, x], zx_dev(there))

        sent(ptrs.at[s, pl.ds(0, CHIPS - 1)], s_pag.at[s], pt_owner)

        mx = mx0 if s == 0 else mx1
        mixed = [None] * used
        for dx in (0, 1, 3, 2):
            g = lax.rem(x + dx, NX)
            if dx == 0:

                @pl.when(pt_owner)
                def _():
                    wait_bytes(pt.at[s, c, x, pl.ds(0, 6)], r_pag.at[s, x])

                @pl.when(jnp.logical_not(pt_owner))
                def _():
                    wait_bytes(pt.at[s, c, x], r_pag.at[s, x])

            else:
                wait_bytes(pt.at[s, c, g], r_pag.at[s, g])
            cols = pl.ds(pl.multiple_of(g * GROUP, GROUP), GROUP)
            rows = jnp.concatenate([pt[s, c, g, n] for n in range(7)], axis=1)
            for j in range(used):
                term = nt_dot(rows, hbuf[j, :, :, :, cols].reshape(256, GROUP))
                mixed[j] = term if mixed[j] is None else mixed[j] + term
        for j in range(used):
            mx[y, :, j * 256 : (j + 1) * 256] = mixed[j].astype(BF)
        for k in Y_ORDER:
            send(mx.at[y], mx.at[y], s_mx.at[s], r_mx.at[s], y_dev(k))
        sent(mx.at[pl.ds(0, NY - 1)], s_mx.at[s])

        send(pt.at[s, c], pt.at[s, c], s_ptc.at[s], r_ptc.at[s], sib)
        sent(pt.at[s, 0], s_ptc.at[s])
        if s == 0:
            share_t(0)

        wait_bytes(pt.at[s, 0], r_ptc.at[s])

        def both(step):
            return jnp.concatenate(
                [
                    jnp.concatenate([pt[step, e, g, n] for g in range(NX) for n in range(7)], axis=1)
                    for e in range(2)
                ],
                axis=0,
            )

        now = both(s)
        other = now if s == 0 else both(0)
        gram = gram0 if s == 0 else gram1
        gram[y] = pack(nt_dot(now, jnp.concatenate([now, other, now, other], axis=0)), gram.shape[1])
        for k in Y_ORDER:
            send(gram.at[y], gram.at[y], s_g.at[s], r_g.at[s], y_dev(k))
        sent(gram.at[pl.ds(0, NY - 1)], s_g.at[s])
        if s == 0:
            spread_t(1)

        wait_bytes(mx.at[pl.ds(0, NY - 1)], r_mx.at[s])
        mixed = sum_slots(mx, NY).astype(BF)

        if s == 0:
            wait_bytes(tbuf.at[0, :, 0], r_tc.at[0])
        part = None
        for j in range(used):
            term = dot(mixed[:, j * 256 : (j + 1) * 256], tbuf[j].reshape(256, 1024))
            part = term if part is None else part + term
        part = part.astype(BF)
        for b in range(QBLOCKS):
            zsrc[s, b] = part[:, b * LANES : (b + 1) * LANES]
        for dz in (4, 3, 5, 2, 6, 1, 7, 0):
            n = lax.rem(z + dz, NZ)
            for h in range(2):
                b = lax.rem(n, 4) + 4 * h
                there = n * NX + lax.rem(h + 2 * c + 2 * lax.div(n, 4), NX)

                @pl.when(there != chip)
                def _(b=b, there=there):
                    send(zsrc.at[s, b], zrs.at[s, chip], s_zrs.at[s], r_zrs.at[s], zx_dev(there))

        sent(zrs.at[s, pl.ds(0, 15)], s_zrs.at[s], q_owner)
        sent(zrs.at[s, pl.ds(0, 16)], s_zrs.at[s], jnp.logical_not(q_owner))

        wait_bytes(gram.at[pl.ds(0, NY - 1)], r_g.at[s])
        inner = unpack(sum_slots(gram, NY))
        minv[s] = inverse_lower(inner)
        if s == 1:
            cross = lax.dot_general(
                inner[:, RANK : 2 * RANK], minv[0], (((1,), (1,)), ((), ())),
                preferred_element_type=F32, precision=lax.Precision.HIGHEST,
            )
            shift = exact_dot(cross, qf[...])

        @pl.when(q_owner)
        def _():
            zrs[s, chip] = zsrc[s, q_mine]
            wait_bytes(zrs.at[s, pl.ds(0, CHIPS - 1)], r_zrs.at[s])
            zall[s, c, q_mine] = sum_slots(zrs.at[s], CHIPS) * (1.0 / 64.0)
            for d in NEAR_ORDER:
                there = zx_chip(*d)
                send(zall.at[s, c, q_mine], zall.at[s, c, q_mine], s_qag.at[s], r_qag.at[s], zx_dev(there))

        sent(zall.at[s, :, pl.ds(0, 7)], s_qag.at[s], q_owner)
        sent(zall.at[s, 0, 0], s_qag.at[s], q_owner)
        if s == 0:
            share_t(1)
        else:
            finish()

        @pl.when(q_owner)
        def _():
            wait_bytes(zall.at[s, c, pl.ds(0, QBLOCKS - 1)], r_qag.at[s])

        @pl.when(jnp.logical_not(q_owner))
        def _():
            wait_bytes(zall.at[s, c], r_qag.at[s])

        send(zall.at[s, c], zall.at[s, c], s_zx.at[s], r_zx.at[s], sib)
        sent(zall.at[s, 0], s_zx.at[s])
        wait_bytes(zall.at[s, 0], r_zx.at[s])
        value = jnp.concatenate(
            [jnp.concatenate([zall[s, e, b] for b in range(QBLOCKS)], axis=1) for e in range(2)], axis=0
        )
        if s == 1:
            value = value - shift
        value = exact_dot(minv[s], value)
        if s == 0:
            qf[...] = value
            rows = qf[pl.ds(pl.multiple_of(c * HALF, HALF), HALF), :].astype(BF)
            wait_bytes(tbuf.at[1, :, 0], r_tc.at[1])
            for j in range(2):
                sk1[y, :, j * 256 : (j + 1) * 256] = nt_dot(rows, tbuf[j].reshape(256, 1024)).astype(BF)
            for k in Y_ORDER:
                send(sk1.at[y], sk1.at[y], s_sk.at[1], r_sk.at[1], y_dev(k))
            sent(sk1.at[pl.ds(0, NY - 1)], s_sk.at[1])
            wbuf[y] = pack(exact_nt_dot(value, jnp.concatenate([value] * 4, axis=0)), 8)
            for k in Y_ORDER:
                send(wbuf.at[y], wbuf.at[y], s_w, r_w, y_dev(k))
            sent(wbuf.at[pl.ds(0, NY - 1)], s_w)
            wait_bytes(sk1.at[pl.ds(0, NY - 1)], r_sk.at[1])
            left = sum_slots(sk1, NY).astype(BF)
        else:
            out[...] = value

    finish()


def on_device(hidden, cotangent, start_q):
    hidden = hidden.reshape(2, NY, 16, 3584)
    dma = pltpu.SemaphoreType.DMA
    vm = pltpu.VMEM
    in_hbm = pl.BlockSpec(memory_space=pltpu.HBM)
    return pl.pallas_call(
        kernel,
        out_shape=pltpu.VMEM((RANK, 1024), F32),
        in_specs=[in_hbm] * 3,
        out_specs=pl.BlockSpec(memory_space=pltpu.VMEM),
        scratch_shapes=[
            vm((2, NY, 2, 16, 3584), BF),
            vm((2, 16, 8192), BF),
            vm((2, NY, 2, 16, 1024), BF),
            vm((RANK, 1024), F32),
            vm((HALF, 1024), BF),
            vm((NY - 1, HALF, 1024), BF),
            vm((NY, HALF, LANES), BF),
            vm((NY, HALF, 512), BF),
            vm((2, NX, 7, HALF, LANES), BF),
            vm((2, CHIPS, HALF, LANES), BF),
            vm((2, 2, NX, 7, HALF, LANES), BF),
            vm((NY, HALF, 256), BF),
            vm((NY, HALF, 512), BF),
            vm((NY, 8, LANES), F32),
            vm((NY, 16, LANES), F32),
            vm((NY, 8, LANES), F32),
            vm((2, QBLOCKS, HALF, LANES), BF),
            vm((2, CHIPS, HALF, LANES), BF),
            vm((2, 2, QBLOCKS, HALF, LANES), F32),
            vm((2, RANK, RANK), F32),
            vm((RANK, RANK), F32),
            dma((6,)),
            dma((3,)), dma((3,)),
            dma, dma((NY - 1,)),
            dma((2,)), dma((2,)),
            dma((2,)), dma((2,)),
            dma((2,)), dma((2,)),
            dma((2,)), dma((2,)),
            dma((2,)), dma((2, NX)),
            dma((2,)), dma((2,)),
            dma((2,)), dma((2,)),
            dma((2,)), dma((2,)),
            dma, dma,
            dma((2,)), dma((2,)),
            dma((2,)), dma((2,)),
            dma((2,)), dma((2,)),
        ],
        compiler_params=pltpu.CompilerParams(
            collective_id=0, has_side_effects=True, vmem_limit_bytes=56 * 1024 * 1024
        ),
        name="powersgd",
    )(hidden, cotangent, start_q)


def solution(mesh):
    return jax.shard_map(
        on_device,
        mesh=mesh,
        in_specs=(P(None, "dp", "mp"), P(None, ("dp", "mp"), None), P(None, "mp")),
        out_specs=P(None, "mp"),
        check_vma=False,
    )
```

```python
import functools

import jax
import jax.numpy as jnp
from jax import lax
from jax.experimental import pallas as pl
from jax.experimental.pallas import tpu as pltpu
from jax.sharding import PartitionSpec as P

MESH = pl.DeviceIdType.MESH
BF = jnp.bfloat16
F32 = jnp.float32
NY = 8
NZ = 8
NX = 4
CHIPS = NZ * NX
TILES = 28
QBLOCKS = 8
HALF = 16
RANK = 32
LANES = 128
GROUP = 7 * LANES
Y_ORDER = (4, 3, 5, 2, 6, 1, 7)


def _hops(dz, dx):
    return min(dz, NZ - dz) + min(dx, NX - dx)


ZX_ORDER = sorted(
    [(dz, dx) for dz in range(NZ) for dx in range(NX) if (dz, dx) != (0, 0)],
    key=lambda d: (-_hops(*d), d),
)
NEAR_ORDER = [d for d in ZX_ORDER if _hops(*d) < 3 or (_hops(*d) == 3 and d[0] < 4)]


def nt_dot(a, b):
    return lax.dot_general(a, b, (((1,), (1,)), ((), ())), preferred_element_type=F32)


def dot(a, b):
    return jnp.dot(a, b, preferred_element_type=F32)


def exact_dot(a, b):
    return jnp.dot(a, b, preferred_element_type=F32, precision=lax.Precision.HIGHEST)


def wait_bytes(ref, sem):
    pltpu.make_async_copy(ref, ref, sem).wait()


def exact_nt_dot(a, b):
    return lax.dot_general(
        a, b, (((1,), (1,)), ((), ())), preferred_element_type=F32, precision=lax.Precision.HIGHEST
    )


def pack(value, rows):
    width = LANES * rows // RANK
    lanes = lax.broadcasted_iota(jnp.int32, (rows, LANES), 1)
    packed = value[:rows]
    for k in range(1, RANK // rows):
        packed = jnp.where(lanes >= k * width, value[k * rows : (k + 1) * rows], packed)
    return packed


def unpack(packed):
    rows = packed.shape[0]
    width = LANES * rows // RANK
    return jnp.concatenate(
        [packed] + [pltpu.roll(packed, LANES - k * width, 1) for k in range(1, RANK // rows)], axis=0
    )


def sum_slots(ref, count):
    terms = [ref[n].astype(F32) for n in range(count)]
    while len(terms) > 1:
        terms = [a + b for a, b in zip(terms[::2], terms[1::2])]
    return terms[0]


def inverse_lower(gram):
    rows = lax.broadcasted_iota(jnp.int32, (RANK, LANES), 0)
    lanes = lax.broadcasted_iota(jnp.int32, (RANK, LANES), 1)
    work = jnp.where(lanes < RANK, gram, jnp.where(lanes == rows + RANK, 1.0, 0.0))
    row_ids = lax.broadcasted_iota(jnp.int32, (RANK, 1), 0)
    scale = jnp.zeros((RANK, 1), F32)
    for j in range(RANK):
        row = work[j : j + 1, :]
        pivot = work[j : j + 1, j : j + 1]
        scale = jnp.where(row_ids == j, pivot, scale)
        if j < RANK - 1:
            factor = jnp.where(row_ids > j, work[:, j : j + 1] / pivot, 0.0)
            work = work - factor * row
    return (work * lax.rsqrt(scale))[:, RANK : 2 * RANK]


def kernel(
    hid, cot, startq, out,
    hbuf, cbuf, tbuf, qf, qsrc, qgat, sk0, sk1, ptsrc, ptrs, pt, mx, part0, gram0, gram1, wbuf,
    zsrc, zrs, zall, minv, umat,
    s_local, s_core, r_core, s_q, r_q, s_sk, r_sk, s_t, r_t, s_tc, r_tc, s_prs, r_prs, s_pag, r_pag,
    s_ptc, r_ptc, s_mx, r_mx, s_g, r_g, s_w, r_w, s_zrs, r_zrs, s_qag, r_qag,
):
    dp = lax.axis_index("dp")
    y = lax.axis_index("mp")
    c = lax.rem(dp, 2)
    chip = lax.div(dp, 2)
    z = lax.div(chip, NX)
    x = lax.rem(chip, NX)
    sib = {"dp": dp + 1 - 2 * c, "mp": y}
    pt_owner = z < NZ - 1
    q_side = lax.rem(x + 8 - 2 * c - 2 * lax.div(z, 4), NX)
    q_owner = q_side < 2
    q_mine = lax.rem(z, 4) + 4 * lax.rem(q_side, 2)
    ending = []

    def y_dev(k):
        return {"dp": dp, "mp": lax.rem(y + k, NY)}

    def zx_chip(dz, dx):
        return lax.rem(z + dz, NZ) * NX + lax.rem(x + dx, NX)

    def zx_dev(there, core=None):
        return {"dp": there * 2 + (c if core is None else core), "mp": y}

    def send(src, dst, ssem, rsem, dev):
        pltpu.make_async_remote_copy(
            src_ref=src, dst_ref=dst, send_sem=ssem, recv_sem=rsem, device_id=dev, device_id_type=MESH
        ).start()

    def sent(ref, sem, when=None):
        def wait():
            wait_bytes(ref, sem)

        ending.append(wait if when is None else lambda: pl.when(when)(wait))

    def finish():
        while ending:
            ending.pop(0)()

    load_q = pltpu.make_async_copy(startq, qf, s_local.at[0])
    load_q.start()
    bar = pltpu.get_barrier_semaphore()
    for k in Y_ORDER:
        pl.semaphore_signal(bar, inc=1, device_id=y_dev(k), device_id_type=MESH)
    for d in ZX_ORDER:
        pl.semaphore_signal(bar, inc=1, device_id=zx_dev(zx_chip(*d)), device_id_type=MESH)
    for dz, dx in NEAR_ORDER:
        back = zx_dev(zx_chip(NZ - dz, NX - dx), 1 - c)
        pl.semaphore_signal(bar, inc=1, device_id=back, device_id_type=MESH)
    pl.semaphore_signal(bar, inc=1, device_id=sib, device_id_type=MESH)
    load_c = pltpu.make_async_copy(cot.at[0], cbuf.at[c], s_local.at[1])
    load_c.start()
    load_h = [pltpu.make_async_copy(hid.at[j], hbuf.at[j, :, c], s_local.at[2 + j]) for j in range(2)]
    load_h[0].start()
    load_h[1].start()
    load_q.wait()
    qsrc[...] = qf[pl.ds(pl.multiple_of(c * HALF, HALF), HALF), :].astype(BF)
    pl.semaphore_wait(bar, NY - 1 + CHIPS - 1 + len(NEAR_ORDER) + 1)

    for n, k in enumerate(Y_ORDER):
        send(qsrc, qgat.at[n], s_q, r_q.at[n], y_dev(k))
    sent(qgat, s_q)
    send(cot.at[0], cbuf.at[c], s_core.at[0], r_core.at[0], sib)
    sent(cbuf.at[0], s_core.at[0])
    for j in range(2):
        send(hid.at[j], hbuf.at[j, :, c], s_core.at[1 + j], r_core.at[1 + j], sib)
        sent(hbuf.at[j, :, 0], s_core.at[1 + j])
    load_c.wait()
    wait_bytes(cbuf.at[0], r_core.at[0])

    def block_sketch(q_rows, owner):
        cols = pl.ds(pl.multiple_of(owner * 1024, 1024), 1024)
        return nt_dot(q_rows, cbuf[:, :, cols].reshape(RANK, 1024))

    sketch = block_sketch(qsrc[...], y)
    for n, k in sorted(enumerate(Y_ORDER), key=lambda e: min(e[1], NY - e[1])):
        wait_bytes(qgat.at[n], r_q.at[n])
        sketch = sketch + block_sketch(qgat[n], lax.rem(y - k + NY, NY))
    spot = lax.broadcasted_iota(jnp.int32, (RANK, LANES), 0) + RANK * lax.rem(y, 4)
    place = jnp.where(lax.broadcasted_iota(jnp.int32, (RANK, LANES), 1) == spot, 1.0, 0.0).astype(BF)
    sk0[y] = dot(sketch.astype(BF), place).astype(BF)
    for k in Y_ORDER:
        send(sk0.at[y], sk0.at[y], s_sk.at[0], r_sk.at[0], y_dev(k))
    sent(sk0.at[pl.ds(0, NY - 1)], s_sk.at[0])
    wait_bytes(sk0.at[pl.ds(0, NY - 1)], r_sk.at[0])

    own_cols = pl.ds(pl.multiple_of(y * 1024, 1024), 1024)
    load_t = [pltpu.make_async_copy(cot.at[j, :, own_cols], tbuf.at[j, y, c], s_local.at[4 + j]) for j in range(2)]

    def spread_t(j):
        for k in Y_ORDER:
            there = lax.rem(y + k, NY)
            cols = pl.ds(pl.multiple_of(there * 1024, 1024), 1024)
            send(cot.at[j, :, cols], tbuf.at[j, y, c], s_t.at[j], r_t.at[j], y_dev(k))
        sent(tbuf.at[j, pl.ds(0, NY - 1), 0], s_t.at[j])
        load_t[j].start()

    def share_t(j):
        load_t[j].wait()
        wait_bytes(tbuf.at[j, pl.ds(0, NY - 1), 0], r_t.at[j])
        send(tbuf.at[j, :, c], tbuf.at[j, :, c], s_tc.at[j], r_tc.at[j], sib)
        sent(tbuf.at[j, :, 0], s_tc.at[j])

    left = jnp.concatenate(
        [
            (sk0[0] + sk0[1]) + (sk0[2] + sk0[3]),
            (sk0[4] + sk0[5]) + (sk0[6] + sk0[7]),
        ],
        axis=1,
    )

    for s in range(2):
        used = s + 1
        if s == 0:
            load_h[0].wait()
            wait_bytes(hbuf.at[0, :, 0], r_core.at[1])
        even = lax.rem(z, 2)

        def send_tiles(g, dx, odd):
            for dz in (4, 2, 6, 0):
                n = lax.rem(z + dz + odd, NZ)

                @pl.when(jnp.logical_and(n < NZ - 1, n * NX + g != chip))
                def _(n=n, g=g):
                    send(ptsrc.at[s, g, n], ptrs.at[s, chip], s_prs.at[s], r_prs.at[s], zx_dev(n * NX + g))

        if s == 1:
            wait_bytes(sk1.at[0, pl.ds(0, NY - 1)], r_sk.at[1])
            part0[...] = dot(sum_slots(sk1.at[0], NY).astype(BF), hbuf[0].reshape(256, 3584))
            wait_bytes(sk1.at[1, pl.ds(0, NY - 1)], r_sk.at[2])
            left = sum_slots(sk1.at[1], NY).astype(BF)
        for dx in (2, 1, 3, 0):
            g = lax.rem(x + dx, NX)
            cols = pl.ds(pl.multiple_of(g * GROUP, GROUP), GROUP)
            part = dot(left, hbuf[s, :, :, :, cols].reshape(256, GROUP))
            if s == 1:
                part = part + part0[:, cols]
            part = part.astype(BF)
            for n in range(7):
                ptsrc[s, g, n] = part[:, n * LANES : (n + 1) * LANES]
            send_tiles(g, dx, even)
        for dx in (2, 1, 3, 0):
            send_tiles(lax.rem(x + dx, NX), dx, 1 - even)
        if s == 0:
            spread_t(0)

        sent(ptrs.at[s, pl.ds(0, TILES - 1)], s_prs.at[s], pt_owner)
        sent(ptrs.at[s, pl.ds(0, TILES)], s_prs.at[s], jnp.logical_not(pt_owner))

        if s == 0:
            load_h[1].wait()
            wait_bytes(hbuf.at[1, :, 0], r_core.at[2])
        if s == 1:
            wait_bytes(wbuf.at[pl.ds(0, NY - 1)], r_w)
            weights = unpack(sum_slots(wbuf, NY))
            umat[...] = exact_dot(weights[:, :RANK], minv[0])

        @pl.when(pt_owner)
        def _():
            correction = 0.0
            if s == 1:
                past = jnp.concatenate([pt[0, 0, x, z], pt[0, 1, x, z]], axis=0).astype(F32)
                own_rows = umat[pl.ds(pl.multiple_of(c * HALF, HALF), HALF), :]
                correction = exact_dot(own_rows, past)
            ptrs[s, chip] = ptsrc[s, x, z]
            wait_bytes(ptrs.at[s, pl.ds(0, CHIPS - 1)], r_prs.at[s])
            total = sum_slots(ptrs.at[s], CHIPS) * (1.0 / 64.0) - correction
            pt[s, c, x, z] = total.astype(BF)
            for dx in (0, 1, 3, 2):
                for dz in (4, 3, 5, 2, 6, 1, 7) + ((0,) if dx else ()):
                    there = zx_chip(dz, dx)
                    send(pt.at[s, c, x, z], pt.at[s, c, x, z], s_pag.at[s], r_pag.at[s, x], zx_dev(there))

        sent(ptrs.at[s, pl.ds(0, CHIPS - 1)], s_pag.at[s], pt_owner)

        mixed = [None] * used
        for dx in (0, 1, 3, 2):
            g = lax.rem(x + dx, NX)
            if dx == 0:

                @pl.when(pt_owner)
                def _():
                    wait_bytes(pt.at[s, c, x, pl.ds(0, 6)], r_pag.at[s, x])

                @pl.when(jnp.logical_not(pt_owner))
                def _():
                    wait_bytes(pt.at[s, c, x], r_pag.at[s, x])

            else:
                wait_bytes(pt.at[s, c, g], r_pag.at[s, g])
            cols = pl.ds(pl.multiple_of(g * GROUP, GROUP), GROUP)
            rows = jnp.concatenate([pt[s, c, g, n] for n in range(7)], axis=1)
            for j in range(used):
                term = nt_dot(rows, hbuf[j, :, :, :, cols].reshape(256, GROUP))
                mixed[j] = term if mixed[j] is None else mixed[j] + term
        for j in range(used):
            mx[s, j, y] = mixed[j].astype(BF)
            for k in Y_ORDER:
                send(mx.at[s, j, y], mx.at[s, j, y], s_mx.at[s, j], r_mx.at[s, j], y_dev(k))
            sent(mx.at[s, j, pl.ds(0, NY - 1)], s_mx.at[s, j])

        send(pt.at[s, c], pt.at[s, c], s_ptc.at[s], r_ptc.at[s], sib)
        sent(pt.at[s, 0], s_ptc.at[s])
        if s == 0:
            share_t(0)

        wait_bytes(pt.at[s, 0], r_ptc.at[s])

        def both(step):
            return jnp.concatenate(
                [
                    jnp.concatenate([pt[step, e, g, n] for g in range(NX) for n in range(7)], axis=1)
                    for e in range(2)
                ],
                axis=0,
            )

        now = both(s)
        other = now if s == 0 else both(0)
        gram = gram0 if s == 0 else gram1
        gram[y] = pack(nt_dot(now, jnp.concatenate([now, other, now, other], axis=0)), gram.shape[1])
        for k in Y_ORDER:
            send(gram.at[y], gram.at[y], s_g.at[s], r_g.at[s], y_dev(k))
        sent(gram.at[pl.ds(0, NY - 1)], s_g.at[s])
        if s == 0:
            spread_t(1)

        if s == 0:
            wait_bytes(tbuf.at[0, :, 0], r_tc.at[0])
        part = None
        for j in range(used):
            wait_bytes(mx.at[s, j, pl.ds(0, NY - 1)], r_mx.at[s, j])
            term = dot(sum_slots(mx.at[s, j], NY).astype(BF), tbuf[j].reshape(256, 1024))
            part = term if part is None else part + term
        part = part.astype(BF)
        for b in range(QBLOCKS):
            zsrc[s, b] = part[:, b * LANES : (b + 1) * LANES]
        for dz in (4, 3, 5, 2, 6, 1, 7, 0):
            n = lax.rem(z + dz, NZ)
            for h in range(2):
                b = lax.rem(n, 4) + 4 * h
                there = n * NX + lax.rem(h + 2 * c + 2 * lax.div(n, 4), NX)

                @pl.when(there != chip)
                def _(b=b, there=there):
                    send(zsrc.at[s, b], zrs.at[s, chip], s_zrs.at[s], r_zrs.at[s], zx_dev(there))

        sent(zrs.at[s, pl.ds(0, 15)], s_zrs.at[s], q_owner)
        sent(zrs.at[s, pl.ds(0, 16)], s_zrs.at[s], jnp.logical_not(q_owner))

        wait_bytes(gram.at[pl.ds(0, NY - 1)], r_g.at[s])
        inner = unpack(sum_slots(gram, NY))
        minv[s] = inverse_lower(inner)
        if s == 1:
            cross = lax.dot_general(
                inner[:, RANK : 2 * RANK], minv[0], (((1,), (1,)), ((), ())),
                preferred_element_type=F32, precision=lax.Precision.HIGHEST,
            )
            shift = exact_dot(cross, qf[...])

        z_mine = (2 * s + c) * QBLOCKS + q_mine

        @pl.when(q_owner)
        def _():
            zrs[s, chip] = zsrc[s, q_mine]
            wait_bytes(zrs.at[s, pl.ds(0, CHIPS - 1)], r_zrs.at[s])
            zall[z_mine] = sum_slots(zrs.at[s], CHIPS) * (1.0 / 64.0)
            tile = zall.at[z_mine]
            for d in NEAR_ORDER:
                for core in (c, 1 - c):
                    send(tile, tile, s_qag.at[s], r_qag.at[s], zx_dev(zx_chip(*d), core))
            send(tile, tile, s_qag.at[s], r_qag.at[s], sib)

        sent(zall.at[pl.ds(0, 31)], s_qag.at[s], q_owner)
        if s == 0:
            share_t(1)
        else:
            finish()

        @pl.when(q_owner)
        def _():
            wait_bytes(zall.at[pl.ds(0, 15)], r_qag.at[s])

        @pl.when(jnp.logical_not(q_owner))
        def _():
            wait_bytes(zall.at[pl.ds(0, 16)], r_qag.at[s])

        value = jnp.concatenate(
            [
                jnp.concatenate([zall[(2 * s + e) * QBLOCKS + b] for b in range(QBLOCKS)], axis=1)
                for e in range(2)
            ],
            axis=0,
        )
        if s == 1:
            value = value - shift
        value = exact_dot(minv[s], value)
        if s == 0:
            qf[...] = value
            rows = qf[pl.ds(pl.multiple_of(c * HALF, HALF), HALF), :].astype(BF)
            wait_bytes(tbuf.at[1, :, 0], r_tc.at[1])
            for j in range(2):
                sk1[j, y] = nt_dot(rows, tbuf[j].reshape(256, 1024)).astype(BF)
                for k in Y_ORDER:
                    send(sk1.at[j, y], sk1.at[j, y], s_sk.at[1 + j], r_sk.at[1 + j], y_dev(k))
                sent(sk1.at[j, pl.ds(0, NY - 1)], s_sk.at[1 + j])
            wbuf[y] = pack(exact_nt_dot(value, jnp.concatenate([value] * 4, axis=0)), 8)
            for k in Y_ORDER:
                send(wbuf.at[y], wbuf.at[y], s_w, r_w, y_dev(k))
            sent(wbuf.at[pl.ds(0, NY - 1)], s_w)
        else:
            out[...] = value

    finish()


def on_device(hidden, cotangent, start_q):
    hidden = hidden.reshape(2, NY, 16, 3584)
    dma = pltpu.SemaphoreType.DMA
    vm = pltpu.VMEM
    in_hbm = pl.BlockSpec(memory_space=pltpu.HBM)
    return pl.pallas_call(
        kernel,
        out_shape=pltpu.VMEM((RANK, 1024), F32),
        in_specs=[in_hbm] * 3,
        out_specs=pl.BlockSpec(memory_space=pltpu.VMEM),
        scratch_shapes=[
            vm((2, NY, 2, 16, 3584), BF),
            vm((2, 16, 8192), BF),
            vm((2, NY, 2, 16, 1024), BF),
            vm((RANK, 1024), F32),
            vm((HALF, 1024), BF),
            vm((NY - 1, HALF, 1024), BF),
            vm((NY, HALF, LANES), BF),
            vm((2, NY, HALF, 256), BF),
            vm((2, NX, 7, HALF, LANES), BF),
            vm((2, CHIPS, HALF, LANES), BF),
            vm((2, 2, NX, 7, HALF, LANES), BF),
            vm((2, 2, NY, HALF, 256), BF),
            vm((HALF, 3584), F32),
            vm((NY, 8, LANES), F32),
            vm((NY, 16, LANES), F32),
            vm((NY, 8, LANES), F32),
            vm((2, QBLOCKS, HALF, LANES), BF),
            vm((2, CHIPS, HALF, LANES), BF),
            vm((4 * QBLOCKS, HALF, LANES), F32),
            vm((2, RANK, RANK), F32),
            vm((RANK, RANK), F32),
            dma((6,)),
            dma((3,)), dma((3,)),
            dma, dma((NY - 1,)),
            dma((3,)), dma((3,)),
            dma((2,)), dma((2,)),
            dma((2,)), dma((2,)),
            dma((2,)), dma((2,)),
            dma((2,)), dma((2, NX)),
            dma((2,)), dma((2,)),
            dma((2, 2)), dma((2, 2)),
            dma((2,)), dma((2,)),
            dma, dma,
            dma((2,)), dma((2,)),
            dma((2,)), dma((2,)),
        ],
        compiler_params=pltpu.CompilerParams(
            collective_id=0, has_side_effects=True, vmem_limit_bytes=56 * 1024 * 1024
        ),
        name="powersgd",
    )(hidden, cotangent, start_q)


def solution(mesh):
    return jax.shard_map(
        on_device,
        mesh=mesh,
        in_specs=(P(None, "dp", "mp"), P(None, ("dp", "mp"), None), P(None, "mp")),
        out_specs=P(None, "mp"),
        check_vma=False,
    )
```

```python
import functools

import jax
import jax.numpy as jnp
from jax import lax
from jax.experimental import pallas as pl
from jax.experimental.pallas import tpu as pltpu
from jax.sharding import PartitionSpec as P

MESH = pl.DeviceIdType.MESH
BF = jnp.bfloat16
F32 = jnp.float32
NY = 8
NZ = 8
NX = 4
CHIPS = NZ * NX
TILES = 28
QBLOCKS = 8
HALF = 16
RANK = 32
LANES = 128
GROUP = NX * LANES
Y_ORDER = (4, 3, 5, 2, 6, 1, 7)


def _hops(dz, dx):
    return min(dz, NZ - dz) + min(dx, NX - dx)


ZX_ORDER = sorted(
    [(dz, dx) for dz in range(NZ) for dx in range(NX) if (dz, dx) != (0, 0)],
    key=lambda d: (-_hops(*d), d),
)
NEAR = ((2, 0), (1, 1), (7, 1), (1, 0), (7, 0), (0, 1), (0, 3), (0, 0))
PLANES_IN = (0, 1, 6, 2, 5, 3, 4)
PLANES_OUT = (4, 3, 5, 2, 6, 1, 0)


def nt_dot(a, b):
    return lax.dot_general(a, b, (((1,), (1,)), ((), ())), preferred_element_type=F32)


def dot(a, b):
    return jnp.dot(a, b, preferred_element_type=F32)


def exact_dot(a, b):
    return jnp.dot(a, b, preferred_element_type=F32, precision=lax.Precision.HIGHEST)


def wait_bytes(ref, sem):
    pltpu.make_async_copy(ref, ref, sem).wait()


def exact_nt_dot(a, b):
    return lax.dot_general(
        a, b, (((1,), (1,)), ((), ())), preferred_element_type=F32, precision=lax.Precision.HIGHEST
    )


def pack(value, rows):
    width = LANES * rows // RANK
    lanes = lax.broadcasted_iota(jnp.int32, (rows, LANES), 1)
    packed = value[:rows]
    for k in range(1, RANK // rows):
        packed = jnp.where(lanes >= k * width, value[k * rows : (k + 1) * rows], packed)
    return packed


def unpack(packed):
    rows = packed.shape[0]
    width = LANES * rows // RANK
    return jnp.concatenate(
        [packed] + [pltpu.roll(packed, LANES - k * width, 1) for k in range(1, RANK // rows)], axis=0
    )


def sum_slots(ref, count):
    terms = [ref[n].astype(F32) for n in range(count)]
    while len(terms) > 1:
        terms = [a + b for a, b in zip(terms[::2], terms[1::2])]
    return terms[0]


def inverse_lower(gram):
    rows = lax.broadcasted_iota(jnp.int32, (RANK, LANES), 0)
    lanes = lax.broadcasted_iota(jnp.int32, (RANK, LANES), 1)
    work = jnp.where(lanes < RANK, gram, jnp.where(lanes == rows + RANK, 1.0, 0.0))
    row_ids = lax.broadcasted_iota(jnp.int32, (RANK, 1), 0)
    scale = jnp.zeros((RANK, 1), F32)
    for j in range(RANK):
        row = work[j : j + 1, :]
        pivot = work[j : j + 1, j : j + 1]
        scale = jnp.where(row_ids == j, pivot, scale)
        if j < RANK - 1:
            factor = jnp.where(row_ids > j, work[:, j : j + 1] / pivot, 0.0)
            work = work - factor * row
    return (work * lax.rsqrt(scale))[:, RANK : 2 * RANK]


def kernel(
    hid, cot, startq, out,
    hbuf, cbuf, tbuf, qf, qsrc, qgat, sk0, sk1, ptsrc, ptrs, pt, mx, part0, gram0, gram1, wbuf,
    zsrc, zrs, zall, minv, umat,
    s_local, s_core, r_core, s_q, r_q, s_sk, r_sk, s_t, r_t, s_tc, r_tc, s_prs, r_prs, s_pag, r_pag,
    s_ptc, r_ptc, s_mx, r_mx, s_g, r_g, s_w, r_w, s_zrs, r_zrs, s_qag, r_qag,
):
    dp = lax.axis_index("dp")
    y = lax.axis_index("mp")
    c = lax.rem(dp, 2)
    chip = lax.div(dp, 2)
    z = lax.div(chip, NX)
    x = lax.rem(chip, NX)
    sib = {"dp": dp + 1 - 2 * c, "mp": y}
    pt_owner = z < NZ - 1
    q_mine = 4 * lax.rem(x, 2) + lax.rem(z + 2 * lax.div(x, 2), 4)
    ending = []

    def y_dev(k):
        return {"dp": dp, "mp": lax.rem(y + k, NY)}

    def zx_chip(dz, dx):
        return lax.rem(z + dz, NZ) * NX + lax.rem(x + dx, NX)

    def zx_dev(there, core=None):
        return {"dp": there * 2 + (c if core is None else core), "mp": y}

    def send(src, dst, ssem, rsem, dev):
        pltpu.make_async_remote_copy(
            src_ref=src, dst_ref=dst, send_sem=ssem, recv_sem=rsem, device_id=dev, device_id_type=MESH
        ).start()

    def sent(ref, sem, when=None):
        def wait():
            wait_bytes(ref, sem)

        ending.append(wait if when is None else lambda: pl.when(when)(wait))

    def finish():
        while ending:
            ending.pop(0)()

    load_q = pltpu.make_async_copy(startq, qf, s_local.at[0])
    load_q.start()
    bar = pltpu.get_barrier_semaphore()
    for k in Y_ORDER:
        pl.semaphore_signal(bar, inc=1, device_id=y_dev(k), device_id_type=MESH)
    for d in ZX_ORDER:
        pl.semaphore_signal(bar, inc=1, device_id=zx_dev(zx_chip(*d)), device_id_type=MESH)
    for dz, dx in NEAR[:-1]:
        back = zx_dev(zx_chip(NZ - dz, NX - dx), 1 - c)
        pl.semaphore_signal(bar, inc=1, device_id=back, device_id_type=MESH)
    pl.semaphore_signal(bar, inc=1, device_id=sib, device_id_type=MESH)
    load_c = pltpu.make_async_copy(cot.at[0], cbuf.at[c], s_local.at[1])
    load_c.start()
    load_h = [pltpu.make_async_copy(hid.at[j], hbuf.at[j, :, c], s_local.at[2 + j]) for j in range(2)]
    load_h[0].start()
    load_h[1].start()
    load_q.wait()
    qsrc[...] = qf[pl.ds(pl.multiple_of(c * HALF, HALF), HALF), :].astype(BF)
    pl.semaphore_wait(bar, NY - 1 + CHIPS - 1 + len(NEAR))

    for n, k in enumerate(Y_ORDER):
        send(qsrc, qgat.at[n], s_q, r_q.at[n], y_dev(k))
    sent(qgat, s_q)
    send(cot.at[0], cbuf.at[c], s_core.at[0], r_core.at[0], sib)
    sent(cbuf.at[0], s_core.at[0])
    load_c.wait()
    wait_bytes(cbuf.at[0], r_core.at[0])

    def block_sketch(q_rows, owner):
        cols = pl.ds(pl.multiple_of(owner * 1024, 1024), 1024)
        return nt_dot(q_rows, cbuf[:, :, cols].reshape(RANK, 1024))

    sketch = block_sketch(qsrc[...], y)
    for n, k in sorted(enumerate(Y_ORDER), key=lambda e: min(e[1], NY - e[1])):
        wait_bytes(qgat.at[n], r_q.at[n])
        sketch = sketch + block_sketch(qgat[n], lax.rem(y - k + NY, NY))
    spot = lax.broadcasted_iota(jnp.int32, (RANK, LANES), 0) + RANK * lax.rem(y, 4)
    place = jnp.where(lax.broadcasted_iota(jnp.int32, (RANK, LANES), 1) == spot, 1.0, 0.0).astype(BF)
    sk0[y] = dot(sketch.astype(BF), place).astype(BF)
    for k in Y_ORDER:
        send(sk0.at[y], sk0.at[y], s_sk.at[0], r_sk.at[0], y_dev(k))
    sent(sk0.at[pl.ds(0, NY - 1)], s_sk.at[0])

    def share_h(j):
        send(hid.at[j], hbuf.at[j, :, c], s_core.at[1 + j], r_core.at[1 + j], sib)
        sent(hbuf.at[j, :, 0], s_core.at[1 + j])

    share_h(0)
    wait_bytes(sk0.at[pl.ds(0, NY - 1)], r_sk.at[0])

    own_cols = pl.ds(pl.multiple_of(y * 1024, 1024), 1024)
    load_t = [pltpu.make_async_copy(cot.at[j, :, own_cols], tbuf.at[j, y, c], s_local.at[4 + j]) for j in range(2)]

    def spread_t(j):
        for k in Y_ORDER:
            there = lax.rem(y + k, NY)
            cols = pl.ds(pl.multiple_of(there * 1024, 1024), 1024)
            send(cot.at[j, :, cols], tbuf.at[j, y, c], s_t.at[j], r_t.at[j], y_dev(k))
        sent(tbuf.at[j, pl.ds(0, NY - 1), 0], s_t.at[j])
        load_t[j].start()

    def share_t(j):
        load_t[j].wait()
        wait_bytes(tbuf.at[j, pl.ds(0, NY - 1), 0], r_t.at[j])
        send(tbuf.at[j, :, c], tbuf.at[j, :, c], s_tc.at[j], r_tc.at[j], sib)
        sent(tbuf.at[j, :, 0], s_tc.at[j])

    left = jnp.concatenate(
        [
            (sk0[0] + sk0[1]) + (sk0[2] + sk0[3]),
            (sk0[4] + sk0[5]) + (sk0[6] + sk0[7]),
        ],
        axis=1,
    )

    for s in range(2):
        used = s + 1
        if s == 0:
            load_h[0].wait()
            wait_bytes(hbuf.at[0, :, 0], r_core.at[1])
        if s == 1:
            wait_bytes(sk1.at[0, pl.ds(0, NY - 1)], r_sk.at[1])
            part0[...] = dot(sum_slots(sk1.at[0], NY).astype(BF), hbuf[0].reshape(256, 3584))
            load_h[1].wait()
            wait_bytes(hbuf.at[1, :, 0], r_core.at[2])
            wait_bytes(sk1.at[1, pl.ds(0, NY - 1)], r_sk.at[2])
            left = sum_slots(sk1.at[1], NY).astype(BF)
        for step in PLANES_OUT:
            n = lax.rem(z + step, NZ - 1)
            cols = pl.ds(pl.multiple_of(n * GROUP, GROUP), GROUP)
            part = dot(left, hbuf[s, :, :, :, cols].reshape(256, GROUP))
            if s == 1:
                part = part + part0[:, cols]
            part = part.astype(BF)
            for g in range(NX):
                ptsrc[s, n * NX + g] = part[:, g * LANES : (g + 1) * LANES]
            for dx in (2, 1, 3, 0):
                there = n * NX + lax.rem(x + dx, NX)

                def post(there=there):
                    send(ptsrc.at[s, there], ptrs.at[s, chip], s_prs.at[s], r_prs.at[s], zx_dev(there))

                if step == 0 and dx == 0:
                    pl.when(jnp.logical_not(pt_owner))(post)
                else:
                    post()
        if s == 0:
            share_h(1)
            spread_t(0)

        sent(ptrs.at[s, pl.ds(0, TILES - 1)], s_prs.at[s], pt_owner)
        sent(ptrs.at[s, pl.ds(0, TILES)], s_prs.at[s], jnp.logical_not(pt_owner))

        if s == 1:
            wait_bytes(wbuf.at[pl.ds(0, NY - 1)], r_w)
            weights = unpack(sum_slots(wbuf, NY))
            umat[...] = exact_dot(weights[:, :RANK], minv[0])

        @pl.when(pt_owner)
        def _():
            correction = 0.0
            if s == 1:
                past = jnp.concatenate([pt[0, 0, chip], pt[0, 1, chip]], axis=0).astype(F32)
                own_rows = umat[pl.ds(pl.multiple_of(c * HALF, HALF), HALF), :]
                correction = exact_dot(own_rows, past)
            ptrs[s, chip] = ptsrc[s, chip]
            wait_bytes(ptrs.at[s, pl.ds(0, CHIPS - 1)], r_prs.at[s])
            total = sum_slots(ptrs.at[s], CHIPS) * (1.0 / 64.0) - correction
            pt[s, c, chip] = total.astype(BF)
            tile = pt.at[s, c, chip]
            for d in ZX_ORDER:
                send(tile, tile, s_pag.at[s], r_pag.at[s, z], zx_dev(zx_chip(*d)))

        sent(ptrs.at[s, pl.ds(0, CHIPS - 1)], s_pag.at[s], pt_owner)

        mixed = [None] * used
        for step in PLANES_IN:
            n = lax.rem(z + step, NZ - 1)
            first = pl.multiple_of(n * NX, NX)
            if step == 0:

                @pl.when(pt_owner)
                def _():
                    wait_bytes(pt.at[s, c, pl.ds(0, NX - 1)], r_pag.at[s, z])

                @pl.when(jnp.logical_not(pt_owner))
                def _():
                    wait_bytes(pt.at[s, c, pl.ds(0, NX)], r_pag.at[s, n])

            else:
                wait_bytes(pt.at[s, c, pl.ds(0, NX)], r_pag.at[s, n])
            cols = pl.ds(pl.multiple_of(n * GROUP, GROUP), GROUP)
            rows = jnp.concatenate([pt[s, c, first + g] for g in range(NX)], axis=1)
            for j in range(used):
                term = nt_dot(rows, hbuf[j, :, :, :, cols].reshape(256, GROUP))
                mixed[j] = term if mixed[j] is None else mixed[j] + term
        for j in range(used):
            mx[s, j, y] = mixed[j].astype(BF)
            for k in Y_ORDER:
                send(mx.at[s, j, y], mx.at[s, j, y], s_mx.at[s, j], r_mx.at[s, j], y_dev(k))
            sent(mx.at[s, j, pl.ds(0, NY - 1)], s_mx.at[s, j])

        send(pt.at[s, c], pt.at[s, c], s_ptc.at[s], r_ptc.at[s], sib)
        sent(pt.at[s, 0], s_ptc.at[s])
        if s == 0:
            share_t(0)

        wait_bytes(pt.at[s, 0], r_ptc.at[s])

        def both(step):
            return jnp.concatenate(
                [
                    jnp.concatenate([pt[step, e, n] for n in range(TILES)], axis=1)
                    for e in range(2)
                ],
                axis=0,
            )

        now = both(s)
        other = now if s == 0 else both(0)
        gram = gram0 if s == 0 else gram1
        gram[y] = pack(nt_dot(now, jnp.concatenate([now, other, now, other], axis=0)), gram.shape[1])
        for k in Y_ORDER:
            send(gram.at[y], gram.at[y], s_g.at[s], r_g.at[s], y_dev(k))
        sent(gram.at[pl.ds(0, NY - 1)], s_g.at[s])
        if s == 0:
            spread_t(1)

        if s == 0:
            wait_bytes(tbuf.at[0, :, 0], r_tc.at[0])
        part = None
        for j in range(used):
            wait_bytes(mx.at[s, j, pl.ds(0, NY - 1)], r_mx.at[s, j])
            term = dot(sum_slots(mx.at[s, j], NY).astype(BF), tbuf[j].reshape(256, 1024))
            part = term if part is None else part + term
        part = part.astype(BF)
        for b in range(QBLOCKS):
            zsrc[s, b] = part[:, b * LANES : (b + 1) * LANES]
        for dz, dx in ZX_ORDER:
            there = zx_chip(dz, dx)
            b = 4 * lax.rem(x + dx, 2) + lax.rem(z + dz + 2 * lax.div(lax.rem(x + dx, NX), 2), 4)
            send(zsrc.at[s, b], zrs.at[s, chip], s_zrs.at[s], r_zrs.at[s], zx_dev(there))
        sent(zrs.at[s, pl.ds(0, CHIPS - 1)], s_zrs.at[s])

        wait_bytes(gram.at[pl.ds(0, NY - 1)], r_g.at[s])
        inner = unpack(sum_slots(gram, NY))
        minv[s] = inverse_lower(inner)
        if s == 1:
            cross = lax.dot_general(
                inner[:, RANK : 2 * RANK], minv[0], (((1,), (1,)), ((), ())),
                preferred_element_type=F32, precision=lax.Precision.HIGHEST,
            )
            shift = exact_dot(cross, qf[...])

        z_mine = (2 * s + c) * QBLOCKS + q_mine

        zrs[s, chip] = zsrc[s, q_mine]
        wait_bytes(zrs.at[s, pl.ds(0, CHIPS - 1)], r_zrs.at[s])
        zall[z_mine] = sum_slots(zrs.at[s], CHIPS) * (1.0 / 64.0)
        tile = zall.at[z_mine]
        for d in NEAR:
            for core in (c, 1 - c) if d != (0, 0) else (1 - c,):
                send(tile, tile, s_qag.at[s], r_qag.at[s], zx_dev(zx_chip(*d), core))
        sent(zall.at[pl.ds(0, 15)], s_qag.at[s])
        if s == 0:
            share_t(1)
        else:
            finish()
        wait_bytes(zall.at[pl.ds(0, 15)], r_qag.at[s])
        value = jnp.concatenate(
            [
                jnp.concatenate([zall[(2 * s + e) * QBLOCKS + b] for b in range(QBLOCKS)], axis=1)
                for e in range(2)
            ],
            axis=0,
        )
        if s == 1:
            value = value - shift
        value = exact_dot(minv[s], value)
        if s == 0:
            qf[...] = value
            rows = qf[pl.ds(pl.multiple_of(c * HALF, HALF), HALF), :].astype(BF)
            wait_bytes(tbuf.at[1, :, 0], r_tc.at[1])
            for j in range(2):
                sk1[j, y] = nt_dot(rows, tbuf[j].reshape(256, 1024)).astype(BF)
                for k in Y_ORDER:
                    send(sk1.at[j, y], sk1.at[j, y], s_sk.at[1 + j], r_sk.at[1 + j], y_dev(k))
                sent(sk1.at[j, pl.ds(0, NY - 1)], s_sk.at[1 + j])
            wbuf[y] = pack(exact_nt_dot(value, jnp.concatenate([value] * 4, axis=0)), 8)
            for k in Y_ORDER:
                send(wbuf.at[y], wbuf.at[y], s_w, r_w, y_dev(k))
            sent(wbuf.at[pl.ds(0, NY - 1)], s_w)
        else:
            out[...] = value

    finish()


def on_device(hidden, cotangent, start_q):
    hidden = hidden.reshape(2, NY, 16, 3584)
    dma = pltpu.SemaphoreType.DMA
    vm = pltpu.VMEM
    in_hbm = pl.BlockSpec(memory_space=pltpu.HBM)
    return pl.pallas_call(
        kernel,
        out_shape=pltpu.VMEM((RANK, 1024), F32),
        in_specs=[in_hbm] * 3,
        out_specs=pl.BlockSpec(memory_space=pltpu.VMEM),
        scratch_shapes=[
            vm((2, NY, 2, 16, 3584), BF),
            vm((2, 16, 8192), BF),
            vm((2, NY, 2, 16, 1024), BF),
            vm((RANK, 1024), F32),
            vm((HALF, 1024), BF),
            vm((NY - 1, HALF, 1024), BF),
            vm((NY, HALF, LANES), BF),
            vm((2, NY, HALF, 256), BF),
            vm((2, TILES, HALF, LANES), BF),
            vm((2, CHIPS, HALF, LANES), BF),
            vm((2, 2, TILES, HALF, LANES), BF),
            vm((2, 2, NY, HALF, 256), BF),
            vm((HALF, 3584), F32),
            vm((NY, 8, LANES), F32),
            vm((NY, 16, LANES), F32),
            vm((NY, 8, LANES), F32),
            vm((2, QBLOCKS, HALF, LANES), BF),
            vm((2, CHIPS, HALF, LANES), BF),
            vm((4 * QBLOCKS, HALF, LANES), F32),
            vm((2, RANK, RANK), F32),
            vm((RANK, RANK), F32),
            dma((6,)),
            dma((3,)), dma((3,)),
            dma, dma((NY - 1,)),
            dma((3,)), dma((3,)),
            dma((2,)), dma((2,)),
            dma((2,)), dma((2,)),
            dma((2,)), dma((2,)),
            dma((2,)), dma((2, NZ - 1)),
            dma((2,)), dma((2,)),
            dma((2, 2)), dma((2, 2)),
            dma((2,)), dma((2,)),
            dma, dma,
            dma((2,)), dma((2,)),
            dma((2,)), dma((2,)),
        ],
        compiler_params=pltpu.CompilerParams(
            collective_id=0, has_side_effects=True, vmem_limit_bytes=56 * 1024 * 1024
        ),
        name="powersgd",
    )(hidden, cotangent, start_q)


def solution(mesh):
    return jax.shard_map(
        on_device,
        mesh=mesh,
        in_specs=(P(None, "dp", "mp"), P(None, ("dp", "mp"), None), P(None, "mp")),
        out_specs=P(None, "mp"),
        check_vma=False,
    )
```

```python
import functools

import jax
import jax.numpy as jnp
from jax import lax
from jax.experimental import pallas as pl
from jax.experimental.pallas import tpu as pltpu
from jax.sharding import PartitionSpec as P

MESH = pl.DeviceIdType.MESH
BF = jnp.bfloat16
F32 = jnp.float32
NY = 8
NZ = 8
NX = 4
CHIPS = NZ * NX
TILES = 28
QBLOCKS = 8
HALF = 16
RANK = 32
LANES = 128
GROUP = NX * LANES
Y_ORDER = (4, 3, 5, 2, 6, 1, 7)


def _hops(dz, dx):
    return min(dz, NZ - dz) + min(dx, NX - dx)


ZX_ORDER = sorted(
    [(dz, dx) for dz in range(NZ) for dx in range(NX) if (dz, dx) != (0, 0)],
    key=lambda d: (-_hops(*d), d),
)
NEAR = ((2, 0), (1, 1), (7, 1), (1, 0), (7, 0), (0, 1), (0, 3), (0, 0))
PLANES_IN = (0, 1, 6, 2, 5, 3, 4)
PLANES_OUT = (4, 3, 5, 2, 6, 1, 0)


def nt_dot(a, b):
    return lax.dot_general(a, b, (((1,), (1,)), ((), ())), preferred_element_type=F32)


def dot(a, b):
    return jnp.dot(a, b, preferred_element_type=F32)


def exact_dot(a, b):
    return jnp.dot(a, b, preferred_element_type=F32, precision=lax.Precision.HIGHEST)


def wait_bytes(ref, sem):
    pltpu.make_async_copy(ref, ref, sem).wait()


def exact_nt_dot(a, b):
    return lax.dot_general(
        a, b, (((1,), (1,)), ((), ())), preferred_element_type=F32, precision=lax.Precision.HIGHEST
    )


def pack(value, rows):
    width = LANES * rows // RANK
    lanes = lax.broadcasted_iota(jnp.int32, (rows, LANES), 1)
    packed = value[:rows]
    for k in range(1, RANK // rows):
        packed = jnp.where(lanes >= k * width, value[k * rows : (k + 1) * rows], packed)
    return packed


def unpack(packed):
    rows = packed.shape[0]
    width = LANES * rows // RANK
    return jnp.concatenate(
        [packed] + [pltpu.roll(packed, LANES - k * width, 1) for k in range(1, RANK // rows)], axis=0
    )


def sum_slots(ref, count):
    terms = [ref[n].astype(F32) for n in range(count)]
    while len(terms) > 1:
        terms = [a + b for a, b in zip(terms[::2], terms[1::2])]
    return terms[0]


def inverse_lower(gram):
    rows = lax.broadcasted_iota(jnp.int32, (RANK, LANES), 0)
    lanes = lax.broadcasted_iota(jnp.int32, (RANK, LANES), 1)
    work = jnp.where(lanes < RANK, gram, jnp.where(lanes == rows + RANK, 1.0, 0.0))
    row_ids = lax.broadcasted_iota(jnp.int32, (RANK, 1), 0)
    scale = jnp.zeros((RANK, 1), F32)
    for j in range(RANK):
        row = work[j : j + 1, :]
        pivot = work[j : j + 1, j : j + 1]
        scale = jnp.where(row_ids == j, pivot, scale)
        if j < RANK - 1:
            factor = jnp.where(row_ids > j, work[:, j : j + 1] / pivot, 0.0)
            work = work - factor * row
    return (work * lax.rsqrt(scale))[:, RANK : 2 * RANK]


def kernel(
    hid, cot, startq, out,
    hbuf, cbuf, tbuf, qf, qsrc, qgat, sk0, sk1, ptsrc, ptrs, pt, mx, part0, gram0, gram1, wbuf,
    zsrc, zrs, zall, minv, umat,
    s_local, s_core, r_core, s_q, r_q, s_sk, r_sk, s_t, r_t, s_tc, r_tc, s_prs, r_prs, s_pag, r_pag,
    s_ptc, r_ptc, s_mx, r_mx, s_g, r_g, s_w, r_w, s_zrs, r_zrs, s_qag, r_qag,
):
    dp = lax.axis_index("dp")
    y = lax.axis_index("mp")
    c = lax.rem(dp, 2)
    chip = lax.div(dp, 2)
    z = lax.div(chip, NX)
    x = lax.rem(chip, NX)
    sib = {"dp": dp + 1 - 2 * c, "mp": y}
    pt_owner = z < NZ - 1
    q_mine = 4 * lax.rem(x, 2) + lax.rem(z + 2 * lax.div(x, 2), 4)
    ending = []

    def y_dev(k):
        return {"dp": dp, "mp": lax.rem(y + k, NY)}

    def zx_chip(dz, dx):
        return lax.rem(z + dz, NZ) * NX + lax.rem(x + dx, NX)

    def zx_dev(there, core=None):
        return {"dp": there * 2 + (c if core is None else core), "mp": y}

    def send(src, dst, ssem, rsem, dev):
        pltpu.make_async_remote_copy(
            src_ref=src, dst_ref=dst, send_sem=ssem, recv_sem=rsem, device_id=dev, device_id_type=MESH
        ).start()

    def sent(ref, sem, when=None):
        def wait():
            wait_bytes(ref, sem)

        ending.append(wait if when is None else lambda: pl.when(when)(wait))

    def finish():
        while ending:
            ending.pop(0)()

    load_q = pltpu.make_async_copy(startq, qf, s_local.at[0])
    load_q.start()
    bar = pltpu.get_barrier_semaphore()
    greeted = [(_hops(*d), zx_dev(zx_chip(*d))) for d in ZX_ORDER]
    greeted += [(min(k, NY - k), y_dev(k)) for k in Y_ORDER]
    greeted += [(_hops(*d), zx_dev(zx_chip(NZ - d[0], NX - d[1]), 1 - c)) for d in NEAR[:-1]]
    greeted += [(0, sib)]
    for _, there in sorted(greeted, key=lambda e: -e[0]):
        pl.semaphore_signal(bar, inc=1, device_id=there, device_id_type=MESH)
    load_c = pltpu.make_async_copy(cot.at[0], cbuf.at[c], s_local.at[1])
    load_c.start()
    load_h = [pltpu.make_async_copy(hid.at[j], hbuf.at[j, :, c], s_local.at[2 + j]) for j in range(2)]
    load_h[0].start()
    load_h[1].start()
    load_q.wait()
    qsrc[...] = qf[pl.ds(pl.multiple_of(c * HALF, HALF), HALF), :].astype(BF)
    pl.semaphore_wait(bar, NY - 1 + CHIPS - 1 + len(NEAR))

    for n, k in enumerate(Y_ORDER):
        send(qsrc, qgat.at[n], s_q, r_q.at[n], y_dev(k))
    sent(qgat, s_q)
    send(cot.at[0], cbuf.at[c], s_core.at[0], r_core.at[0], sib)
    sent(cbuf.at[0], s_core.at[0])
    load_c.wait()
    wait_bytes(cbuf.at[0], r_core.at[0])

    def block_sketch(q_rows, owner):
        cols = pl.ds(pl.multiple_of(owner * 1024, 1024), 1024)
        return nt_dot(q_rows, cbuf[:, :, cols].reshape(RANK, 1024))

    sketch = block_sketch(qsrc[...], y)
    for n, k in sorted(enumerate(Y_ORDER), key=lambda e: min(e[1], NY - e[1])):
        wait_bytes(qgat.at[n], r_q.at[n])
        sketch = sketch + block_sketch(qgat[n], lax.rem(y - k + NY, NY))
    spot = lax.broadcasted_iota(jnp.int32, (RANK, LANES), 0) + RANK * lax.rem(y, 4)
    place = jnp.where(lax.broadcasted_iota(jnp.int32, (RANK, LANES), 1) == spot, 1.0, 0.0).astype(BF)
    sk0[y] = dot(sketch.astype(BF), place).astype(BF)
    for k in Y_ORDER:
        send(sk0.at[y], sk0.at[y], s_sk.at[0], r_sk.at[0], y_dev(k))
    sent(sk0.at[pl.ds(0, NY - 1)], s_sk.at[0])

    def share_h(j):
        send(hid.at[j], hbuf.at[j, :, c], s_core.at[1 + j], r_core.at[1 + j], sib)
        sent(hbuf.at[j, :, 0], s_core.at[1 + j])

    share_h(0)
    wait_bytes(sk0.at[pl.ds(0, NY - 1)], r_sk.at[0])

    own_cols = pl.ds(pl.multiple_of(y * 1024, 1024), 1024)
    load_t = [pltpu.make_async_copy(cot.at[j, :, own_cols], tbuf.at[j, y, c], s_local.at[4 + j]) for j in range(2)]

    def spread_t(j):
        for k in Y_ORDER:
            there = lax.rem(y + k, NY)
            cols = pl.ds(pl.multiple_of(there * 1024, 1024), 1024)
            send(cot.at[j, :, cols], tbuf.at[j, y, c], s_t.at[j], r_t.at[j], y_dev(k))
        sent(tbuf.at[j, pl.ds(0, NY - 1), 0], s_t.at[j])
        load_t[j].start()

    def share_t(j):
        load_t[j].wait()
        wait_bytes(tbuf.at[j, pl.ds(0, NY - 1), 0], r_t.at[j])
        send(tbuf.at[j, :, c], tbuf.at[j, :, c], s_tc.at[j], r_tc.at[j], sib)
        sent(tbuf.at[j, :, 0], s_tc.at[j])

    left = jnp.concatenate(
        [
            (sk0[0] + sk0[1]) + (sk0[2] + sk0[3]),
            (sk0[4] + sk0[5]) + (sk0[6] + sk0[7]),
        ],
        axis=1,
    )

    for s in range(2):
        used = s + 1
        if s == 0:
            load_h[0].wait()
            wait_bytes(hbuf.at[0, :, 0], r_core.at[1])
        if s == 1:
            wait_bytes(sk1.at[0, pl.ds(0, NY - 1)], r_sk.at[1])
            part0[...] = dot(sum_slots(sk1.at[0], NY).astype(BF), hbuf[0].reshape(256, 3584))
            load_h[1].wait()
            wait_bytes(hbuf.at[1, :, 0], r_core.at[2])
            wait_bytes(sk1.at[1, pl.ds(0, NY - 1)], r_sk.at[2])
            left = sum_slots(sk1.at[1], NY).astype(BF)
        for step in PLANES_OUT:
            n = lax.rem(z + step, NZ - 1)
            cols = pl.ds(pl.multiple_of(n * GROUP, GROUP), GROUP)
            part = dot(left, hbuf[s, :, :, :, cols].reshape(256, GROUP))
            if s == 1:
                part = part + part0[:, cols]
            part = part.astype(BF)
            for g in range(NX):
                ptsrc[s, n * NX + g] = part[:, g * LANES : (g + 1) * LANES]
            for dx in (2, 1, 3, 0):
                there = n * NX + lax.rem(x + dx, NX)

                def post(there=there):
                    send(ptsrc.at[s, there], ptrs.at[s, chip], s_prs.at[s], r_prs.at[s], zx_dev(there))

                if step == 0 and dx == 0:
                    pl.when(jnp.logical_not(pt_owner))(post)
                else:
                    post()
        if s == 0:
            share_h(1)
            spread_t(0)

        sent(ptrs.at[s, pl.ds(0, TILES - 1)], s_prs.at[s], pt_owner)
        sent(ptrs.at[s, pl.ds(0, TILES)], s_prs.at[s], jnp.logical_not(pt_owner))

        if s == 1:
            wait_bytes(wbuf.at[pl.ds(0, NY - 1)], r_w)
            weights = unpack(sum_slots(wbuf, NY))
            umat[...] = exact_dot(weights[:, :RANK], minv[0])
            qf[...] = lax.dot_general(
                minv[0], qf[...], (((0,), (0,)), ((), ())), preferred_element_type=F32, precision=lax.Precision.HIGHEST
            )

        @pl.when(pt_owner)
        def _():
            correction = 0.0
            if s == 1:
                past = jnp.concatenate([pt[0, 0, chip], pt[0, 1, chip]], axis=0).astype(F32)
                own_rows = umat[pl.ds(pl.multiple_of(c * HALF, HALF), HALF), :]
                correction = exact_dot(own_rows, past)
            ptrs[s, chip] = ptsrc[s, chip]
            wait_bytes(ptrs.at[s, pl.ds(0, CHIPS - 1)], r_prs.at[s])
            total = sum_slots(ptrs.at[s], CHIPS) * (1.0 / 64.0) - correction
            pt[s, c, chip] = total.astype(BF)
            tile = pt.at[s, c, chip]
            for d in ZX_ORDER:
                send(tile, tile, s_pag.at[s], r_pag.at[s, z], zx_dev(zx_chip(*d)))

        sent(ptrs.at[s, pl.ds(0, CHIPS - 1)], s_pag.at[s], pt_owner)

        mixed = [None] * used
        for step in PLANES_IN:
            n = lax.rem(z + step, NZ - 1)
            first = pl.multiple_of(n * NX, NX)
            if step == 0:

                @pl.when(pt_owner)
                def _():
                    wait_bytes(pt.at[s, c, pl.ds(0, NX - 1)], r_pag.at[s, z])

                @pl.when(jnp.logical_not(pt_owner))
                def _():
                    wait_bytes(pt.at[s, c, pl.ds(0, NX)], r_pag.at[s, n])

            else:
                wait_bytes(pt.at[s, c, pl.ds(0, NX)], r_pag.at[s, n])
            cols = pl.ds(pl.multiple_of(n * GROUP, GROUP), GROUP)
            rows = jnp.concatenate([pt[s, c, first + g] for g in range(NX)], axis=1)
            for j in range(used):
                term = nt_dot(rows, hbuf[j, :, :, :, cols].reshape(256, GROUP))
                mixed[j] = term if mixed[j] is None else mixed[j] + term
        send(pt.at[s, c], pt.at[s, c], s_ptc.at[s], r_ptc.at[s], sib)
        sent(pt.at[s, 0], s_ptc.at[s])
        for j in range(used):
            mx[s, j, y] = mixed[j].astype(BF)
            for k in Y_ORDER:
                send(mx.at[s, j, y], mx.at[s, j, y], s_mx.at[s, j], r_mx.at[s, j], y_dev(k))
            sent(mx.at[s, j, pl.ds(0, NY - 1)], s_mx.at[s, j])

        if s == 0:
            share_t(0)

        wait_bytes(pt.at[s, 0], r_ptc.at[s])

        def both(step):
            return jnp.concatenate(
                [
                    jnp.concatenate([pt[step, e, n] for n in range(TILES)], axis=1)
                    for e in range(2)
                ],
                axis=0,
            )

        now = both(s)
        other = now if s == 0 else both(0)
        gram = gram0 if s == 0 else gram1
        gram[y] = pack(nt_dot(now, jnp.concatenate([now, other, now, other], axis=0)), gram.shape[1])
        for k in Y_ORDER:
            send(gram.at[y], gram.at[y], s_g.at[s], r_g.at[s], y_dev(k))
        sent(gram.at[pl.ds(0, NY - 1)], s_g.at[s])
        if s == 0:
            spread_t(1)

        if s == 0:
            wait_bytes(tbuf.at[0, :, 0], r_tc.at[0])
        part = None
        for j in range(used):
            wait_bytes(mx.at[s, j, pl.ds(0, NY - 1)], r_mx.at[s, j])
            term = dot(sum_slots(mx.at[s, j], NY).astype(BF), tbuf[j].reshape(256, 1024))
            part = term if part is None else part + term
        part = part.astype(BF)
        for b in range(QBLOCKS):
            zsrc[s, b] = part[:, b * LANES : (b + 1) * LANES]
        for dz, dx in ZX_ORDER:
            there = zx_chip(dz, dx)
            b = 4 * lax.rem(x + dx, 2) + lax.rem(z + dz + 2 * lax.div(lax.rem(x + dx, NX), 2), 4)
            send(zsrc.at[s, b], zrs.at[s, chip], s_zrs.at[s], r_zrs.at[s], zx_dev(there))
        sent(zrs.at[s, pl.ds(0, CHIPS - 1)], s_zrs.at[s])

        if s == 0:
            share_t(1)
        else:
            finish()


        z_mine = (2 * s + c) * QBLOCKS + q_mine

        zrs[s, chip] = zsrc[s, q_mine]
        wait_bytes(zrs.at[s, pl.ds(0, CHIPS - 1)], r_zrs.at[s])
        zall[z_mine] = sum_slots(zrs.at[s], CHIPS) * (1.0 / 64.0)
        tile = zall.at[z_mine]
        for d in NEAR:
            for core in (c, 1 - c) if d != (0, 0) else (1 - c,):
                send(tile, tile, s_qag.at[s], r_qag.at[s], zx_dev(zx_chip(*d), core))
        sent(zall.at[pl.ds(0, 15)], s_qag.at[s])

        wait_bytes(gram.at[pl.ds(0, NY - 1)], r_g.at[s])
        inner = unpack(sum_slots(gram, NY))
        if s == 1:
            shift = exact_dot(inner[:, RANK : 2 * RANK], qf[...])
        minv[s] = inverse_lower(inner)
        wait_bytes(zall.at[pl.ds(0, 15)], r_qag.at[s])
        value = jnp.concatenate(
            [
                jnp.concatenate([zall[(2 * s + e) * QBLOCKS + b] for b in range(QBLOCKS)], axis=1)
                for e in range(2)
            ],
            axis=0,
        )
        if s == 1:
            value = value - shift
        value = exact_dot(minv[s], value)
        if s == 0:
            qf[...] = value
            rows = qf[pl.ds(pl.multiple_of(c * HALF, HALF), HALF), :].astype(BF)
            wait_bytes(tbuf.at[1, :, 0], r_tc.at[1])
            for j in range(2):
                sk1[j, y] = nt_dot(rows, tbuf[j].reshape(256, 1024)).astype(BF)
                for k in Y_ORDER:
                    send(sk1.at[j, y], sk1.at[j, y], s_sk.at[1 + j], r_sk.at[1 + j], y_dev(k))
                sent(sk1.at[j, pl.ds(0, NY - 1)], s_sk.at[1 + j])
            wbuf[y] = pack(exact_nt_dot(value, jnp.concatenate([value] * 4, axis=0)), 8)
            for k in Y_ORDER:
                send(wbuf.at[y], wbuf.at[y], s_w, r_w, y_dev(k))
            sent(wbuf.at[pl.ds(0, NY - 1)], s_w)
        else:
            out[...] = value

    finish()


def on_device(hidden, cotangent, start_q):
    hidden = hidden.reshape(2, NY, 16, 3584)
    dma = pltpu.SemaphoreType.DMA
    vm = pltpu.VMEM
    in_hbm = pl.BlockSpec(memory_space=pltpu.HBM)
    return pl.pallas_call(
        kernel,
        out_shape=pltpu.VMEM((RANK, 1024), F32),
        in_specs=[in_hbm] * 3,
        out_specs=pl.BlockSpec(memory_space=pltpu.VMEM),
        scratch_shapes=[
            vm((2, NY, 2, 16, 3584), BF),
            vm((2, 16, 8192), BF),
            vm((2, NY, 2, 16, 1024), BF),
            vm((RANK, 1024), F32),
            vm((HALF, 1024), BF),
            vm((NY - 1, HALF, 1024), BF),
            vm((NY, HALF, LANES), BF),
            vm((2, NY, HALF, 256), BF),
            vm((2, TILES, HALF, LANES), BF),
            vm((2, CHIPS, HALF, LANES), BF),
            vm((2, 2, TILES, HALF, LANES), BF),
            vm((2, 2, NY, HALF, 256), BF),
            vm((HALF, 3584), F32),
            vm((NY, 8, LANES), F32),
            vm((NY, 16, LANES), F32),
            vm((NY, 8, LANES), F32),
            vm((2, QBLOCKS, HALF, LANES), BF),
            vm((2, CHIPS, HALF, LANES), BF),
            vm((4 * QBLOCKS, HALF, LANES), F32),
            vm((2, RANK, RANK), F32),
            vm((RANK, RANK), F32),
            dma((6,)),
            dma((3,)), dma((3,)),
            dma, dma((NY - 1,)),
            dma((3,)), dma((3,)),
            dma((2,)), dma((2,)),
            dma((2,)), dma((2,)),
            dma((2,)), dma((2,)),
            dma((2,)), dma((2, NZ - 1)),
            dma((2,)), dma((2,)),
            dma((2, 2)), dma((2, 2)),
            dma((2,)), dma((2,)),
            dma, dma,
            dma((2,)), dma((2,)),
            dma((2,)), dma((2,)),
        ],
        compiler_params=pltpu.CompilerParams(
            collective_id=0, has_side_effects=True, vmem_limit_bytes=56 * 1024 * 1024
        ),
        name="powersgd",
    )(hidden, cotangent, start_q)


def solution(mesh):
    return jax.shard_map(
        on_device,
        mesh=mesh,
        in_specs=(P(None, "dp", "mp"), P(None, ("dp", "mp"), None), P(None, "mp")),
        out_specs=P(None, "mp"),
        check_vma=False,
    )
```

```python
import functools

import jax
import jax.numpy as jnp
from jax import lax
from jax.experimental import pallas as pl
from jax.experimental.pallas import tpu as pltpu
from jax.sharding import PartitionSpec as P

MESH = pl.DeviceIdType.MESH
BF = jnp.bfloat16
F32 = jnp.float32
NY = 8
NZ = 8
NX = 4
CHIPS = NZ * NX
TILES = 28
QBLOCKS = 8
HALF = 16
RANK = 32
LANES = 128
GROUP = NX * LANES
Y_ORDER = (4, 3, 5, 2, 6, 1, 7)


def _hops(dz, dx):
    return min(dz, NZ - dz) + min(dx, NX - dx)


ZX_ORDER = sorted(
    [(dz, dx) for dz in range(NZ) for dx in range(NX) if (dz, dx) != (0, 0)],
    key=lambda d: (-_hops(*d), d),
)
NEAR = ((2, 0), (1, 1), (7, 1), (1, 0), (7, 0), (0, 1), (0, 3), (0, 0))
PLANES_IN = (0, 1, 6, 2, 5, 3, 4)
PLANES_OUT = (4, 3, 5, 2, 6, 1, 0)


def nt_dot(a, b):
    return lax.dot_general(a, b, (((1,), (1,)), ((), ())), preferred_element_type=F32)


def dot(a, b):
    return jnp.dot(a, b, preferred_element_type=F32)


def exact_dot(a, b):
    return jnp.dot(a, b, preferred_element_type=F32, precision=lax.Precision.HIGHEST)


def wait_bytes(ref, sem):
    pltpu.make_async_copy(ref, ref, sem).wait()


def exact_nt_dot(a, b):
    return lax.dot_general(
        a, b, (((1,), (1,)), ((), ())), preferred_element_type=F32, precision=lax.Precision.HIGHEST
    )


def pack(value, rows):
    width = LANES * rows // RANK
    lanes = lax.broadcasted_iota(jnp.int32, (rows, LANES), 1)
    packed = value[:rows]
    for k in range(1, RANK // rows):
        packed = jnp.where(lanes >= k * width, value[k * rows : (k + 1) * rows], packed)
    return packed


def unpack(packed):
    rows = packed.shape[0]
    width = LANES * rows // RANK
    return jnp.concatenate(
        [packed] + [pltpu.roll(packed, LANES - k * width, 1) for k in range(1, RANK // rows)], axis=0
    )


def sum_slots(ref, count):
    terms = [ref[n].astype(F32) for n in range(count)]
    while len(terms) > 1:
        terms = [a + b for a, b in zip(terms[::2], terms[1::2])]
    return terms[0]


def inverse_lower(gram):
    rows = lax.broadcasted_iota(jnp.int32, (RANK, LANES), 0)
    lanes = lax.broadcasted_iota(jnp.int32, (RANK, LANES), 1)
    work = jnp.where(lanes < RANK, gram, jnp.where(lanes == rows + RANK, 1.0, 0.0))
    row_ids = lax.broadcasted_iota(jnp.int32, (RANK, 1), 0)
    scale = jnp.zeros((RANK, 1), F32)
    for j in range(RANK):
        row = work[j : j + 1, :]
        pivot = work[j : j + 1, j : j + 1]
        scale = jnp.where(row_ids == j, pivot, scale)
        if j < RANK - 1:
            factor = jnp.where(row_ids > j, work[:, j : j + 1] / pivot, 0.0)
            work = work - factor * row
    return (work * lax.rsqrt(scale))[:, RANK : 2 * RANK]


def kernel(
    hid, cot, startq, out,
    hbuf, cbuf, tbuf, qf, qsrc, qgat, sk0, sk1, ptsrc, ptrs, pt, mx, part0, gram0, gram1, wbuf,
    zsrc, zrs, zall, mparts, shifted, minv, umat,
    s_local, s_core, r_core, s_q, r_q, s_sk, r_sk, s_t, r_t, s_tc, r_tc, s_prs, r_prs, s_pag, r_pag,
    s_ptc, r_ptc, s_mx, r_mx, s_g, r_g, s_w, r_w, s_zrs, r_zrs, s_qag, r_qag,
):
    dp = lax.axis_index("dp")
    y = lax.axis_index("mp")
    c = lax.rem(dp, 2)
    chip = lax.div(dp, 2)
    z = lax.div(chip, NX)
    x = lax.rem(chip, NX)
    sib = {"dp": dp + 1 - 2 * c, "mp": y}
    pt_owner = z < NZ - 1
    q_mine = 4 * lax.rem(x, 2) + lax.rem(z + 2 * lax.div(x, 2), 4)
    ending = []

    def y_dev(k):
        return {"dp": dp, "mp": lax.rem(y + k, NY)}

    def zx_chip(dz, dx):
        return lax.rem(z + dz, NZ) * NX + lax.rem(x + dx, NX)

    def zx_dev(there, core=None):
        return {"dp": there * 2 + (c if core is None else core), "mp": y}

    def send(src, dst, ssem, rsem, dev):
        pltpu.make_async_remote_copy(
            src_ref=src, dst_ref=dst, send_sem=ssem, recv_sem=rsem, device_id=dev, device_id_type=MESH
        ).start()

    def sent(ref, sem, when=None):
        def wait():
            wait_bytes(ref, sem)

        ending.append(wait if when is None else lambda: pl.when(when)(wait))

    def finish():
        while ending:
            ending.pop(0)()

    load_q = pltpu.make_async_copy(startq, qf, s_local.at[0])
    load_q.start()
    bar = pltpu.get_barrier_semaphore()
    greeted = [(_hops(*d), zx_dev(zx_chip(*d))) for d in ZX_ORDER]
    greeted += [(min(k, NY - k), y_dev(k)) for k in Y_ORDER]
    greeted += [(_hops(*d), zx_dev(zx_chip(NZ - d[0], NX - d[1]), 1 - c)) for d in NEAR[:-1]]
    greeted += [(0, sib)]
    for _, there in sorted(greeted, key=lambda e: -e[0]):
        pl.semaphore_signal(bar, inc=1, device_id=there, device_id_type=MESH)
    load_c = pltpu.make_async_copy(cot.at[0], cbuf.at[c], s_local.at[1])
    load_c.start()
    load_h = [pltpu.make_async_copy(hid.at[j], hbuf.at[j, :, c], s_local.at[2 + j]) for j in range(2)]
    load_h[0].start()
    load_h[1].start()
    load_q.wait()
    qsrc[...] = qf[pl.ds(pl.multiple_of(c * HALF, HALF), HALF), :].astype(BF)
    pl.semaphore_wait(bar, NY - 1 + CHIPS - 1 + len(NEAR))

    for n, k in enumerate(Y_ORDER):
        send(qsrc, qgat.at[n], s_q, r_q.at[n], y_dev(k))
    sent(qgat, s_q)
    send(cot.at[0], cbuf.at[c], s_core.at[0], r_core.at[0], sib)
    sent(cbuf.at[0], s_core.at[0])
    load_c.wait()
    wait_bytes(cbuf.at[0], r_core.at[0])

    def block_sketch(q_rows, owner):
        cols = pl.ds(pl.multiple_of(owner * 1024, 1024), 1024)
        return nt_dot(q_rows, cbuf[:, :, cols].reshape(RANK, 1024))

    sketch = block_sketch(qsrc[...], y)
    for n, k in sorted(enumerate(Y_ORDER), key=lambda e: min(e[1], NY - e[1])):
        wait_bytes(qgat.at[n], r_q.at[n])
        sketch = sketch + block_sketch(qgat[n], lax.rem(y - k + NY, NY))
    spot = lax.broadcasted_iota(jnp.int32, (RANK, LANES), 0) + RANK * lax.rem(y, 4)
    place = jnp.where(lax.broadcasted_iota(jnp.int32, (RANK, LANES), 1) == spot, 1.0, 0.0).astype(BF)
    sk0[y] = dot(sketch.astype(BF), place).astype(BF)
    for k in Y_ORDER:
        send(sk0.at[y], sk0.at[y], s_sk.at[0], r_sk.at[0], y_dev(k))
    sent(sk0.at[pl.ds(0, NY - 1)], s_sk.at[0])

    def share_h(j):
        send(hid.at[j], hbuf.at[j, :, c], s_core.at[1 + j], r_core.at[1 + j], sib)
        sent(hbuf.at[j, :, 0], s_core.at[1 + j])

    share_h(0)
    wait_bytes(sk0.at[pl.ds(0, NY - 1)], r_sk.at[0])

    own_cols = pl.ds(pl.multiple_of(y * 1024, 1024), 1024)
    load_t = [pltpu.make_async_copy(cot.at[j, :, own_cols], tbuf.at[j, y, c], s_local.at[4 + j]) for j in range(2)]

    def spread_t(j):
        for k in Y_ORDER:
            there = lax.rem(y + k, NY)
            cols = pl.ds(pl.multiple_of(there * 1024, 1024), 1024)
            send(cot.at[j, :, cols], tbuf.at[j, y, c], s_t.at[j], r_t.at[j], y_dev(k))
        sent(tbuf.at[j, pl.ds(0, NY - 1), 0], s_t.at[j])
        load_t[j].start()

    def share_t(j):
        load_t[j].wait()
        wait_bytes(tbuf.at[j, pl.ds(0, NY - 1), 0], r_t.at[j])
        send(tbuf.at[j, :, c], tbuf.at[j, :, c], s_tc.at[j], r_tc.at[j], sib)
        sent(tbuf.at[j, :, 0], s_tc.at[j])

    left = jnp.concatenate(
        [
            (sk0[0] + sk0[1]) + (sk0[2] + sk0[3]),
            (sk0[4] + sk0[5]) + (sk0[6] + sk0[7]),
        ],
        axis=1,
    )

    for s in range(2):
        used = s + 1
        if s == 0:
            load_h[0].wait()
            wait_bytes(hbuf.at[0, :, 0], r_core.at[1])
        if s == 1:
            wait_bytes(sk1.at[0, pl.ds(0, NY - 1)], r_sk.at[1])
            part0[...] = dot(sum_slots(sk1.at[0], NY).astype(BF), hbuf[0].reshape(256, 3584))
            load_h[1].wait()
            wait_bytes(hbuf.at[1, :, 0], r_core.at[2])
            wait_bytes(sk1.at[1, pl.ds(0, NY - 1)], r_sk.at[2])
            left = sum_slots(sk1.at[1], NY).astype(BF)
        for step in PLANES_OUT:
            n = lax.rem(z + step, NZ - 1)
            cols = pl.ds(pl.multiple_of(n * GROUP, GROUP), GROUP)
            part = dot(left, hbuf[s, :, :, :, cols].reshape(256, GROUP))
            if s == 1:
                part = part + part0[:, cols]
            part = part.astype(BF)
            for g in range(NX):
                ptsrc[s, n * NX + g] = part[:, g * LANES : (g + 1) * LANES]
            for dx in (2, 1, 3, 0):
                there = n * NX + lax.rem(x + dx, NX)

                def post(there=there):
                    send(ptsrc.at[s, there], ptrs.at[s, chip], s_prs.at[s], r_prs.at[s], zx_dev(there))

                if step == 0 and dx == 0:
                    pl.when(jnp.logical_not(pt_owner))(post)
                else:
                    post()
        if s == 0:
            share_h(1)
            spread_t(0)

        sent(ptrs.at[s, pl.ds(0, TILES - 1)], s_prs.at[s], pt_owner)
        sent(ptrs.at[s, pl.ds(0, TILES)], s_prs.at[s], jnp.logical_not(pt_owner))

        if s == 1:
            wait_bytes(wbuf.at[pl.ds(0, NY - 1)], r_w)
            weights = unpack(sum_slots(wbuf, NY))
            umat[...] = exact_dot(weights[:, :RANK], minv[0])
            qf[...] = lax.dot_general(
                minv[0], qf[...], (((0,), (0,)), ((), ())), preferred_element_type=F32, precision=lax.Precision.HIGHEST
            )

        @pl.when(pt_owner)
        def _():
            correction = 0.0
            if s == 1:
                past = jnp.concatenate([pt[0, 0, chip], pt[0, 1, chip]], axis=0).astype(F32)
                own_rows = umat[pl.ds(pl.multiple_of(c * HALF, HALF), HALF), :]
                correction = exact_dot(own_rows, past)
            ptrs[s, chip] = ptsrc[s, chip]
            wait_bytes(ptrs.at[s, pl.ds(0, CHIPS - 1)], r_prs.at[s])
            total = sum_slots(ptrs.at[s], CHIPS) * (1.0 / 64.0) - correction
            pt[s, c, chip] = total.astype(BF)
            tile = pt.at[s, c, chip]
            for d in ZX_ORDER:
                send(tile, tile, s_pag.at[s], r_pag.at[s, z], zx_dev(zx_chip(*d)))

        sent(ptrs.at[s, pl.ds(0, CHIPS - 1)], s_pag.at[s], pt_owner)

        mixed = [None] * used
        for step in PLANES_IN:
            n = lax.rem(z + step, NZ - 1)
            first = pl.multiple_of(n * NX, NX)
            if step == 0:

                @pl.when(pt_owner)
                def _():
                    wait_bytes(pt.at[s, c, pl.ds(0, NX - 1)], r_pag.at[s, z])

                @pl.when(jnp.logical_not(pt_owner))
                def _():
                    wait_bytes(pt.at[s, c, pl.ds(0, NX)], r_pag.at[s, n])

            else:
                wait_bytes(pt.at[s, c, pl.ds(0, NX)], r_pag.at[s, n])
            cols = pl.ds(pl.multiple_of(n * GROUP, GROUP), GROUP)
            rows = jnp.concatenate([pt[s, c, first + g] for g in range(NX)], axis=1)
            for j in range(used):
                term = nt_dot(rows, hbuf[j, :, :, :, cols].reshape(256, GROUP))
                mixed[j] = term if mixed[j] is None else mixed[j] + term
        send(pt.at[s, c], pt.at[s, c], s_ptc.at[s], r_ptc.at[s], sib)
        sent(pt.at[s, 0], s_ptc.at[s])
        for j in range(used):
            mx[s, j, y] = mixed[j].astype(BF)
            for k in Y_ORDER:
                send(mx.at[s, j, y], mx.at[s, j, y], s_mx.at[s, j], r_mx.at[s, j], y_dev(k))
            sent(mx.at[s, j, pl.ds(0, NY - 1)], s_mx.at[s, j])

        if s == 0:
            share_t(0)

        wait_bytes(pt.at[s, 0], r_ptc.at[s])

        def both(step):
            return jnp.concatenate(
                [
                    jnp.concatenate([pt[step, e, n] for n in range(TILES)], axis=1)
                    for e in range(2)
                ],
                axis=0,
            )

        now = both(s)
        other = now if s == 0 else both(0)
        gram = gram0 if s == 0 else gram1
        gram[y] = pack(nt_dot(now, jnp.concatenate([now, other, now, other], axis=0)), gram.shape[1])
        for k in Y_ORDER:
            send(gram.at[y], gram.at[y], s_g.at[s], r_g.at[s], y_dev(k))
        sent(gram.at[pl.ds(0, NY - 1)], s_g.at[s])
        if s == 0:
            spread_t(1)

        if s == 0:
            wait_bytes(tbuf.at[0, :, 0], r_tc.at[0])
        part = None
        for j in range(used):
            wait_bytes(mx.at[s, j, pl.ds(0, NY - 1)], r_mx.at[s, j])
            term = dot(sum_slots(mx.at[s, j], NY).astype(BF), tbuf[j].reshape(256, 1024))
            part = term if part is None else part + term
        part = part.astype(BF)
        for b in range(QBLOCKS):
            zsrc[s, b] = part[:, b * LANES : (b + 1) * LANES]
        for dz, dx in ZX_ORDER:
            there = zx_chip(dz, dx)
            b = 4 * lax.rem(x + dx, 2) + lax.rem(z + dz + 2 * lax.div(lax.rem(x + dx, NX), 2), 4)
            send(zsrc.at[s, b], zrs.at[s, chip], s_zrs.at[s], r_zrs.at[s], zx_dev(there))
        sent(zrs.at[s, pl.ds(0, CHIPS - 1)], s_zrs.at[s])

        wait_bytes(gram.at[pl.ds(0, NY - 1)], r_g.at[s])
        inner = unpack(sum_slots(gram, NY))
        minv[s] = inverse_lower(inner)
        rest = minv[s]
        for n in range(3):
            part = rest.astype(BF)
            mparts[n * RANK : (n + 1) * RANK, :] = part
            rest = rest - part.astype(F32)
        if s == 1:
            shifted[...] = exact_dot(minv[1], exact_dot(inner[:, RANK : 2 * RANK], qf[...]))


        z_mine = (2 * s + c) * QBLOCKS + q_mine

        zrs[s, chip] = zsrc[s, q_mine]
        wait_bytes(zrs.at[s, pl.ds(0, CHIPS - 1)], r_zrs.at[s])
        zall[z_mine] = (sum_slots(zrs.at[s], CHIPS) * (1.0 / 64.0)).astype(BF)
        tile = zall.at[z_mine]
        for d in NEAR:
            for core in (c, 1 - c) if d != (0, 0) else (1 - c,):
                send(tile, tile, s_qag.at[s], r_qag.at[s], zx_dev(zx_chip(*d), core))
        sent(zall.at[pl.ds(0, 15)], s_qag.at[s])

        if s == 0:
            share_t(1)
        else:
            finish()
        wait_bytes(zall.at[pl.ds(0, 15)], r_qag.at[s])
        value = jnp.concatenate(
            [
                jnp.concatenate([zall[(2 * s + e) * QBLOCKS + b] for b in range(QBLOCKS)], axis=1)
                for e in range(2)
            ],
            axis=0,
        )
        parts = dot(mparts[...], value)
        value = parts[:RANK] + (parts[RANK : 2 * RANK] + parts[2 * RANK :])
        if s == 1:
            value = value - shifted[...]
        if s == 0:
            qf[...] = value
            rows = qf[pl.ds(pl.multiple_of(c * HALF, HALF), HALF), :].astype(BF)
            wait_bytes(tbuf.at[1, :, 0], r_tc.at[1])
            for j in range(2):
                sk1[j, y] = nt_dot(rows, tbuf[j].reshape(256, 1024)).astype(BF)
                for k in Y_ORDER:
                    send(sk1.at[j, y], sk1.at[j, y], s_sk.at[1 + j], r_sk.at[1 + j], y_dev(k))
                sent(sk1.at[j, pl.ds(0, NY - 1)], s_sk.at[1 + j])
            wbuf[y] = pack(exact_nt_dot(value, jnp.concatenate([value] * 4, axis=0)), 8)
            for k in Y_ORDER:
                send(wbuf.at[y], wbuf.at[y], s_w, r_w, y_dev(k))
            sent(wbuf.at[pl.ds(0, NY - 1)], s_w)
        else:
            out[...] = value

    finish()


def on_device(hidden, cotangent, start_q):
    hidden = hidden.reshape(2, NY, 16, 3584)
    dma = pltpu.SemaphoreType.DMA
    vm = pltpu.VMEM
    in_hbm = pl.BlockSpec(memory_space=pltpu.HBM)
    return pl.pallas_call(
        kernel,
        out_shape=pltpu.VMEM((RANK, 1024), F32),
        in_specs=[in_hbm] * 3,
        out_specs=pl.BlockSpec(memory_space=pltpu.VMEM),
        scratch_shapes=[
            vm((2, NY, 2, 16, 3584), BF),
            vm((2, 16, 8192), BF),
            vm((2, NY, 2, 16, 1024), BF),
            vm((RANK, 1024), F32),
            vm((HALF, 1024), BF),
            vm((NY - 1, HALF, 1024), BF),
            vm((NY, HALF, LANES), BF),
            vm((2, NY, HALF, 256), BF),
            vm((2, TILES, HALF, LANES), BF),
            vm((2, CHIPS, HALF, LANES), BF),
            vm((2, 2, TILES, HALF, LANES), BF),
            vm((2, 2, NY, HALF, 256), BF),
            vm((HALF, 3584), F32),
            vm((NY, 8, LANES), F32),
            vm((NY, 16, LANES), F32),
            vm((NY, 8, LANES), F32),
            vm((2, QBLOCKS, HALF, LANES), BF),
            vm((2, CHIPS, HALF, LANES), BF),
            vm((4 * QBLOCKS, HALF, LANES), BF),
            vm((3 * RANK, RANK), BF),
            vm((RANK, 1024), F32),
            vm((2, RANK, RANK), F32),
            vm((RANK, RANK), F32),
            dma((6,)),
            dma((3,)), dma((3,)),
            dma, dma((NY - 1,)),
            dma((3,)), dma((3,)),
            dma((2,)), dma((2,)),
            dma((2,)), dma((2,)),
            dma((2,)), dma((2,)),
            dma((2,)), dma((2, NZ - 1)),
            dma((2,)), dma((2,)),
            dma((2, 2)), dma((2, 2)),
            dma((2,)), dma((2,)),
            dma, dma,
            dma((2,)), dma((2,)),
            dma((2,)), dma((2,)),
        ],
        compiler_params=pltpu.CompilerParams(
            collective_id=0, has_side_effects=True, vmem_limit_bytes=56 * 1024 * 1024
        ),
        name="powersgd",
    )(hidden, cotangent, start_q)


def solution(mesh):
    return jax.shard_map(
        on_device,
        mesh=mesh,
        in_specs=(P(None, "dp", "mp"), P(None, ("dp", "mp"), None), P(None, "mp")),
        out_specs=P(None, "mp"),
        check_vma=False,
    )
```

```python
import functools

import jax
import jax.numpy as jnp
from jax import lax
from jax.experimental import pallas as pl
from jax.experimental.pallas import tpu as pltpu
from jax.sharding import PartitionSpec as P

MESH = pl.DeviceIdType.MESH
BF = jnp.bfloat16
F32 = jnp.float32
NY = 8
NZ = 8
NX = 4
CHIPS = NZ * NX
TILES = 28
QBLOCKS = 8
HALF = 16
RANK = 32
LANES = 128
GROUP = NX * LANES
Y_ORDER = (4, 3, 5, 2, 6, 1, 7)


def _hops(dz, dx):
    return min(dz, NZ - dz) + min(dx, NX - dx)


ZX_ORDER = sorted(
    [(dz, dx) for dz in range(NZ) for dx in range(NX) if (dz, dx) != (0, 0)],
    key=lambda d: (-_hops(*d), d),
)
NEAR = ((2, 0), (1, 1), (7, 1), (1, 0), (7, 0), (0, 1), (0, 3), (0, 0))
PLANES_IN = (0, 1, 6, 2, 5, 3, 4)
PLANES_OUT = (4, 3, 5, 2, 6, 1, 0)


def nt_dot(a, b):
    return lax.dot_general(a, b, (((1,), (1,)), ((), ())), preferred_element_type=F32)


def dot(a, b):
    return jnp.dot(a, b, preferred_element_type=F32)


def exact_dot(a, b):
    return jnp.dot(a, b, preferred_element_type=F32, precision=lax.Precision.HIGHEST)


def wait_bytes(ref, sem):
    pltpu.make_async_copy(ref, ref, sem).wait()


def exact_nt_dot(a, b):
    return lax.dot_general(
        a, b, (((1,), (1,)), ((), ())), preferred_element_type=F32, precision=lax.Precision.HIGHEST
    )


def pack(value, rows):
    width = LANES * rows // RANK
    lanes = lax.broadcasted_iota(jnp.int32, (rows, LANES), 1)
    packed = value[:rows]
    for k in range(1, RANK // rows):
        packed = jnp.where(lanes >= k * width, value[k * rows : (k + 1) * rows], packed)
    return packed


def unpack(packed):
    rows = packed.shape[0]
    width = LANES * rows // RANK
    return jnp.concatenate(
        [packed] + [pltpu.roll(packed, LANES - k * width, 1) for k in range(1, RANK // rows)], axis=0
    )


def sum_slots(ref, count):
    terms = [ref[n].astype(F32) for n in range(count)]
    while len(terms) > 1:
        terms = [a + b for a, b in zip(terms[::2], terms[1::2])]
    return terms[0]


def inverse_lower(gram):
    rows = lax.broadcasted_iota(jnp.int32, (RANK, LANES), 0)
    lanes = lax.broadcasted_iota(jnp.int32, (RANK, LANES), 1)
    work = jnp.where(lanes < RANK, gram, jnp.where(lanes == rows + RANK, 1.0, 0.0))
    row_ids = lax.broadcasted_iota(jnp.int32, (RANK, 1), 0)
    scale = jnp.zeros((RANK, 1), F32)
    for j in range(RANK):
        row = work[j : j + 1, :]
        pivot = work[j : j + 1, j : j + 1]
        scale = jnp.where(row_ids == j, pivot, scale)
        if j < RANK - 1:
            factor = jnp.where(row_ids > j, work[:, j : j + 1] / pivot, 0.0)
            work = work - factor * row
    return (work * lax.rsqrt(scale))[:, RANK : 2 * RANK]


def kernel(
    hid, cot, startq, out,
    hbuf, cbuf, tbuf, qf, qsrc, qgat, sk0, sk1, ptsrc, ptrs, pt, mx, part0, gram0, gram1, wbuf,
    zsrc, zrs, zall, mparts, shifted, minv, umat,
    s_local, s_core, r_core, s_q, r_q, s_sk, r_sk, s_t, r_t, s_tc, r_tc, s_prs, r_prs, s_pag, r_pag,
    s_ptc, r_ptc, s_mx, r_mx, s_g, r_g, s_w, r_w, s_zrs, r_zrs, s_qag, r_qag,
):
    dp = lax.axis_index("dp")
    y = lax.axis_index("mp")
    c = lax.rem(dp, 2)
    chip = lax.div(dp, 2)
    z = lax.div(chip, NX)
    x = lax.rem(chip, NX)
    sib = {"dp": dp + 1 - 2 * c, "mp": y}
    pt_owner = z < NZ - 1
    q_mine = 4 * lax.rem(x, 2) + lax.rem(z + 2 * lax.div(x, 2), 4)
    ending = []

    def y_dev(k):
        return {"dp": dp, "mp": lax.rem(y + k, NY)}

    def zx_chip(dz, dx):
        return lax.rem(z + dz, NZ) * NX + lax.rem(x + dx, NX)

    def zx_dev(there, core=None):
        return {"dp": there * 2 + (c if core is None else core), "mp": y}

    def send(src, dst, ssem, rsem, dev):
        pltpu.make_async_remote_copy(
            src_ref=src, dst_ref=dst, send_sem=ssem, recv_sem=rsem, device_id=dev, device_id_type=MESH
        ).start()

    def sent(ref, sem, when=None):
        def wait():
            wait_bytes(ref, sem)

        ending.append(wait if when is None else lambda: pl.when(when)(wait))

    def finish():
        while ending:
            ending.pop(0)()

    load_q = pltpu.make_async_copy(startq, qf, s_local.at[0])
    load_q.start()
    bar = pltpu.get_barrier_semaphore()
    greeted = [(_hops(*d), zx_dev(zx_chip(*d))) for d in ZX_ORDER]
    greeted += [(min(k, NY - k), y_dev(k)) for k in Y_ORDER]
    greeted += [(_hops(*d), zx_dev(zx_chip(NZ - d[0], NX - d[1]), 1 - c)) for d in NEAR[:-1]]
    greeted += [(0, sib)]
    for _, there in sorted(greeted, key=lambda e: -e[0]):
        pl.semaphore_signal(bar, inc=1, device_id=there, device_id_type=MESH)
    load_c = pltpu.make_async_copy(cot.at[0], cbuf.at[c], s_local.at[1])
    load_c.start()
    load_h = [pltpu.make_async_copy(hid.at[j], hbuf.at[j, :, c], s_local.at[2 + j]) for j in range(2)]
    load_h[0].start()
    load_h[1].start()
    load_q.wait()
    qsrc[...] = qf[pl.ds(pl.multiple_of(c * HALF, HALF), HALF), :].astype(BF)
    pl.semaphore_wait(bar, NY - 1 + CHIPS - 1 + len(NEAR))

    for n, k in enumerate(Y_ORDER):
        send(qsrc, qgat.at[n], s_q, r_q.at[n], y_dev(k))
    sent(qgat, s_q)
    send(cot.at[0], cbuf.at[c], s_core.at[0], r_core.at[0], sib)
    sent(cbuf.at[0], s_core.at[0])
    load_c.wait()
    wait_bytes(cbuf.at[0], r_core.at[0])

    def block_sketch(q_rows, owner):
        cols = pl.ds(pl.multiple_of(owner * 1024, 1024), 1024)
        return nt_dot(q_rows, cbuf[:, :, cols].reshape(RANK, 1024))

    sketch = block_sketch(qsrc[...], y)
    for n, k in sorted(enumerate(Y_ORDER), key=lambda e: min(e[1], NY - e[1])):
        wait_bytes(qgat.at[n], r_q.at[n])
        sketch = sketch + block_sketch(qgat[n], lax.rem(y - k + NY, NY))
    spot = lax.broadcasted_iota(jnp.int32, (RANK, LANES), 0) + RANK * lax.rem(y, 4)
    place = jnp.where(lax.broadcasted_iota(jnp.int32, (RANK, LANES), 1) == spot, 1.0, 0.0).astype(BF)
    sk0[y] = dot(sketch.astype(BF), place).astype(BF)
    for k in Y_ORDER:
        send(sk0.at[y], sk0.at[y], s_sk.at[0], r_sk.at[0], y_dev(k))
    sent(sk0.at[pl.ds(0, NY - 1)], s_sk.at[0])

    def share_h(j):
        send(hid.at[j], hbuf.at[j, :, c], s_core.at[1 + j], r_core.at[1 + j], sib)
        sent(hbuf.at[j, :, 0], s_core.at[1 + j])

    share_h(0)
    wait_bytes(sk0.at[pl.ds(0, NY - 1)], r_sk.at[0])

    own_cols = pl.ds(pl.multiple_of(y * 1024, 1024), 1024)
    load_t = [pltpu.make_async_copy(cot.at[j, :, own_cols], tbuf.at[j, y, c], s_local.at[4 + j]) for j in range(2)]

    def spread_t(j):
        for k in Y_ORDER:
            there = lax.rem(y + k, NY)
            cols = pl.ds(pl.multiple_of(there * 1024, 1024), 1024)
            send(cot.at[j, :, cols], tbuf.at[j, y, c], s_t.at[j], r_t.at[j], y_dev(k))
        sent(tbuf.at[j, pl.ds(0, NY - 1), 0], s_t.at[j])
        load_t[j].start()

    def share_t(j):
        load_t[j].wait()
        wait_bytes(tbuf.at[j, pl.ds(0, NY - 1), 0], r_t.at[j])
        send(tbuf.at[j, :, c], tbuf.at[j, :, c], s_tc.at[j], r_tc.at[j], sib)
        sent(tbuf.at[j, :, 0], s_tc.at[j])

    left = jnp.concatenate(
        [
            (sk0[0] + sk0[1]) + (sk0[2] + sk0[3]),
            (sk0[4] + sk0[5]) + (sk0[6] + sk0[7]),
        ],
        axis=1,
    )

    for s in range(2):
        used = s + 1
        if s == 0:
            load_h[0].wait()
            wait_bytes(hbuf.at[0, :, 0], r_core.at[1])
        if s == 1:
            wait_bytes(sk1.at[0, pl.ds(0, NY - 1)], r_sk.at[1])
            part0[...] = dot(sum_slots(sk1.at[0], NY).astype(BF), hbuf[0].reshape(256, 3584))
            load_h[1].wait()
            wait_bytes(hbuf.at[1, :, 0], r_core.at[2])
            wait_bytes(sk1.at[1, pl.ds(0, NY - 1)], r_sk.at[2])
            left = sum_slots(sk1.at[1], NY).astype(BF)
        for step in PLANES_OUT:
            n = lax.rem(z + step, NZ - 1)
            cols = pl.ds(pl.multiple_of(n * GROUP, GROUP), GROUP)
            part = dot(left, hbuf[s, :, :, :, cols].reshape(256, GROUP))
            if s == 1:
                part = part + part0[:, cols]
            part = part.astype(BF)
            for g in range(NX):
                ptsrc[s, n * NX + g] = part[:, g * LANES : (g + 1) * LANES]
            for dx in (2, 1, 3, 0):
                there = n * NX + lax.rem(x + dx, NX)

                def post(there=there):
                    send(ptsrc.at[s, there], ptrs.at[s, chip], s_prs.at[s], r_prs.at[s], zx_dev(there))

                if step == 0 and dx == 0:
                    pl.when(jnp.logical_not(pt_owner))(post)
                else:
                    post()
        if s == 0:
            share_h(1)
            spread_t(0)

        sent(ptrs.at[s, pl.ds(0, TILES - 1)], s_prs.at[s], pt_owner)
        sent(ptrs.at[s, pl.ds(0, TILES)], s_prs.at[s], jnp.logical_not(pt_owner))

        if s == 1:
            wait_bytes(wbuf.at[pl.ds(0, NY - 1)], r_w)
            weights = unpack(sum_slots(wbuf, NY))
            umat[...] = exact_dot(weights[:, :RANK], minv[0])
            qf[...] = lax.dot_general(
                minv[0], qf[...], (((0,), (0,)), ((), ())), preferred_element_type=F32, precision=lax.Precision.HIGHEST
            )

        @pl.when(pt_owner)
        def _():
            correction = 0.0
            if s == 1:
                past = jnp.concatenate([pt[0, 0, chip], pt[0, 1, chip]], axis=0).astype(F32)
                own_rows = umat[pl.ds(pl.multiple_of(c * HALF, HALF), HALF), :]
                correction = exact_dot(own_rows, past)
            ptrs[s, chip] = ptsrc[s, chip]
            wait_bytes(ptrs.at[s, pl.ds(0, CHIPS - 1)], r_prs.at[s])
            total = sum_slots(ptrs.at[s], CHIPS) * (1.0 / 64.0) - correction
            pt[s, c, chip] = total.astype(BF)
            tile = pt.at[s, c, chip]
            for d in ZX_ORDER:
                send(tile, tile, s_pag.at[s], r_pag.at[s, z], zx_dev(zx_chip(*d)))

        sent(ptrs.at[s, pl.ds(0, CHIPS - 1)], s_pag.at[s], pt_owner)

        mixed = [None] * used
        for step in PLANES_IN:
            n = lax.rem(z + step, NZ - 1)
            first = pl.multiple_of(n * NX, NX)
            if step == 0:

                @pl.when(pt_owner)
                def _():
                    wait_bytes(pt.at[s, c, pl.ds(0, NX - 1)], r_pag.at[s, z])

                @pl.when(jnp.logical_not(pt_owner))
                def _():
                    wait_bytes(pt.at[s, c, pl.ds(0, NX)], r_pag.at[s, n])

            else:
                wait_bytes(pt.at[s, c, pl.ds(0, NX)], r_pag.at[s, n])
            cols = pl.ds(pl.multiple_of(n * GROUP, GROUP), GROUP)
            rows = jnp.concatenate([pt[s, c, first + g] for g in range(NX)], axis=1)
            for j in range(used):
                term = nt_dot(rows, hbuf[j, :, :, :, cols].reshape(256, GROUP))
                mixed[j] = term if mixed[j] is None else mixed[j] + term
        send(pt.at[s, c], pt.at[s, c], s_ptc.at[s], r_ptc.at[s], sib)
        sent(pt.at[s, 0], s_ptc.at[s])
        for j in range(used):
            mx[s, j, y] = mixed[j].astype(BF)
            for k in Y_ORDER:
                send(mx.at[s, j, y], mx.at[s, j, y], s_mx.at[s, j], r_mx.at[s, j], y_dev(k))
            sent(mx.at[s, j, pl.ds(0, NY - 1)], s_mx.at[s, j])

        if s == 0:
            share_t(0)

        wait_bytes(pt.at[s, 0], r_ptc.at[s])

        def both(step):
            return jnp.concatenate(
                [
                    jnp.concatenate([pt[step, e, n] for n in range(TILES)], axis=1)
                    for e in range(2)
                ],
                axis=0,
            )

        now = both(s)
        other = now if s == 0 else both(0)
        gram = gram0 if s == 0 else gram1
        gram[y] = pack(nt_dot(now, jnp.concatenate([now, other, now, other], axis=0)), gram.shape[1])
        for k in Y_ORDER:
            send(gram.at[y], gram.at[y], s_g.at[s], r_g.at[s], y_dev(k))
        sent(gram.at[pl.ds(0, NY - 1)], s_g.at[s])
        if s == 0:
            spread_t(1)

        if s == 0:
            wait_bytes(tbuf.at[0, :, 0], r_tc.at[0])
        part = None
        for j in range(used):
            wait_bytes(mx.at[s, j, pl.ds(0, NY - 1)], r_mx.at[s, j])
            term = dot(sum_slots(mx.at[s, j], NY).astype(BF), tbuf[j].reshape(256, 1024))
            part = term if part is None else part + term
        part = part.astype(BF)
        for b in range(QBLOCKS):
            zsrc[s, b] = part[:, b * LANES : (b + 1) * LANES]
        for dz, dx in ZX_ORDER:
            there = zx_chip(dz, dx)
            b = 4 * lax.rem(x + dx, 2) + lax.rem(z + dz + 2 * lax.div(lax.rem(x + dx, NX), 2), 4)
            send(zsrc.at[s, b], zrs.at[s, chip], s_zrs.at[s], r_zrs.at[s], zx_dev(there))
        sent(zrs.at[s, pl.ds(0, CHIPS - 1)], s_zrs.at[s])

        if s == 0:
            share_t(1)
        else:
            finish()


        z_mine = (2 * s + c) * QBLOCKS + q_mine

        zrs[s, chip] = zsrc[s, q_mine]
        wait_bytes(zrs.at[s, pl.ds(0, CHIPS - 1)], r_zrs.at[s])
        zall[z_mine] = (sum_slots(zrs.at[s], CHIPS) * (1.0 / 64.0)).astype(BF)
        tile = zall.at[z_mine]
        for d in NEAR:
            for core in (c, 1 - c) if d != (0, 0) else (1 - c,):
                send(tile, tile, s_qag.at[s], r_qag.at[s], zx_dev(zx_chip(*d), core))
        sent(zall.at[pl.ds(0, 15)], s_qag.at[s])

        wait_bytes(gram.at[pl.ds(0, NY - 1)], r_g.at[s])
        inner = unpack(sum_slots(gram, NY))
        if s == 1:
            shift = exact_dot(inner[:, RANK : 2 * RANK], qf[...])
        minv[s] = inverse_lower(inner)
        rest = minv[s]
        for n in range(3):
            part = rest.astype(BF)
            mparts[n * RANK : (n + 1) * RANK, :] = part
            rest = rest - part.astype(F32)
        if s == 1:
            shifted[...] = exact_dot(minv[1], shift)
        wait_bytes(zall.at[pl.ds(0, 15)], r_qag.at[s])
        value = jnp.concatenate(
            [
                jnp.concatenate([zall[(2 * s + e) * QBLOCKS + b] for b in range(QBLOCKS)], axis=1)
                for e in range(2)
            ],
            axis=0,
        )
        parts = dot(mparts[...], value)
        value = parts[:RANK] + (parts[RANK : 2 * RANK] + parts[2 * RANK :])
        if s == 1:
            value = value - shifted[...]
        if s == 0:
            qf[...] = value
            rows = qf[pl.ds(pl.multiple_of(c * HALF, HALF), HALF), :].astype(BF)
            wait_bytes(tbuf.at[1, :, 0], r_tc.at[1])
            for j in range(2):
                sk1[j, y] = nt_dot(rows, tbuf[j].reshape(256, 1024)).astype(BF)
                for k in Y_ORDER:
                    send(sk1.at[j, y], sk1.at[j, y], s_sk.at[1 + j], r_sk.at[1 + j], y_dev(k))
                sent(sk1.at[j, pl.ds(0, NY - 1)], s_sk.at[1 + j])
            wbuf[y] = pack(exact_nt_dot(value, jnp.concatenate([value] * 4, axis=0)), 8)
            for k in Y_ORDER:
                send(wbuf.at[y], wbuf.at[y], s_w, r_w, y_dev(k))
            sent(wbuf.at[pl.ds(0, NY - 1)], s_w)
        else:
            out[...] = value

    finish()


def on_device(hidden, cotangent, start_q):
    hidden = hidden.reshape(2, NY, 16, 3584)
    dma = pltpu.SemaphoreType.DMA
    vm = pltpu.VMEM
    in_hbm = pl.BlockSpec(memory_space=pltpu.HBM)
    return pl.pallas_call(
        kernel,
        out_shape=pltpu.VMEM((RANK, 1024), F32),
        in_specs=[in_hbm] * 3,
        out_specs=pl.BlockSpec(memory_space=pltpu.VMEM),
        scratch_shapes=[
            vm((2, NY, 2, 16, 3584), BF),
            vm((2, 16, 8192), BF),
            vm((2, NY, 2, 16, 1024), BF),
            vm((RANK, 1024), F32),
            vm((HALF, 1024), BF),
            vm((NY - 1, HALF, 1024), BF),
            vm((NY, HALF, LANES), BF),
            vm((2, NY, HALF, 256), BF),
            vm((2, TILES, HALF, LANES), BF),
            vm((2, CHIPS, HALF, LANES), BF),
            vm((2, 2, TILES, HALF, LANES), BF),
            vm((2, 2, NY, HALF, 256), BF),
            vm((HALF, 3584), F32),
            vm((NY, 8, LANES), F32),
            vm((NY, 16, LANES), F32),
            vm((NY, 8, LANES), F32),
            vm((2, QBLOCKS, HALF, LANES), BF),
            vm((2, CHIPS, HALF, LANES), BF),
            vm((4 * QBLOCKS, HALF, LANES), BF),
            vm((3 * RANK, RANK), BF),
            vm((RANK, 1024), F32),
            vm((2, RANK, RANK), F32),
            vm((RANK, RANK), F32),
            dma((6,)),
            dma((3,)), dma((3,)),
            dma, dma((NY - 1,)),
            dma((3,)), dma((3,)),
            dma((2,)), dma((2,)),
            dma((2,)), dma((2,)),
            dma((2,)), dma((2,)),
            dma((2,)), dma((2, NZ - 1)),
            dma((2,)), dma((2,)),
            dma((2, 2)), dma((2, 2)),
            dma((2,)), dma((2,)),
            dma, dma,
            dma((2,)), dma((2,)),
            dma((2,)), dma((2,)),
        ],
        compiler_params=pltpu.CompilerParams(
            collective_id=0, has_side_effects=True, vmem_limit_bytes=56 * 1024 * 1024
        ),
        name="powersgd",
    )(hidden, cotangent, start_q)


def solution(mesh):
    return jax.shard_map(
        on_device,
        mesh=mesh,
        in_specs=(P(None, "dp", "mp"), P(None, ("dp", "mp"), None), P(None, "mp")),
        out_specs=P(None, "mp"),
        check_vma=False,
    )
```

```python
import functools

import jax
import jax.numpy as jnp
from jax import lax
from jax.experimental import pallas as pl
from jax.experimental.pallas import tpu as pltpu
from jax.sharding import PartitionSpec as P

MESH = pl.DeviceIdType.MESH
BF = jnp.bfloat16
F32 = jnp.float32
NY = 8
NZ = 8
NX = 4
CHIPS = NZ * NX
TILES = 28
QBLOCKS = 8
HALF = 16
RANK = 32
LANES = 128
GROUP = NX * LANES
Y_ORDER = (4, 3, 5, 2, 6, 1, 7)


def _hops(dz, dx):
    return min(dz, NZ - dz) + min(dx, NX - dx)


ZX_ORDER = sorted(
    [(dz, dx) for dz in range(NZ) for dx in range(NX) if (dz, dx) != (0, 0)],
    key=lambda d: (-_hops(*d), d),
)
NEAR = ((2, 0), (1, 1), (7, 1), (1, 0), (7, 0), (0, 1), (0, 3), (0, 0))
PLANES_IN = (0, 1, 6, 2, 5, 3, 4)
PLANES_OUT = (4, 3, 5, 2, 6, 1, 0)


def nt_dot(a, b):
    return lax.dot_general(a, b, (((1,), (1,)), ((), ())), preferred_element_type=F32)


def dot(a, b):
    return jnp.dot(a, b, preferred_element_type=F32)


def exact_dot(a, b):
    return jnp.dot(a, b, preferred_element_type=F32, precision=lax.Precision.HIGHEST)


def wait_bytes(ref, sem):
    pltpu.make_async_copy(ref, ref, sem).wait()


def exact_nt_dot(a, b):
    return lax.dot_general(
        a, b, (((1,), (1,)), ((), ())), preferred_element_type=F32, precision=lax.Precision.HIGHEST
    )


def pack(value, rows):
    width = LANES * rows // RANK
    lanes = lax.broadcasted_iota(jnp.int32, (rows, LANES), 1)
    packed = value[:rows]
    for k in range(1, RANK // rows):
        packed = jnp.where(lanes >= k * width, value[k * rows : (k + 1) * rows], packed)
    return packed


def unpack(packed):
    rows = packed.shape[0]
    width = LANES * rows // RANK
    return jnp.concatenate(
        [packed] + [pltpu.roll(packed, LANES - k * width, 1) for k in range(1, RANK // rows)], axis=0
    )


def sum_terms(terms):
    while len(terms) > 1:
        terms = [a + b for a, b in zip(terms[::2], terms[1::2])] + terms[len(terms) & ~1 :]
    return terms[0]


def sum_slots(ref, count):
    return sum_terms([ref[n].astype(F32) for n in range(count)])


def inverse_lower(gram):
    rows = lax.broadcasted_iota(jnp.int32, (RANK, LANES), 0)
    lanes = lax.broadcasted_iota(jnp.int32, (RANK, LANES), 1)
    work = jnp.where(lanes < RANK, gram, jnp.where(lanes == rows + RANK, 1.0, 0.0))
    row_ids = lax.broadcasted_iota(jnp.int32, (RANK, 1), 0)
    scale = jnp.zeros((RANK, 1), F32)
    for j in range(RANK):
        row = work[j : j + 1, :]
        pivot = work[j : j + 1, j : j + 1]
        scale = jnp.where(row_ids == j, pivot, scale)
        if j < RANK - 1:
            factor = jnp.where(row_ids > j, work[:, j : j + 1] / pivot, 0.0)
            work = work - factor * row
    return (work * lax.rsqrt(scale))[:, RANK : 2 * RANK]


def kernel(
    hid, cot, startq, out,
    hbuf, cbuf, tbuf, qf, qsrc, qgat, sk0, sk1, ptsrc, ptrs, pt, mx, part0, gram0, gram1, wbuf,
    zsrc, zrs, zall, mparts, shifted, minv, umat,
    s_local, s_core, r_core, s_q, r_q, s_sk, r_sk, s_t, r_t, s_tc, r_tc, s_prs, r_prs, s_pag, r_pag,
    s_ptc, r_ptc, s_mx, r_mx, s_g, r_g, s_w, r_w, s_zrs, r_zrs, s_qag, r_qag,
):
    dp = lax.axis_index("dp")
    y = lax.axis_index("mp")
    c = lax.rem(dp, 2)
    chip = lax.div(dp, 2)
    z = lax.div(chip, NX)
    x = lax.rem(chip, NX)
    sib = {"dp": dp + 1 - 2 * c, "mp": y}
    pt_owner = z < NZ - 1
    q_mine = 4 * lax.rem(x, 2) + lax.rem(z + 2 * lax.div(x, 2), 4)
    ending = []

    def y_dev(k):
        return {"dp": dp, "mp": lax.rem(y + k, NY)}

    def zx_chip(dz, dx):
        return lax.rem(z + dz, NZ) * NX + lax.rem(x + dx, NX)

    def zx_dev(there, core=None):
        return {"dp": there * 2 + (c if core is None else core), "mp": y}

    def send(src, dst, ssem, rsem, dev):
        pltpu.make_async_remote_copy(
            src_ref=src, dst_ref=dst, send_sem=ssem, recv_sem=rsem, device_id=dev, device_id_type=MESH
        ).start()

    def sent(ref, sem, when=None):
        def wait():
            wait_bytes(ref, sem)

        ending.append(wait if when is None else lambda: pl.when(when)(wait))

    def finish():
        while ending:
            ending.pop(0)()

    load_q = pltpu.make_async_copy(startq, qf, s_local.at[0])
    load_q.start()
    bar = pltpu.get_barrier_semaphore()
    greeted = [(_hops(*d), zx_dev(zx_chip(*d))) for d in ZX_ORDER]
    greeted += [(min(k, NY - k), y_dev(k)) for k in Y_ORDER]
    greeted += [(_hops(*d), zx_dev(zx_chip(NZ - d[0], NX - d[1]), 1 - c)) for d in NEAR[:-1]]
    greeted += [(0, sib)]
    for _, there in sorted(greeted, key=lambda e: -e[0]):
        pl.semaphore_signal(bar, inc=1, device_id=there, device_id_type=MESH)
    load_c = pltpu.make_async_copy(cot.at[0], cbuf.at[c], s_local.at[1])
    load_c.start()
    load_h = [pltpu.make_async_copy(hid.at[j], hbuf.at[j, :, c], s_local.at[2 + j]) for j in range(2)]
    load_h[0].start()
    load_h[1].start()
    load_q.wait()
    qsrc[...] = qf[pl.ds(pl.multiple_of(c * HALF, HALF), HALF), :].astype(BF)
    pl.semaphore_wait(bar, NY - 1 + CHIPS - 1 + len(NEAR))

    for n, k in enumerate(Y_ORDER):
        send(qsrc, qgat.at[n], s_q, r_q.at[n], y_dev(k))
    sent(qgat, s_q)
    send(cot.at[0], cbuf.at[c], s_core.at[0], r_core.at[0], sib)
    sent(cbuf.at[0], s_core.at[0])
    load_c.wait()
    wait_bytes(cbuf.at[0], r_core.at[0])

    def block_sketch(q_rows, owner):
        cols = pl.ds(pl.multiple_of(owner * 1024, 1024), 1024)
        return nt_dot(q_rows, cbuf[:, :, cols].reshape(RANK, 1024))

    terms = [block_sketch(qsrc[...], y)]
    for some in ((1, 7, 2, 6), (3, 5, 4)):
        for k in some:
            wait_bytes(qgat.at[Y_ORDER.index(k)], r_q.at[Y_ORDER.index(k)])
        terms += [block_sketch(qgat[Y_ORDER.index(k)], lax.rem(y - k + NY, NY)) for k in some]
    sketch = sum_terms(terms)
    spot = lax.broadcasted_iota(jnp.int32, (RANK, LANES), 0) + RANK * lax.rem(y, 4)
    place = jnp.where(lax.broadcasted_iota(jnp.int32, (RANK, LANES), 1) == spot, 1.0, 0.0).astype(BF)
    sk0[y] = dot(sketch.astype(BF), place).astype(BF)
    for k in Y_ORDER:
        send(sk0.at[y], sk0.at[y], s_sk.at[0], r_sk.at[0], y_dev(k))
    sent(sk0.at[pl.ds(0, NY - 1)], s_sk.at[0])

    def share_h(j):
        send(hid.at[j], hbuf.at[j, :, c], s_core.at[1 + j], r_core.at[1 + j], sib)
        sent(hbuf.at[j, :, 0], s_core.at[1 + j])

    share_h(0)
    wait_bytes(sk0.at[pl.ds(0, NY - 1)], r_sk.at[0])

    own_cols = pl.ds(pl.multiple_of(y * 1024, 1024), 1024)
    load_t = [pltpu.make_async_copy(cot.at[j, :, own_cols], tbuf.at[j, y, c], s_local.at[4 + j]) for j in range(2)]

    def spread_t(j):
        for k in Y_ORDER:
            there = lax.rem(y + k, NY)
            cols = pl.ds(pl.multiple_of(there * 1024, 1024), 1024)
            send(cot.at[j, :, cols], tbuf.at[j, y, c], s_t.at[j], r_t.at[j], y_dev(k))
        sent(tbuf.at[j, pl.ds(0, NY - 1), 0], s_t.at[j])
        load_t[j].start()

    def share_t(j):
        load_t[j].wait()
        wait_bytes(tbuf.at[j, pl.ds(0, NY - 1), 0], r_t.at[j])
        send(tbuf.at[j, :, c], tbuf.at[j, :, c], s_tc.at[j], r_tc.at[j], sib)
        sent(tbuf.at[j, :, 0], s_tc.at[j])

    left = jnp.concatenate(
        [
            (sk0[0] + sk0[1]) + (sk0[2] + sk0[3]),
            (sk0[4] + sk0[5]) + (sk0[6] + sk0[7]),
        ],
        axis=1,
    )

    for s in range(2):
        used = s + 1
        if s == 0:
            load_h[0].wait()
            wait_bytes(hbuf.at[0, :, 0], r_core.at[1])
        if s == 1:
            wait_bytes(sk1.at[0, pl.ds(0, NY - 1)], r_sk.at[1])
            part0[...] = dot(sum_slots(sk1.at[0], NY).astype(BF), hbuf[0].reshape(256, 3584))
            load_h[1].wait()
            wait_bytes(hbuf.at[1, :, 0], r_core.at[2])
            wait_bytes(sk1.at[1, pl.ds(0, NY - 1)], r_sk.at[2])
            left = sum_slots(sk1.at[1], NY).astype(BF)
        for step in PLANES_OUT:
            n = lax.rem(z + step, NZ - 1)
            cols = pl.ds(pl.multiple_of(n * GROUP, GROUP), GROUP)
            part = dot(left, hbuf[s, :, :, :, cols].reshape(256, GROUP))
            if s == 1:
                part = part + part0[:, cols]
            part = part.astype(BF)
            for g in range(NX):
                ptsrc[s, n * NX + g] = part[:, g * LANES : (g + 1) * LANES]
            for dx in (2, 1, 3, 0):
                there = n * NX + lax.rem(x + dx, NX)

                def post(there=there):
                    send(ptsrc.at[s, there], ptrs.at[s, chip], s_prs.at[s], r_prs.at[s], zx_dev(there))

                if step == 0 and dx == 0:
                    pl.when(jnp.logical_not(pt_owner))(post)
                else:
                    post()
        if s == 0:
            share_h(1)
            spread_t(0)

        sent(ptrs.at[s, pl.ds(0, TILES - 1)], s_prs.at[s], pt_owner)
        sent(ptrs.at[s, pl.ds(0, TILES)], s_prs.at[s], jnp.logical_not(pt_owner))

        if s == 1:
            wait_bytes(wbuf.at[pl.ds(0, NY - 1)], r_w)
            weights = unpack(sum_slots(wbuf, NY))
            umat[...] = exact_dot(weights[:, :RANK], minv[0])
            qf[...] = lax.dot_general(
                minv[0], qf[...], (((0,), (0,)), ((), ())), preferred_element_type=F32, precision=lax.Precision.HIGHEST
            )

        @pl.when(pt_owner)
        def _():
            correction = 0.0
            if s == 1:
                past = jnp.concatenate([pt[0, 0, chip], pt[0, 1, chip]], axis=0).astype(F32)
                own_rows = umat[pl.ds(pl.multiple_of(c * HALF, HALF), HALF), :]
                correction = exact_dot(own_rows, past)
            ptrs[s, chip] = ptsrc[s, chip]
            wait_bytes(ptrs.at[s, pl.ds(0, CHIPS - 1)], r_prs.at[s])
            total = sum_slots(ptrs.at[s], CHIPS) * (1.0 / 64.0) - correction
            pt[s, c, chip] = total.astype(BF)
            tile = pt.at[s, c, chip]
            for d in ZX_ORDER:
                send(tile, tile, s_pag.at[s], r_pag.at[s, z], zx_dev(zx_chip(*d)))

        sent(ptrs.at[s, pl.ds(0, CHIPS - 1)], s_pag.at[s], pt_owner)

        mixed = [None] * used
        for step in PLANES_IN:
            n = lax.rem(z + step, NZ - 1)
            if step == 0:

                @pl.when(pt_owner)
                def _():
                    wait_bytes(pt.at[s, c, pl.ds(0, NX - 1)], r_pag.at[s, z])

                @pl.when(jnp.logical_not(pt_owner))
                def _():
                    wait_bytes(pt.at[s, c, pl.ds(0, NX)], r_pag.at[s, n])

            else:
                wait_bytes(pt.at[s, c, pl.ds(0, NX)], r_pag.at[s, n])
            if step not in (5, 4):
                continue
            for late in PLANES_IN[:5] if step == 5 else PLANES_IN[5:]:
                n = lax.rem(z + late, NZ - 1)
                cols = pl.ds(pl.multiple_of(n * GROUP, GROUP), GROUP)
                rows = jnp.concatenate([pt[s, c, n * NX + g] for g in range(NX)], axis=1)
                for j in range(used):
                    term = nt_dot(rows, hbuf[j, :, :, :, cols].reshape(256, GROUP))
                    mixed[j] = term if mixed[j] is None else mixed[j] + term
        send(pt.at[s, c], pt.at[s, c], s_ptc.at[s], r_ptc.at[s], sib)
        sent(pt.at[s, 0], s_ptc.at[s])
        for j in range(used):
            mx[s, j, y] = mixed[j].astype(BF)
            for k in Y_ORDER:
                send(mx.at[s, j, y], mx.at[s, j, y], s_mx.at[s, j], r_mx.at[s, j], y_dev(k))
            sent(mx.at[s, j, pl.ds(0, NY - 1)], s_mx.at[s, j])

        if s == 0:
            share_t(0)

        wait_bytes(pt.at[s, 0], r_ptc.at[s])

        def both(step):
            return jnp.concatenate(
                [
                    jnp.concatenate([pt[step, e, n] for n in range(TILES)], axis=1)
                    for e in range(2)
                ],
                axis=0,
            )

        now = both(s)
        other = now if s == 0 else both(0)
        gram = gram0 if s == 0 else gram1
        gram[y] = pack(nt_dot(now, jnp.concatenate([now, other, now, other], axis=0)), gram.shape[1])
        for k in Y_ORDER:
            send(gram.at[y], gram.at[y], s_g.at[s], r_g.at[s], y_dev(k))
        sent(gram.at[pl.ds(0, NY - 1)], s_g.at[s])
        if s == 0:
            spread_t(1)

        if s == 0:
            wait_bytes(tbuf.at[0, :, 0], r_tc.at[0])
        part = None
        for j in range(used):
            wait_bytes(mx.at[s, j, pl.ds(0, NY - 1)], r_mx.at[s, j])
            term = dot(sum_slots(mx.at[s, j], NY).astype(BF), tbuf[j].reshape(256, 1024))
            part = term if part is None else part + term
        part = part.astype(BF)
        for b in range(QBLOCKS):
            zsrc[s, b] = part[:, b * LANES : (b + 1) * LANES]
        for dz, dx in ZX_ORDER:
            there = zx_chip(dz, dx)
            b = 4 * lax.rem(x + dx, 2) + lax.rem(z + dz + 2 * lax.div(lax.rem(x + dx, NX), 2), 4)
            send(zsrc.at[s, b], zrs.at[s, chip], s_zrs.at[s], r_zrs.at[s], zx_dev(there))
        sent(zrs.at[s, pl.ds(0, CHIPS - 1)], s_zrs.at[s])

        if s == 0:
            share_t(1)
        else:
            finish()


        z_mine = (2 * s + c) * QBLOCKS + q_mine

        zrs[s, chip] = zsrc[s, q_mine]
        wait_bytes(zrs.at[s, pl.ds(0, CHIPS - 1)], r_zrs.at[s])
        zall[z_mine] = (sum_slots(zrs.at[s], CHIPS) * (1.0 / 64.0)).astype(BF)
        tile = zall.at[z_mine]
        for d in NEAR:
            for core in (c, 1 - c) if d != (0, 0) else (1 - c,):
                send(tile, tile, s_qag.at[s], r_qag.at[s], zx_dev(zx_chip(*d), core))
        sent(zall.at[pl.ds(0, 15)], s_qag.at[s])

        wait_bytes(gram.at[pl.ds(0, NY - 1)], r_g.at[s])
        inner = unpack(sum_slots(gram, NY))
        if s == 1:
            shift = exact_dot(inner[:, RANK : 2 * RANK], qf[...])
        minv[s] = inverse_lower(inner)
        rest = minv[s]
        for n in range(3):
            part = rest.astype(BF)
            mparts[n * RANK : (n + 1) * RANK, :] = part
            rest = rest - part.astype(F32)
        if s == 1:
            shifted[...] = exact_dot(minv[1], shift)
        wait_bytes(zall.at[pl.ds(0, 15)], r_qag.at[s])
        value = jnp.concatenate(
            [
                jnp.concatenate([zall[(2 * s + e) * QBLOCKS + b] for b in range(QBLOCKS)], axis=1)
                for e in range(2)
            ],
            axis=0,
        )
        parts = dot(mparts[...], value)
        value = parts[:RANK] + (parts[RANK : 2 * RANK] + parts[2 * RANK :])
        if s == 1:
            value = value - shifted[...]
        if s == 0:
            qf[...] = value
            rows = jnp.where(c == 0, value[:HALF], value[HALF:]).astype(BF)
            wait_bytes(tbuf.at[1, :, 0], r_tc.at[1])
            for j in range(2):
                sk1[j, y] = nt_dot(rows, tbuf[j].reshape(256, 1024)).astype(BF)
                for k in Y_ORDER:
                    send(sk1.at[j, y], sk1.at[j, y], s_sk.at[1 + j], r_sk.at[1 + j], y_dev(k))
                sent(sk1.at[j, pl.ds(0, NY - 1)], s_sk.at[1 + j])
            wbuf[y] = pack(exact_nt_dot(value, jnp.concatenate([value] * 4, axis=0)), 8)
            for k in Y_ORDER:
                send(wbuf.at[y], wbuf.at[y], s_w, r_w, y_dev(k))
            sent(wbuf.at[pl.ds(0, NY - 1)], s_w)
        else:
            out[...] = value

    finish()


def on_device(hidden, cotangent, start_q):
    hidden = hidden.reshape(2, NY, 16, 3584)
    dma = pltpu.SemaphoreType.DMA
    vm = pltpu.VMEM
    in_hbm = pl.BlockSpec(memory_space=pltpu.HBM)
    return pl.pallas_call(
        kernel,
        out_shape=pltpu.VMEM((RANK, 1024), F32),
        in_specs=[in_hbm] * 3,
        out_specs=pl.BlockSpec(memory_space=pltpu.VMEM),
        scratch_shapes=[
            vm((2, NY, 2, 16, 3584), BF),
            vm((2, 16, 8192), BF),
            vm((2, NY, 2, 16, 1024), BF),
            vm((RANK, 1024), F32),
            vm((HALF, 1024), BF),
            vm((NY - 1, HALF, 1024), BF),
            vm((NY, HALF, LANES), BF),
            vm((2, NY, HALF, 256), BF),
            vm((2, TILES, HALF, LANES), BF),
            vm((2, CHIPS, HALF, LANES), BF),
            vm((2, 2, TILES, HALF, LANES), BF),
            vm((2, 2, NY, HALF, 256), BF),
            vm((HALF, 3584), F32),
            vm((NY, 8, LANES), F32),
            vm((NY, 16, LANES), F32),
            vm((NY, 8, LANES), F32),
            vm((2, QBLOCKS, HALF, LANES), BF),
            vm((2, CHIPS, HALF, LANES), BF),
            vm((4 * QBLOCKS, HALF, LANES), BF),
            vm((3 * RANK, RANK), BF),
            vm((RANK, 1024), F32),
            vm((2, RANK, RANK), F32),
            vm((RANK, RANK), F32),
            dma((6,)),
            dma((3,)), dma((3,)),
            dma, dma((NY - 1,)),
            dma((3,)), dma((3,)),
            dma((2,)), dma((2,)),
            dma((2,)), dma((2,)),
            dma((2,)), dma((2,)),
            dma((2,)), dma((2, NZ - 1)),
            dma((2,)), dma((2,)),
            dma((2, 2)), dma((2, 2)),
            dma((2,)), dma((2,)),
            dma, dma,
            dma((2,)), dma((2,)),
            dma((2,)), dma((2,)),
        ],
        compiler_params=pltpu.CompilerParams(
            collective_id=0, has_side_effects=True, vmem_limit_bytes=56 * 1024 * 1024
        ),
        name="powersgd",
    )(hidden, cotangent, start_q)


def solution(mesh):
    return jax.shard_map(
        on_device,
        mesh=mesh,
        in_specs=(P(None, "dp", "mp"), P(None, ("dp", "mp"), None), P(None, "mp")),
        out_specs=P(None, "mp"),
        check_vma=False,
    )
```

```python
import functools

import jax
import jax.numpy as jnp
from jax import lax
from jax.experimental import pallas as pl
from jax.experimental.pallas import tpu as pltpu
from jax.sharding import PartitionSpec as P

MESH = pl.DeviceIdType.MESH
BF = jnp.bfloat16
F32 = jnp.float32
NY = 8
NZ = 8
NX = 4
CHIPS = NZ * NX
TILES = 28
QBLOCKS = 8
HALF = 16
RANK = 32
LANES = 128
GROUP = NX * LANES
Y_ORDER = (4, 3, 5, 2, 6, 1, 7)


def _hops(dz, dx):
    return min(dz, NZ - dz) + min(dx, NX - dx)


ZX_ORDER = sorted(
    [(dz, dx) for dz in range(NZ) for dx in range(NX) if (dz, dx) != (0, 0)],
    key=lambda d: (-_hops(*d), d),
)
NEAR = ((2, 0), (1, 1), (7, 1), (1, 0), (7, 0), (0, 1), (0, 3), (0, 0))
PLANES_IN = (0, 1, 6, 2, 5, 3, 4)
PLANES_OUT = (4, 3, 5, 2, 6, 1, 0)


def nt_dot(a, b):
    return lax.dot_general(a, b, (((1,), (1,)), ((), ())), preferred_element_type=F32)


def dot(a, b):
    return jnp.dot(a, b, preferred_element_type=F32)


def exact_dot(a, b):
    return jnp.dot(a, b, preferred_element_type=F32, precision=lax.Precision.HIGHEST)


def wait_bytes(ref, sem):
    pltpu.make_async_copy(ref, ref, sem).wait()


def exact_nt_dot(a, b):
    return lax.dot_general(
        a, b, (((1,), (1,)), ((), ())), preferred_element_type=F32, precision=lax.Precision.HIGHEST
    )


def pack(value, rows):
    width = LANES * rows // RANK
    lanes = lax.broadcasted_iota(jnp.int32, (rows, LANES), 1)
    packed = value[:rows]
    for k in range(1, RANK // rows):
        packed = jnp.where(lanes >= k * width, value[k * rows : (k + 1) * rows], packed)
    return packed


def unpack(packed):
    rows = packed.shape[0]
    width = LANES * rows // RANK
    return jnp.concatenate(
        [packed] + [pltpu.roll(packed, LANES - k * width, 1) for k in range(1, RANK // rows)], axis=0
    )


def sum_slots(ref, count):
    terms = [ref[n].astype(F32) for n in range(count)]
    while len(terms) > 1:
        terms = [a + b for a, b in zip(terms[::2], terms[1::2])]
    return terms[0]


def inverse_lower(gram):
    rows = lax.broadcasted_iota(jnp.int32, (RANK, LANES), 0)
    lanes = lax.broadcasted_iota(jnp.int32, (RANK, LANES), 1)
    work = jnp.where(lanes < RANK, gram, jnp.where(lanes == rows + RANK, 1.0, 0.0))
    row_ids = lax.broadcasted_iota(jnp.int32, (RANK, 1), 0)
    scale = jnp.zeros((RANK, 1), F32)
    for j in range(RANK):
        row = work[j : j + 1, :]
        pivot = work[j : j + 1, j : j + 1]
        scale = jnp.where(row_ids == j, pivot, scale)
        if j < RANK - 1:
            factor = jnp.where(row_ids > j, work[:, j : j + 1] / pivot, 0.0)
            work = work - factor * row
    return (work * lax.rsqrt(scale))[:, RANK : 2 * RANK]


def kernel(
    hid, cot, startq, out,
    hbuf, cbuf, tbuf, qf, qsrc, qgat, sk0, sk1, ptsrc, ptrs, pt, mx0, mx1, gram0, gram1, wbuf,
    zsrc, zrs, zall, mparts, shifted, minv, umat,
    s_local, s_core, r_core, s_q, r_q, s_sk, r_sk, s_t, r_t, s_tc, r_tc, s_prs, r_prs, s_pag, r_pag,
    s_ptc, r_ptc, s_mx, r_mx, s_g, r_g, s_w, r_w, s_zrs, r_zrs, s_qag, r_qag,
):
    dp = lax.axis_index("dp")
    y = lax.axis_index("mp")
    c = lax.rem(dp, 2)
    chip = lax.div(dp, 2)
    z = lax.div(chip, NX)
    x = lax.rem(chip, NX)
    sib = {"dp": dp + 1 - 2 * c, "mp": y}
    pt_owner = z < NZ - 1
    q_mine = 4 * lax.rem(x, 2) + lax.rem(z + 2 * lax.div(x, 2), 4)
    ending = []

    def y_dev(k):
        return {"dp": dp, "mp": lax.rem(y + k, NY)}

    def zx_chip(dz, dx):
        return lax.rem(z + dz, NZ) * NX + lax.rem(x + dx, NX)

    def zx_dev(there, core=None):
        return {"dp": there * 2 + (c if core is None else core), "mp": y}

    def send(src, dst, ssem, rsem, dev):
        pltpu.make_async_remote_copy(
            src_ref=src, dst_ref=dst, send_sem=ssem, recv_sem=rsem, device_id=dev, device_id_type=MESH
        ).start()

    def sent(ref, sem, when=None):
        def wait():
            wait_bytes(ref, sem)

        ending.append(wait if when is None else lambda: pl.when(when)(wait))

    def finish():
        while ending:
            ending.pop(0)()

    load_q = pltpu.make_async_copy(startq, qf, s_local.at[0])
    load_q.start()
    bar = pltpu.get_barrier_semaphore()
    greeted = [(_hops(*d), zx_dev(zx_chip(*d))) for d in ZX_ORDER]
    greeted += [(min(k, NY - k), y_dev(k)) for k in Y_ORDER]
    greeted += [(_hops(*d), zx_dev(zx_chip(NZ - d[0], NX - d[1]), 1 - c)) for d in NEAR[:-1]]
    greeted += [(0, sib)]
    for _, there in sorted(greeted, key=lambda e: -e[0]):
        pl.semaphore_signal(bar, inc=1, device_id=there, device_id_type=MESH)
    load_c = pltpu.make_async_copy(cot.at[0], cbuf.at[c], s_local.at[1])
    load_c.start()
    load_h = [pltpu.make_async_copy(hid.at[j], hbuf.at[j, :, c], s_local.at[2 + j]) for j in range(2)]
    load_h[0].start()
    load_h[1].start()
    load_q.wait()
    qsrc[...] = qf[pl.ds(pl.multiple_of(c * HALF, HALF), HALF), :].astype(BF)
    pl.semaphore_wait(bar, NY - 1 + CHIPS - 1 + len(NEAR))

    for n, k in enumerate(Y_ORDER):
        send(qsrc, qgat.at[n], s_q, r_q.at[n], y_dev(k))
    sent(qgat, s_q)
    send(cot.at[0], cbuf.at[c], s_core.at[0], r_core.at[0], sib)
    sent(cbuf.at[0], s_core.at[0])
    load_c.wait()
    wait_bytes(cbuf.at[0], r_core.at[0])

    def block_sketch(q_rows, owner):
        cols = pl.ds(pl.multiple_of(owner * 1024, 1024), 1024)
        return nt_dot(q_rows, cbuf[:, :, cols].reshape(RANK, 1024))

    sketch = block_sketch(qsrc[...], y)
    for n, k in sorted(enumerate(Y_ORDER), key=lambda e: min(e[1], NY - e[1])):
        wait_bytes(qgat.at[n], r_q.at[n])
        sketch = sketch + block_sketch(qgat[n], lax.rem(y - k + NY, NY))
    spot = lax.broadcasted_iota(jnp.int32, (RANK, LANES), 0) + RANK * lax.rem(y, 4)
    place = jnp.where(lax.broadcasted_iota(jnp.int32, (RANK, LANES), 1) == spot, 1.0, 0.0).astype(BF)
    sk0[y] = dot(sketch.astype(BF), place).astype(BF)
    for k in Y_ORDER:
        send(sk0.at[y], sk0.at[y], s_sk.at[0], r_sk.at[0], y_dev(k))
    sent(sk0.at[pl.ds(0, NY - 1)], s_sk.at[0])

    def share_h(j):
        send(hid.at[j], hbuf.at[j, :, c], s_core.at[1 + j], r_core.at[1 + j], sib)
        sent(hbuf.at[j, :, 0], s_core.at[1 + j])

    share_h(0)
    wait_bytes(sk0.at[pl.ds(0, NY - 1)], r_sk.at[0])

    own_cols = pl.ds(pl.multiple_of(y * 1024, 1024), 1024)
    load_t = [pltpu.make_async_copy(cot.at[j, :, own_cols], tbuf.at[j, y, c], s_local.at[4 + j]) for j in range(2)]

    def spread_t(j):
        for k in Y_ORDER:
            there = lax.rem(y + k, NY)
            cols = pl.ds(pl.multiple_of(there * 1024, 1024), 1024)
            send(cot.at[j, :, cols], tbuf.at[j, y, c], s_t.at[j], r_t.at[j], y_dev(k))
        sent(tbuf.at[j, pl.ds(0, NY - 1), 0], s_t.at[j])
        load_t[j].start()

    def share_t(j):
        load_t[j].wait()
        wait_bytes(tbuf.at[j, pl.ds(0, NY - 1), 0], r_t.at[j])
        send(tbuf.at[j, :, c], tbuf.at[j, :, c], s_tc.at[j], r_tc.at[j], sib)
        sent(tbuf.at[j, :, 0], s_tc.at[j])

    left = jnp.concatenate(
        [
            (sk0[0] + sk0[1]) + (sk0[2] + sk0[3]),
            (sk0[4] + sk0[5]) + (sk0[6] + sk0[7]),
        ],
        axis=1,
    )

    for s in range(2):
        used = s + 1
        if s == 0:
            load_h[0].wait()
            wait_bytes(hbuf.at[0, :, 0], r_core.at[1])
        if s == 1:
            load_h[1].wait()
            wait_bytes(hbuf.at[1, :, 0], r_core.at[2])
            wait_bytes(sk1.at[pl.ds(0, NY - 1)], r_sk.at[1])
            left = jnp.concatenate([sum_slots(sk1.at[:, j], NY).astype(BF) for j in range(2)], axis=1)
        for step in PLANES_OUT:
            n = lax.rem(z + step, NZ - 1)
            cols = pl.ds(pl.multiple_of(n * GROUP, GROUP), GROUP)
            part = dot(left[:, :256], hbuf[0, :, :, :, cols].reshape(256, GROUP))
            if s == 1:
                part = part + dot(left[:, 256:], hbuf[1, :, :, :, cols].reshape(256, GROUP))
            part = part.astype(BF)
            for g in range(NX):
                ptsrc[s, n * NX + g] = part[:, g * LANES : (g + 1) * LANES]
            for dx in (2, 1, 3, 0):
                there = n * NX + lax.rem(x + dx, NX)

                def post(there=there):
                    send(ptsrc.at[s, there], ptrs.at[s, chip], s_prs.at[s], r_prs.at[s], zx_dev(there))

                if step == 0 and dx == 0:
                    pl.when(jnp.logical_not(pt_owner))(post)
                else:
                    post()
        if s == 0:
            share_h(1)
            spread_t(0)

        sent(ptrs.at[s, pl.ds(0, TILES - 1)], s_prs.at[s], pt_owner)
        sent(ptrs.at[s, pl.ds(0, TILES)], s_prs.at[s], jnp.logical_not(pt_owner))

        if s == 1:
            wait_bytes(wbuf.at[pl.ds(0, NY - 1)], r_w)
            weights = unpack(sum_slots(wbuf, NY))
            umat[...] = exact_dot(weights[:, :RANK], minv[0])
            qf[...] = lax.dot_general(
                minv[0], qf[...], (((0,), (0,)), ((), ())), preferred_element_type=F32, precision=lax.Precision.HIGHEST
            )

        @pl.when(pt_owner)
        def _():
            correction = 0.0
            if s == 1:
                past = jnp.concatenate([pt[0, 0, chip], pt[0, 1, chip]], axis=0).astype(F32)
                own_rows = umat[pl.ds(pl.multiple_of(c * HALF, HALF), HALF), :]
                correction = exact_dot(own_rows, past)
            ptrs[s, chip] = ptsrc[s, chip]
            wait_bytes(ptrs.at[s, pl.ds(0, CHIPS - 1)], r_prs.at[s])
            total = sum_slots(ptrs.at[s], CHIPS) * (1.0 / 64.0) - correction
            pt[s, c, chip] = total.astype(BF)
            tile = pt.at[s, c, chip]
            for d in ZX_ORDER:
                send(tile, tile, s_pag.at[s], r_pag.at[s, z], zx_dev(zx_chip(*d)))

        sent(ptrs.at[s, pl.ds(0, CHIPS - 1)], s_pag.at[s], pt_owner)

        mx = mx0 if s == 0 else mx1
        mixed = [None] * used
        for step in PLANES_IN:
            n = lax.rem(z + step, NZ - 1)
            first = pl.multiple_of(n * NX, NX)
            if step == 0:

                @pl.when(pt_owner)
                def _():
                    wait_bytes(pt.at[s, c, pl.ds(0, NX - 1)], r_pag.at[s, z])

                @pl.when(jnp.logical_not(pt_owner))
                def _():
                    wait_bytes(pt.at[s, c, pl.ds(0, NX)], r_pag.at[s, n])

            else:
                wait_bytes(pt.at[s, c, pl.ds(0, NX)], r_pag.at[s, n])
            cols = pl.ds(pl.multiple_of(n * GROUP, GROUP), GROUP)
            rows = jnp.concatenate([pt[s, c, first + g] for g in range(NX)], axis=1)
            for j in range(used):
                term = nt_dot(rows, hbuf[j, :, :, :, cols].reshape(256, GROUP))
                mixed[j] = term if mixed[j] is None else mixed[j] + term
        send(pt.at[s, c], pt.at[s, c], s_ptc.at[s], r_ptc.at[s], sib)
        sent(pt.at[s, 0], s_ptc.at[s])
        for j in range(used):
            mx[y, j] = mixed[j].astype(BF)
        for k in Y_ORDER:
            send(mx.at[y], mx.at[y], s_mx.at[s], r_mx.at[s], y_dev(k))
        sent(mx.at[pl.ds(0, NY - 1)], s_mx.at[s])

        if s == 0:
            share_t(0)

        wait_bytes(pt.at[s, 0], r_ptc.at[s])

        def both(step):
            return jnp.concatenate(
                [
                    jnp.concatenate([pt[step, e, n] for n in range(TILES)], axis=1)
                    for e in range(2)
                ],
                axis=0,
            )

        now = both(s)
        other = now if s == 0 else both(0)
        gram = gram0 if s == 0 else gram1
        gram[y] = pack(nt_dot(now, jnp.concatenate([now, other, now, other], axis=0)), gram.shape[1])
        for k in Y_ORDER:
            send(gram.at[y], gram.at[y], s_g.at[s], r_g.at[s], y_dev(k))
        sent(gram.at[pl.ds(0, NY - 1)], s_g.at[s])
        if s == 0:
            spread_t(1)

        if s == 0:
            wait_bytes(tbuf.at[0, :, 0], r_tc.at[0])
        part = None
        wait_bytes(mx.at[pl.ds(0, NY - 1)], r_mx.at[s])
        for j in range(used):
            term = dot(sum_slots(mx.at[:, j], NY).astype(BF), tbuf[j].reshape(256, 1024))
            part = term if part is None else part + term
        part = part.astype(BF)
        for b in range(QBLOCKS):
            zsrc[s, b] = part[:, b * LANES : (b + 1) * LANES]
        for dz, dx in ZX_ORDER:
            there = zx_chip(dz, dx)
            b = 4 * lax.rem(x + dx, 2) + lax.rem(z + dz + 2 * lax.div(lax.rem(x + dx, NX), 2), 4)
            send(zsrc.at[s, b], zrs.at[s, chip], s_zrs.at[s], r_zrs.at[s], zx_dev(there))
        sent(zrs.at[s, pl.ds(0, CHIPS - 1)], s_zrs.at[s])

        wait_bytes(gram.at[pl.ds(0, NY - 1)], r_g.at[s])
        inner = unpack(sum_slots(gram, NY))
        minv[s] = inverse_lower(inner)
        rest = minv[s]
        for n in range(3):
            part = rest.astype(BF)
            mparts[n * RANK : (n + 1) * RANK, :] = part
            rest = rest - part.astype(F32)
        if s == 1:
            shifted[...] = exact_dot(minv[1], exact_dot(inner[:, RANK : 2 * RANK], qf[...]))


        z_mine = (2 * s + c) * QBLOCKS + q_mine

        zrs[s, chip] = zsrc[s, q_mine]
        wait_bytes(zrs.at[s, pl.ds(0, CHIPS - 1)], r_zrs.at[s])
        zall[z_mine] = (sum_slots(zrs.at[s], CHIPS) * (1.0 / 64.0)).astype(BF)
        tile = zall.at[z_mine]
        for d in NEAR:
            for core in (c, 1 - c) if d != (0, 0) else (1 - c,):
                send(tile, tile, s_qag.at[s], r_qag.at[s], zx_dev(zx_chip(*d), core))
        sent(zall.at[pl.ds(0, 15)], s_qag.at[s])

        if s == 0:
            share_t(1)
        else:
            finish()
        wait_bytes(zall.at[pl.ds(0, 15)], r_qag.at[s])
        value = jnp.concatenate(
            [
                jnp.concatenate([zall[(2 * s + e) * QBLOCKS + b] for b in range(QBLOCKS)], axis=1)
                for e in range(2)
            ],
            axis=0,
        )
        parts = dot(mparts[...], value)
        value = parts[:RANK] + (parts[RANK : 2 * RANK] + parts[2 * RANK :])
        if s == 1:
            value = value - shifted[...]
        if s == 0:
            qf[...] = value
            rows = qf[pl.ds(pl.multiple_of(c * HALF, HALF), HALF), :].astype(BF)
            wait_bytes(tbuf.at[1, :, 0], r_tc.at[1])
            for j in range(2):
                sk1[y, j] = nt_dot(rows, tbuf[j].reshape(256, 1024)).astype(BF)
            for k in Y_ORDER:
                send(sk1.at[y], sk1.at[y], s_sk.at[1], r_sk.at[1], y_dev(k))
            sent(sk1.at[pl.ds(0, NY - 1)], s_sk.at[1])
            wbuf[y] = pack(exact_nt_dot(value, jnp.concatenate([value] * 4, axis=0)), 8)
            for k in Y_ORDER:
                send(wbuf.at[y], wbuf.at[y], s_w, r_w, y_dev(k))
            sent(wbuf.at[pl.ds(0, NY - 1)], s_w)
        else:
            out[...] = value

    finish()


def on_device(hidden, cotangent, start_q):
    hidden = hidden.reshape(2, NY, 16, 3584)
    dma = pltpu.SemaphoreType.DMA
    vm = pltpu.VMEM
    in_hbm = pl.BlockSpec(memory_space=pltpu.HBM)
    return pl.pallas_call(
        kernel,
        out_shape=pltpu.VMEM((RANK, 1024), F32),
        in_specs=[in_hbm] * 3,
        out_specs=pl.BlockSpec(memory_space=pltpu.VMEM),
        scratch_shapes=[
            vm((2, NY, 2, 16, 3584), BF),
            vm((2, 16, 8192), BF),
            vm((2, NY, 2, 16, 1024), BF),
            vm((RANK, 1024), F32),
            vm((HALF, 1024), BF),
            vm((NY - 1, HALF, 1024), BF),
            vm((NY, HALF, LANES), BF),
            vm((NY, 2, HALF, 256), BF),
            vm((2, TILES, HALF, LANES), BF),
            vm((2, CHIPS, HALF, LANES), BF),
            vm((2, 2, TILES, HALF, LANES), BF),
            vm((NY, 1, HALF, 256), BF),
            vm((NY, 2, HALF, 256), BF),
            vm((NY, 8, LANES), F32),
            vm((NY, 16, LANES), F32),
            vm((NY, 8, LANES), F32),
            vm((2, QBLOCKS, HALF, LANES), BF),
            vm((2, CHIPS, HALF, LANES), BF),
            vm((4 * QBLOCKS, HALF, LANES), BF),
            vm((3 * RANK, RANK), BF),
            vm((RANK, 1024), F32),
            vm((2, RANK, RANK), F32),
            vm((RANK, RANK), F32),
            dma((6,)),
            dma((3,)), dma((3,)),
            dma, dma((NY - 1,)),
            dma((2,)), dma((2,)),
            dma((2,)), dma((2,)),
            dma((2,)), dma((2,)),
            dma((2,)), dma((2,)),
            dma((2,)), dma((2, NZ - 1)),
            dma((2,)), dma((2,)),
            dma((2,)), dma((2,)),
            dma((2,)), dma((2,)),
            dma, dma,
            dma((2,)), dma((2,)),
            dma((2,)), dma((2,)),
        ],
        compiler_params=pltpu.CompilerParams(
            collective_id=0, has_side_effects=True, vmem_limit_bytes=56 * 1024 * 1024
        ),
        name="powersgd",
    )(hidden, cotangent, start_q)


def solution(mesh):
    return jax.shard_map(
        on_device,
        mesh=mesh,
        in_specs=(P(None, "dp", "mp"), P(None, ("dp", "mp"), None), P(None, "mp")),
        out_specs=P(None, "mp"),
        check_vma=False,
    )
```

```python
import functools

import jax
import jax.numpy as jnp
from jax import lax
from jax.experimental import pallas as pl
from jax.experimental.pallas import tpu as pltpu
from jax.sharding import PartitionSpec as P

MESH = pl.DeviceIdType.MESH
BF = jnp.bfloat16
F32 = jnp.float32
NY = 8
NZ = 8
NX = 4
CHIPS = NZ * NX
TILES = 28
QBLOCKS = 8
HALF = 16
RANK = 32
LANES = 128
GROUP = NX * LANES
Y_ORDER = (4, 3, 5, 2, 6, 1, 7)


def _hops(dz, dx):
    return min(dz, NZ - dz) + min(dx, NX - dx)


ZX_ORDER = sorted(
    [(dz, dx) for dz in range(NZ) for dx in range(NX) if (dz, dx) != (0, 0)],
    key=lambda d: (-_hops(*d), d),
)
NEAR = ((2, 0), (1, 1), (7, 1), (1, 0), (7, 0), (0, 1), (0, 3), (0, 0))
PLANES_IN = (0, 1, 6, 2, 5, 3, 4)
PLANES_OUT = (4, 3, 5, 2, 6, 1, 0)


def nt_dot(a, b):
    return lax.dot_general(a, b, (((1,), (1,)), ((), ())), preferred_element_type=F32)


def dot(a, b):
    return jnp.dot(a, b, preferred_element_type=F32)


def exact_dot(a, b):
    return jnp.dot(a, b, preferred_element_type=F32, precision=lax.Precision.HIGHEST)


def wait_bytes(ref, sem):
    pltpu.make_async_copy(ref, ref, sem).wait()


def exact_nt_dot(a, b):
    return lax.dot_general(
        a, b, (((1,), (1,)), ((), ())), preferred_element_type=F32, precision=lax.Precision.HIGHEST
    )


def pack(value, rows):
    width = LANES * rows // RANK
    lanes = lax.broadcasted_iota(jnp.int32, (rows, LANES), 1)
    packed = value[:rows]
    for k in range(1, RANK // rows):
        packed = jnp.where(lanes >= k * width, value[k * rows : (k + 1) * rows], packed)
    return packed


def unpack(packed):
    rows = packed.shape[0]
    width = LANES * rows // RANK
    return jnp.concatenate(
        [packed] + [pltpu.roll(packed, LANES - k * width, 1) for k in range(1, RANK // rows)], axis=0
    )


def sum_slots(ref, count):
    terms = [ref[n].astype(F32) for n in range(count)]
    while len(terms) > 1:
        terms = [a + b for a, b in zip(terms[::2], terms[1::2])]
    return terms[0]


def inverse_lower(gram):
    rows = lax.broadcasted_iota(jnp.int32, (RANK, LANES), 0)
    lanes = lax.broadcasted_iota(jnp.int32, (RANK, LANES), 1)
    work = jnp.where(lanes < RANK, gram, jnp.where(lanes == rows + RANK, 1.0, 0.0))
    row_ids = lax.broadcasted_iota(jnp.int32, (RANK, 1), 0)
    scale = jnp.zeros((RANK, 1), F32)
    for j in range(RANK):
        row = work[j : j + 1, :]
        pivot = work[j : j + 1, j : j + 1]
        scale = jnp.where(row_ids == j, pivot, scale)
        if j < RANK - 1:
            factor = jnp.where(row_ids > j, work[:, j : j + 1] / pivot, 0.0)
            work = work - factor * row
    return (work * lax.rsqrt(scale))[:, RANK : 2 * RANK]


def kernel(
    hid, cot, startq, out,
    hbuf, cbuf, tbuf, qf, qsrc, qgat, sk0, sk1, ptsrc, ptrs, pt, mx, part0, gram0, gram1, wbuf,
    zsrc, zrs, zall, mparts, shifted, minv, umat,
    s_local, s_core, r_core, s_q, r_q, s_sk, r_sk, s_t, r_t, s_tc, r_tc, s_prs, r_prs, s_pag, r_pag,
    s_ptc, r_ptc, s_mx, r_mx, s_g, r_g, s_w, r_w, s_zrs, r_zrs, s_qag, r_qag,
):
    dp = lax.axis_index("dp")
    y = lax.axis_index("mp")
    c = lax.rem(dp, 2)
    chip = lax.div(dp, 2)
    z = lax.div(chip, NX)
    x = lax.rem(chip, NX)
    sib = {"dp": dp + 1 - 2 * c, "mp": y}
    pt_owner = z < NZ - 1
    q_mine = 4 * lax.rem(x, 2) + lax.rem(z + 2 * lax.div(x, 2), 4)
    ending = []

    def y_dev(k):
        return {"dp": dp, "mp": lax.rem(y + k, NY)}

    def zx_chip(dz, dx):
        return lax.rem(z + dz, NZ) * NX + lax.rem(x + dx, NX)

    def zx_dev(there, core=None):
        return {"dp": there * 2 + (c if core is None else core), "mp": y}

    def send(src, dst, ssem, rsem, dev):
        pltpu.make_async_remote_copy(
            src_ref=src, dst_ref=dst, send_sem=ssem, recv_sem=rsem, device_id=dev, device_id_type=MESH
        ).start()

    def sent(ref, sem, when=None):
        def wait():
            wait_bytes(ref, sem)

        ending.append(wait if when is None else lambda: pl.when(when)(wait))

    def finish():
        while ending:
            ending.pop(0)()

    load_q = pltpu.make_async_copy(startq, qf, s_local.at[0])
    load_q.start()
    bar = pltpu.get_barrier_semaphore()
    greeted = [(_hops(*d), zx_dev(zx_chip(*d))) for d in ZX_ORDER]
    greeted += [(min(k, NY - k), y_dev(k)) for k in Y_ORDER]
    greeted += [(_hops(*d), zx_dev(zx_chip(NZ - d[0], NX - d[1]), 1 - c)) for d in NEAR[:-1]]
    greeted += [(0, sib)]
    for _, there in sorted(greeted, key=lambda e: -e[0]):
        pl.semaphore_signal(bar, inc=1, device_id=there, device_id_type=MESH)
    load_c = pltpu.make_async_copy(cot.at[0], cbuf.at[c], s_local.at[1])
    load_c.start()
    load_h = [pltpu.make_async_copy(hid.at[j], hbuf.at[j, :, c], s_local.at[2 + j]) for j in range(2)]
    load_h[0].start()
    load_h[1].start()
    load_q.wait()
    for part in range(2):
        own_rows = pl.ds(pl.multiple_of(c * HALF, HALF), HALF)
        qsrc[part] = qf[own_rows, part * 512 : (part + 1) * 512].astype(BF)
    pl.semaphore_wait(bar, NY - 1 + CHIPS - 1 + len(NEAR))

    for part in range(2):
        for n, k in enumerate(Y_ORDER):
            send(qsrc.at[part], qgat.at[n, part], s_q, r_q.at[n, part], y_dev(k))
    sent(qgat, s_q)
    send(cot.at[0], cbuf.at[c], s_core.at[0], r_core.at[0], sib)
    sent(cbuf.at[0], s_core.at[0])
    load_c.wait()
    wait_bytes(cbuf.at[0], r_core.at[0])

    def block_sketch(q_rows, owner, part):
        cols = pl.ds(pl.multiple_of(owner * 1024 + part * 512, 512), 512)
        return nt_dot(q_rows, cbuf[:, :, cols].reshape(RANK, 512))

    sketch = block_sketch(qsrc[0], y, 0) + block_sketch(qsrc[1], y, 1)
    for part in range(2):
        for n, k in sorted(enumerate(Y_ORDER), key=lambda e: min(e[1], NY - e[1])):
            wait_bytes(qgat.at[n, part], r_q.at[n, part])
            sketch = sketch + block_sketch(qgat[n, part], lax.rem(y - k + NY, NY), part)
    spot = lax.broadcasted_iota(jnp.int32, (RANK, LANES), 0) + RANK * lax.rem(y, 4)
    place = jnp.where(lax.broadcasted_iota(jnp.int32, (RANK, LANES), 1) == spot, 1.0, 0.0).astype(BF)
    sk0[y] = dot(sketch.astype(BF), place).astype(BF)
    for k in Y_ORDER:
        send(sk0.at[y], sk0.at[y], s_sk.at[0], r_sk.at[0], y_dev(k))
    sent(sk0.at[pl.ds(0, NY - 1)], s_sk.at[0])

    def share_h(j):
        send(hid.at[j], hbuf.at[j, :, c], s_core.at[1 + j], r_core.at[1 + j], sib)
        sent(hbuf.at[j, :, 0], s_core.at[1 + j])

    share_h(0)
    wait_bytes(sk0.at[pl.ds(0, NY - 1)], r_sk.at[0])

    own_cols = pl.ds(pl.multiple_of(y * 1024, 1024), 1024)
    load_t = [pltpu.make_async_copy(cot.at[j, :, own_cols], tbuf.at[j, y, c], s_local.at[4 + j]) for j in range(2)]

    def spread_t(j):
        for k in Y_ORDER:
            there = lax.rem(y + k, NY)
            cols = pl.ds(pl.multiple_of(there * 1024, 1024), 1024)
            send(cot.at[j, :, cols], tbuf.at[j, y, c], s_t.at[j], r_t.at[j], y_dev(k))
        sent(tbuf.at[j, pl.ds(0, NY - 1), 0], s_t.at[j])
        load_t[j].start()

    def share_t(j):
        load_t[j].wait()
        wait_bytes(tbuf.at[j, pl.ds(0, NY - 1), 0], r_t.at[j])
        send(tbuf.at[j, :, c], tbuf.at[j, :, c], s_tc.at[j], r_tc.at[j], sib)
        sent(tbuf.at[j, :, 0], s_tc.at[j])

    left = jnp.concatenate(
        [
            (sk0[0] + sk0[1]) + (sk0[2] + sk0[3]),
            (sk0[4] + sk0[5]) + (sk0[6] + sk0[7]),
        ],
        axis=1,
    )

    for s in range(2):
        used = s + 1
        if s == 0:
            load_h[0].wait()
            wait_bytes(hbuf.at[0, :, 0], r_core.at[1])
        if s == 1:
            wait_bytes(sk1.at[0, pl.ds(0, NY - 1)], r_sk.at[1])
            part0[...] = dot(sum_slots(sk1.at[0], NY).astype(BF), hbuf[0].reshape(256, 3584))
            load_h[1].wait()
            wait_bytes(hbuf.at[1, :, 0], r_core.at[2])
            wait_bytes(sk1.at[1, pl.ds(0, NY - 1)], r_sk.at[2])
            left = sum_slots(sk1.at[1], NY).astype(BF)
        for step in PLANES_OUT:
            n = lax.rem(z + step, NZ - 1)
            cols = pl.ds(pl.multiple_of(n * GROUP, GROUP), GROUP)
            part = dot(left, hbuf[s, :, :, :, cols].reshape(256, GROUP))
            if s == 1:
                part = part + part0[:, cols]
            part = part.astype(BF)
            for g in range(NX):
                ptsrc[s, n * NX + g] = part[:, g * LANES : (g + 1) * LANES]
            for dx in (2, 1, 3, 0):
                there = n * NX + lax.rem(x + dx, NX)

                def post(there=there):
                    send(ptsrc.at[s, there], ptrs.at[s, chip], s_prs.at[s], r_prs.at[s], zx_dev(there))

                if step == 0 and dx == 0:
                    pl.when(jnp.logical_not(pt_owner))(post)
                else:
                    post()
        if s == 0:
            share_h(1)
            spread_t(0)

        sent(ptrs.at[s, pl.ds(0, TILES - 1)], s_prs.at[s], pt_owner)
        sent(ptrs.at[s, pl.ds(0, TILES)], s_prs.at[s], jnp.logical_not(pt_owner))

        if s == 1:
            wait_bytes(wbuf.at[pl.ds(0, NY - 1)], r_w)
            weights = unpack(sum_slots(wbuf, NY))
            umat[...] = exact_dot(weights[:, :RANK], minv[0])
            qf[...] = lax.dot_general(
                minv[0], qf[...], (((0,), (0,)), ((), ())), preferred_element_type=F32, precision=lax.Precision.HIGHEST
            )

        @pl.when(pt_owner)
        def _():
            correction = 0.0
            if s == 1:
                past = jnp.concatenate([pt[0, 0, chip], pt[0, 1, chip]], axis=0).astype(F32)
                own_rows = umat[pl.ds(pl.multiple_of(c * HALF, HALF), HALF), :]
                correction = exact_dot(own_rows, past)
            ptrs[s, chip] = ptsrc[s, chip]
            wait_bytes(ptrs.at[s, pl.ds(0, CHIPS - 1)], r_prs.at[s])
            total = sum_slots(ptrs.at[s], CHIPS) * (1.0 / 64.0) - correction
            pt[s, c, chip] = total.astype(BF)
            tile = pt.at[s, c, chip]
            for d in ZX_ORDER:
                send(tile, tile, s_pag.at[s], r_pag.at[s, z], zx_dev(zx_chip(*d)))

        sent(ptrs.at[s, pl.ds(0, CHIPS - 1)], s_pag.at[s], pt_owner)

        mixed = [None] * used
        for step in PLANES_IN:
            n = lax.rem(z + step, NZ - 1)
            first = pl.multiple_of(n * NX, NX)
            if step == 0:

                @pl.when(pt_owner)
                def _():
                    wait_bytes(pt.at[s, c, pl.ds(0, NX - 1)], r_pag.at[s, z])

                @pl.when(jnp.logical_not(pt_owner))
                def _():
                    wait_bytes(pt.at[s, c, pl.ds(0, NX)], r_pag.at[s, n])

            else:
                wait_bytes(pt.at[s, c, pl.ds(0, NX)], r_pag.at[s, n])
            cols = pl.ds(pl.multiple_of(n * GROUP, GROUP), GROUP)
            rows = jnp.concatenate([pt[s, c, first + g] for g in range(NX)], axis=1)
            for j in range(used):
                term = nt_dot(rows, hbuf[j, :, :, :, cols].reshape(256, GROUP))
                mixed[j] = term if mixed[j] is None else mixed[j] + term
        send(pt.at[s, c], pt.at[s, c], s_ptc.at[s], r_ptc.at[s], sib)
        sent(pt.at[s, 0], s_ptc.at[s])
        for j in range(used):
            mx[s, j, y] = mixed[j].astype(BF)
            for k in Y_ORDER:
                send(mx.at[s, j, y], mx.at[s, j, y], s_mx.at[s, j], r_mx.at[s, j], y_dev(k))
            sent(mx.at[s, j, pl.ds(0, NY - 1)], s_mx.at[s, j])

        if s == 0:
            share_t(0)

        wait_bytes(pt.at[s, 0], r_ptc.at[s])

        def both(step):
            return jnp.concatenate(
                [
                    jnp.concatenate([pt[step, e, n] for n in range(TILES)], axis=1)
                    for e in range(2)
                ],
                axis=0,
            )

        now = both(s)
        other = now if s == 0 else both(0)
        gram = gram0 if s == 0 else gram1
        gram[y] = pack(nt_dot(now, jnp.concatenate([now, other, now, other], axis=0)), gram.shape[1])
        for k in Y_ORDER:
            send(gram.at[y], gram.at[y], s_g.at[s], r_g.at[s], y_dev(k))
        sent(gram.at[pl.ds(0, NY - 1)], s_g.at[s])
        if s == 0:
            spread_t(1)

        if s == 0:
            wait_bytes(tbuf.at[0, :, 0], r_tc.at[0])
        part = None
        for j in range(used):
            wait_bytes(mx.at[s, j, pl.ds(0, NY - 1)], r_mx.at[s, j])
            term = dot(sum_slots(mx.at[s, j], NY).astype(BF), tbuf[j].reshape(256, 1024))
            part = term if part is None else part + term
        part = part.astype(BF)
        for b in range(QBLOCKS):
            zsrc[s, b] = part[:, b * LANES : (b + 1) * LANES]
        for dz, dx in ZX_ORDER:
            there = zx_chip(dz, dx)
            b = 4 * lax.rem(x + dx, 2) + lax.rem(z + dz + 2 * lax.div(lax.rem(x + dx, NX), 2), 4)
            send(zsrc.at[s, b], zrs.at[s, chip], s_zrs.at[s], r_zrs.at[s], zx_dev(there))
        sent(zrs.at[s, pl.ds(0, CHIPS - 1)], s_zrs.at[s])

        wait_bytes(gram.at[pl.ds(0, NY - 1)], r_g.at[s])
        inner = unpack(sum_slots(gram, NY))
        minv[s] = inverse_lower(inner)
        rest = minv[s]
        for n in range(3):
            part = rest.astype(BF)
            mparts[n * RANK : (n + 1) * RANK, :] = part
            rest = rest - part.astype(F32)
        if s == 1:
            shifted[...] = exact_dot(minv[1], exact_dot(inner[:, RANK : 2 * RANK], qf[...]))


        z_mine = (2 * s + c) * QBLOCKS + q_mine

        zrs[s, chip] = zsrc[s, q_mine]
        wait_bytes(zrs.at[s, pl.ds(0, CHIPS - 1)], r_zrs.at[s])
        zall[z_mine] = (sum_slots(zrs.at[s], CHIPS) * (1.0 / 64.0)).astype(BF)
        tile = zall.at[z_mine]
        for d in NEAR:
            for core in (c, 1 - c) if d != (0, 0) else (1 - c,):
                send(tile, tile, s_qag.at[s], r_qag.at[s], zx_dev(zx_chip(*d), core))
        sent(zall.at[pl.ds(0, 15)], s_qag.at[s])

        if s == 0:
            share_t(1)
        else:
            finish()
        wait_bytes(zall.at[pl.ds(0, 15)], r_qag.at[s])
        value = jnp.concatenate(
            [
                jnp.concatenate([zall[(2 * s + e) * QBLOCKS + b] for b in range(QBLOCKS)], axis=1)
                for e in range(2)
            ],
            axis=0,
        )
        parts = dot(mparts[...], value)
        value = parts[:RANK] + (parts[RANK : 2 * RANK] + parts[2 * RANK :])
        if s == 1:
            value = value - shifted[...]
        if s == 0:
            qf[...] = value
            rows = qf[pl.ds(pl.multiple_of(c * HALF, HALF), HALF), :].astype(BF)
            wait_bytes(tbuf.at[1, :, 0], r_tc.at[1])
            for j in range(2):
                sk1[j, y] = nt_dot(rows, tbuf[j].reshape(256, 1024)).astype(BF)
                for k in Y_ORDER:
                    send(sk1.at[j, y], sk1.at[j, y], s_sk.at[1 + j], r_sk.at[1 + j], y_dev(k))
                sent(sk1.at[j, pl.ds(0, NY - 1)], s_sk.at[1 + j])
            wbuf[y] = pack(exact_nt_dot(value, jnp.concatenate([value] * 4, axis=0)), 8)
            for k in Y_ORDER:
                send(wbuf.at[y], wbuf.at[y], s_w, r_w, y_dev(k))
            sent(wbuf.at[pl.ds(0, NY - 1)], s_w)
        else:
            out[...] = value

    finish()


def on_device(hidden, cotangent, start_q):
    hidden = hidden.reshape(2, NY, 16, 3584)
    dma = pltpu.SemaphoreType.DMA
    vm = pltpu.VMEM
    in_hbm = pl.BlockSpec(memory_space=pltpu.HBM)
    return pl.pallas_call(
        kernel,
        out_shape=pltpu.VMEM((RANK, 1024), F32),
        in_specs=[in_hbm] * 3,
        out_specs=pl.BlockSpec(memory_space=pltpu.VMEM),
        scratch_shapes=[
            vm((2, NY, 2, 16, 3584), BF),
            vm((2, 16, 8192), BF),
            vm((2, NY, 2, 16, 1024), BF),
            vm((RANK, 1024), F32),
            vm((2, HALF, 512), BF),
            vm((NY - 1, 2, HALF, 512), BF),
            vm((NY, HALF, LANES), BF),
            vm((2, NY, HALF, 256), BF),
            vm((2, TILES, HALF, LANES), BF),
            vm((2, CHIPS, HALF, LANES), BF),
            vm((2, 2, TILES, HALF, LANES), BF),
            vm((2, 2, NY, HALF, 256), BF),
            vm((HALF, 3584), F32),
            vm((NY, 8, LANES), F32),
            vm((NY, 16, LANES), F32),
            vm((NY, 8, LANES), F32),
            vm((2, QBLOCKS, HALF, LANES), BF),
            vm((2, CHIPS, HALF, LANES), BF),
            vm((4 * QBLOCKS, HALF, LANES), BF),
            vm((3 * RANK, RANK), BF),
            vm((RANK, 1024), F32),
            vm((2, RANK, RANK), F32),
            vm((RANK, RANK), F32),
            dma((6,)),
            dma((3,)), dma((3,)),
            dma, dma((NY - 1, 2)),
            dma((3,)), dma((3,)),
            dma((2,)), dma((2,)),
            dma((2,)), dma((2,)),
            dma((2,)), dma((2,)),
            dma((2,)), dma((2, NZ - 1)),
            dma((2,)), dma((2,)),
            dma((2, 2)), dma((2, 2)),
            dma((2,)), dma((2,)),
            dma, dma,
            dma((2,)), dma((2,)),
            dma((2,)), dma((2,)),
        ],
        compiler_params=pltpu.CompilerParams(
            collective_id=0, has_side_effects=True, vmem_limit_bytes=56 * 1024 * 1024
        ),
        name="powersgd",
    )(hidden, cotangent, start_q)


def solution(mesh):
    return jax.shard_map(
        on_device,
        mesh=mesh,
        in_specs=(P(None, "dp", "mp"), P(None, ("dp", "mp"), None), P(None, "mp")),
        out_specs=P(None, "mp"),
        check_vma=False,
    )
```
